512 devices in a mesh: group: 8 (over x, core), expert: 64 (over z, y).
Axes of the slice: x: 4, y: 4, z: 16, core: 2. Of those that a mesh axis runs over, the one named last changes fastest.
Arguments:
- layer_in: bfloat16 [16384, 1536], P(('group', 'expert')), may hold values from -6 to 6
- grad_out: bfloat16 [16384, 1536], P(('group', 'expert')), may hold values from -6 to 6
- expert_ids: int32 [16384, 8], P(('group', 'expert')), may hold values from 0 to 63, as said below
- gate_probs: bfloat16 [16384, 8], P(('group', 'expert')), may hold values from 0.049804688 to 0.5
- gate_weight: bfloat16 [64, 1536, 384], P('expert'), may hold values from -0.15625 to 0.15625
- up_weight: bfloat16 [64, 1536, 384], P('expert'), may hold values from -0.15625 to 0.15625
- down_weight: bfloat16 [64, 384, 1536], P('expert'), may hold values from -0.3125 to 0.3125
Outputs:
- grad_in: bfloat16 [16384, 1536], P(('group', 'expert'))
- grad_probs: bfloat16 [16384, 8], P(('group', 'expert'))
- grad_gate: float32 [64, 1536, 384], P('expert', 'group')
- grad_up: float32 [64, 1536, 384], P('expert', 'group')
- grad_down: float32 [64, 384, 1536], P('expert', 'group')
The draws below stay inside these ranges and needn't reach their ends.
Inputs may be any that keep to these rules, and one draw needn't show every extreme that they name: `expert_ids`: each token names 8 different experts. Among the rows of the 32 tokens of one device, no expert is named more than 6 times, and one expert, the same for every device, is named exactly 6 times on each device.
All inputs are finite; a program needn't handle non-finite values.
Results may differ from the reference program's by a relative error of at most 0.015.
Values may be sent and summed in bfloat16 or wider, within the bound.
No kernel may reach another device: no remote copies, remote signals or barrier semaphores. Data moves between devices by JAX's collectives and lax.ppermute only.
A program may use at most 64 MiB of HBM per device.

```python
import math
import jax
import jax.numpy as jnp
from jax import lax

D = 1536
FF = 384
TOP = 8
TOK_DEV = 32
EXPERTS = 64
CAP = 6
TOKENS = 16384
N_GROUP = 8


def draw_expert_ids(key, part):
    key = jax.random.fold_in(key, 11)
    blocks = TOKENS // TOK_DEV
    mean_load = TOK_DEV * TOP // EXPERTS
    half_load = mean_load // 2
    hot_expert = jax.random.randint(jax.random.fold_in(key, 1), (), 0, EXPERTS)
    block_keys = jax.random.split(jax.random.fold_in(key, 2), blocks)

    def one_block(block_key):
        pair_key, shift_key, row_key, column_key = jax.random.split(block_key, 4)
        pairing = jax.random.permutation(pair_key, EXPERTS).astype(jnp.int32)
        first_expert = pairing[0]
        pairing = jnp.where(pairing == hot_expert, first_expert, pairing).at[0].set(hot_expert)
        pair_a = pairing[0::2]
        pair_b = pairing[1::2]
        shifted = jax.random.randint(shift_key, (EXPERTS // 2,), 0, half_load + 1).at[0].set(half_load)
        counts = jnp.zeros((EXPERTS,), jnp.int32).at[pair_a].set(mean_load + shifted).at[pair_b].set(mean_load - shifted)
        run_ends = jnp.cumsum(counts)
        places = jnp.arange(TOK_DEV * TOP, dtype=jnp.int32)
        listed = jnp.sum((run_ends[:, None] <= places[None, :]).astype(jnp.int32), axis=0)
        layout = listed.reshape(TOP, TOK_DEV).T
        layout = layout[jax.random.permutation(row_key, TOK_DEV)]
        scores = jax.random.randint(column_key, (TOK_DEV, TOP), 0, 1 << 20) * TOP + jnp.arange(TOP, dtype=jnp.int32)[None, :]
        within = jnp.argsort(scores, axis=1)
        return jnp.take_along_axis(layout, within, axis=1)
    return jax.vmap(one_block)(block_keys).reshape(TOKENS, TOP).astype(jnp.int32)


def block_scale(rng, extent, shards, low, top_value):
    loudness = 1.0
    for dim, parts in shards:
        draws = jax.random.uniform(jax.random.fold_in(jax.random.fold_in(rng, 6), dim), (parts,), jnp.float32, low / len(shards), top_value / len(shards))
        loudness = loudness * jnp.repeat(jnp.exp(draws), extent[dim] // parts).reshape((-1,) + (1,) * (len(extent) - 1 - dim))
    return loudness


def bell_draw(stream_key, extent, deviation, bound, shards=(), kind=jnp.bfloat16):
    values = jax.random.normal(stream_key, extent, jnp.float32) * deviation
    if len(shards) > 0:
        values = block_scale(stream_key, extent, shards, -0.22, 0.18) * values
    return jnp.clip(values, min=-bound, max=bound).astype(kind)


def setup_inputs(seed: int = 0) -> dict:
    keys = jax.random.split(jax.random.key(seed), 8)
    return {
        "layer_in": bell_draw(keys[0], (TOKENS, D), 1.0, 6.0, ((0, 512),)),
        "grad_out": bell_draw(keys[1], (TOKENS, D), 1.0, 6.0, ((0, 512),)),
        "expert_ids": draw_expert_ids(jax.random.fold_in(keys[7], 71), 0),
        "gate_probs": jnp.clip(jnp.exp(math.log(0.5) - 2.306499 * jax.random.uniform(keys[3], (TOKENS, TOP), jnp.float32) ** block_scale(keys[3], (TOKENS, TOP), ((0, 512),), -0.2, 0.2)), 0.049804688, 0.5).astype(jnp.bfloat16),
        "gate_weight": bell_draw(keys[4], (EXPERTS, D, FF), D ** -0.5, 0.15625, ((0, 64),)),
        "up_weight": bell_draw(keys[5], (EXPERTS, D, FF), D ** -0.5, 0.15625, ((0, 64),)),
        "down_weight": bell_draw(keys[6], (EXPERTS, FF, D), FF ** -0.5, 0.3125, ((0, 64),)),
    }


def expert_rows(rows_in, rows_grad, rows_prob, gate_mat, up_mat, down_mat):
    pre_gate = jnp.dot(rows_in, gate_mat, preferred_element_type=jnp.float32)
    pre_up = jnp.dot(rows_in, up_mat, preferred_element_type=jnp.float32)
    sigmoid_gate = jax.nn.sigmoid(pre_gate)
    silu_gate = pre_gate * sigmoid_gate
    hidden = (silu_gate * pre_up).astype(jnp.bfloat16)
    out_rows = jnp.dot(hidden, down_mat, preferred_element_type=jnp.float32)
    prob_grad = jnp.sum(rows_grad.astype(jnp.float32) * out_rows, axis=1).astype(jnp.bfloat16)
    scaled = (rows_prob.astype(jnp.float32)[:, None] * rows_grad.astype(jnp.float32)).astype(jnp.bfloat16)
    grad_hidden = lax.dot_general(scaled, down_mat, (((1,), (1,)), ((), ())), preferred_element_type=jnp.float32)
    gate_grad = (grad_hidden * pre_up * sigmoid_gate * (1.0 + pre_gate * (1.0 - sigmoid_gate))).astype(jnp.bfloat16)
    up_grad = (grad_hidden * silu_gate).astype(jnp.bfloat16)
    returned = lax.dot_general(gate_grad, gate_mat, (((1,), (1,)), ((), ())), preferred_element_type=jnp.float32)
    returned = returned + lax.dot_general(up_grad, up_mat, (((1,), (1,)), ((), ())), preferred_element_type=jnp.float32)
    return returned.astype(jnp.bfloat16), prob_grad, hidden, gate_grad, up_grad, scaled


def route_table(expert_ids):
    blocks = TOKENS // TOK_DEV
    block_ids = expert_ids.reshape(blocks, TOK_DEV * TOP)
    one_hot = (block_ids[:, :, None] == jnp.arange(EXPERTS, dtype=jnp.int32)[None, None, :]).astype(jnp.int32)
    before = jnp.cumsum(one_hot, axis=1) - one_hot
    slot_rank = jnp.sum(before * one_hot, axis=2)
    block_base = (jnp.arange(blocks, dtype=jnp.int32) * (EXPERTS * CAP))[:, None]
    position = block_base + block_ids * CAP + slot_rank
    row_number = jnp.arange(TOKENS * TOP, dtype=jnp.int32)
    slot_table = jnp.full((blocks * EXPERTS * CAP,), -1, jnp.int32)
    slot_table = slot_table.at[position.reshape(-1)].set(row_number)
    return slot_table.reshape(blocks, EXPERTS, CAP).transpose(1, 0, 2).reshape(EXPERTS, blocks * CAP)


def group_sum(left, right):
    left_f = left.reshape(N_GROUP, -1, left.shape[1]).astype(jnp.float32)
    right_f = right.reshape(N_GROUP, -1, right.shape[1]).astype(jnp.float32)
    partial_sums = jnp.einsum("grd,grf->gdf", left_f, right_f, precision=lax.Precision.HIGHEST)
    rounded = lax.optimization_barrier(partial_sums.astype(jnp.bfloat16))
    return jnp.sum(rounded.astype(jnp.float32), axis=0)


def reference(layer_in, grad_out, expert_ids, gate_probs, gate_weight, up_weight, down_weight):
    slot_table = route_table(expert_ids)
    flat_probs = gate_probs.reshape(-1)

    def per_expert(totals, inputs):
        grad_total, prob_total = totals
        source, gate_mat, up_mat, down_mat = inputs
        filled = source >= 0
        safe_row = jnp.where(filled, source, 0)
        token_row = safe_row // TOP
        rows_in = jnp.where(filled[:, None], layer_in[token_row], jnp.zeros((), layer_in.dtype))
        rows_grad = jnp.where(filled[:, None], grad_out[token_row], jnp.zeros((), grad_out.dtype))
        rows_prob = jnp.where(filled, flat_probs[safe_row], jnp.zeros((), gate_probs.dtype))
        returned, prob_grad, hidden, gate_grad, up_grad, scaled = expert_rows(rows_in, rows_grad, rows_prob, gate_mat, up_mat, down_mat)
        grad_total = grad_total.at[token_row].add(jnp.where(filled[:, None], returned.astype(jnp.float32), jnp.float32(0.0)))
        prob_total = prob_total.at[safe_row].add(jnp.where(filled, prob_grad.astype(jnp.float32), jnp.float32(0.0)))
        grads = (group_sum(rows_in, gate_grad), group_sum(rows_in, up_grad), group_sum(hidden, scaled))
        return (grad_total, prob_total), grads

    start = (jnp.zeros((TOKENS, D), jnp.float32), jnp.zeros((TOKENS * TOP,), jnp.float32))
    totals, grads = lax.scan(per_expert, start, (slot_table, gate_weight, up_weight, down_weight))
    grad_in = totals[0].astype(jnp.bfloat16)
    grad_probs = totals[1].reshape(TOKENS, TOP).astype(jnp.bfloat16)
    return grad_in, grad_probs, grads[0], grads[1], grads[2]
```

```python
import functools

import jax
import jax.numpy as jnp
from jax import lax
from jax.experimental import pallas as pl
from jax.experimental.pallas import tpu as pltpu
from jax.sharding import Mesh, PartitionSpec as P

F32 = jnp.float32
BF16 = jnp.bfloat16
LANES = 128
CAP = 6
FAR = 4
NEAR = 16
TOP = 8
MIB = 1 << 20


def iota(shape, dim):
    return lax.broadcasted_iota(jnp.int32, shape, dim)


def dot(a, b, contract=((1,), (0,))):
    return lax.dot_general(a, b, (contract, ((), ())), preferred_element_type=F32)


def whole(n):
    return [pl.BlockSpec(memory_space=pltpu.VMEM)] * n


def slot_parts(i):
    sixth = lax.shift_right_logical(i * 10923, 16)
    expert = lax.shift_right_logical(i * 2731, 16)
    return expert, sixth - FAR * expert, i - CAP * sixth


def select_kernel(base_ref, tok_ref, send_ref, pick_ref):
    tokens = tok_ref.shape[0]
    slots = send_ref.shape[0]
    width = send_ref.shape[1] // 2
    block = tokens // FAR
    extras = tok_ref[:, 2 * width :].astype(F32)
    lane = iota((tokens, LANES), 1)
    expert_lane = jnp.where(lane < NEAR, lane + base_ref[0], -1).astype(F32)
    member = jnp.zeros((tokens, LANES), F32)
    prob = jnp.zeros((tokens, LANES), F32)
    for k in range(TOP):
        hit = extras[:, k : k + 1] == expert_lane
        member = jnp.where(hit, 1.0, member)
        prob = jnp.where(hit, extras[:, TOP + k : TOP + k + 1], prob)
    row, col = iota((tokens, tokens), 0), iota((tokens, tokens), 1)
    shift = block.bit_length() - 1
    same = lax.shift_right_logical(row, shift) == lax.shift_right_logical(col, shift)
    earlier = jnp.where(same & (col < row), 1.0, 0.0).astype(BF16)
    rank = dot(earlier, member.astype(BF16))
    code = jnp.where(member > 0.0, rank, -1.0).astype(BF16)
    eye = jnp.where(row == col, 1.0, 0.0).astype(BF16)
    code_t = dot(code, eye, ((0,), (0,))).astype(BF16)
    prob_t = dot(prob.astype(BF16), eye, ((0,), (0,))).astype(BF16)

    expert, home, place = slot_parts(iota((slots, LANES), 0))
    spread = jnp.where(iota((slots, LANES), 1) == expert, 1.0, 0.0).astype(BF16)
    code_row = dot(spread, code_t)
    token_block = lax.shift_right_logical(iota((slots, tokens), 1), shift)
    chosen = (code_row == place.astype(F32)) & (token_block == home)
    select = jnp.where(chosen, 1.0, 0.0).astype(BF16)
    prob_row = jnp.sum(jnp.where(chosen, dot(spread, prob_t), 0.0), axis=1, keepdims=True)
    send_ref[:, :width] = dot(select, tok_ref[:, :width]).astype(BF16)
    grads = dot(select, tok_ref[:, width : 2 * width])
    send_ref[:, width:] = (prob_row * grads).astype(BF16)

    expert, home, place = slot_parts(iota((LANES, slots), 1))
    spread = jnp.where(iota((LANES, slots), 0) == expert, 1.0, 0.0).astype(BF16)
    code_col = dot(code, spread)
    token_block = lax.shift_right_logical(iota((tokens, slots), 0), shift)
    chosen = (code_col == place.astype(F32)) & (token_block == home)
    pick_ref[...] = jnp.where(chosen, 1.0, 0.0).astype(BF16)


def expert_kernel(rows_ref, gate_ref, up_ref, down_ref, ret_ref, part_ref):
    width, hidden_width = gate_ref.shape
    groups = part_ref.shape[0]
    share = width // groups
    down_share = hidden_width // groups
    rows = rows_ref[:, :width]
    scaled = rows_ref[:, width:]
    gate, up, down = gate_ref[...], up_ref[...], down_ref[...]
    pre_gate = dot(rows, gate)
    pre_up = dot(rows, up)
    grad_hidden = dot(scaled, down, ((1,), (1,)))
    sig = jax.nn.sigmoid(pre_gate)
    silu = pre_gate * sig
    hidden = (silu * pre_up).astype(BF16)
    prob_grad = jnp.sum(hidden.astype(F32) * grad_hidden, axis=1, keepdims=True)
    gate_grad = (grad_hidden * pre_up * sig * (1.0 + pre_gate * (1.0 - sig))).astype(BF16)
    up_grad = (grad_hidden * silu).astype(BF16)
    back = dot(gate_grad, gate, ((1,), (1,))) + dot(up_grad, up, ((1,), (1,)))
    ret_ref[:, :width] = back.astype(BF16)
    ret_ref[:, width:] = jnp.broadcast_to(prob_grad, (rows.shape[0], LANES)).astype(BF16)
    both = jnp.concatenate([gate_grad, up_grad], axis=1)
    for pair in range(groups // 2):
        columns = rows_ref[:, pair * 2 * share : (pair + 1) * 2 * share]
        part = dot(columns, both, ((0,), (0,))).astype(BF16)
        part_ref[2 * pair, :share, :] = part[:share]
        part_ref[2 * pair + 1, :share, :] = part[share:]
    half = width // 2
    for side in range(2):
        part = dot(hidden, scaled[:, side * half : (side + 1) * half], ((0,), (0,))).astype(BF16)
        for g in range(groups):
            low = share + side * down_share
            part_ref[g, low : low + down_share, :] = part[g * down_share : (g + 1) * down_share]


def combine_kernel(base_ref, back_ref, pick_ref, extra_ref, sum_ref):
    slots = back_ref.shape[0]
    width = back_ref.shape[1] - LANES
    tokens = sum_ref.shape[0]
    pick = pick_ref[...]
    sum_ref[:, :width] = dot(pick, back_ref[:, :width]).astype(BF16)
    expert, _, _ = slot_parts(iota((slots, LANES), 0))
    own = iota((slots, LANES), 1) == expert
    spread = jnp.where(own, back_ref[:, width:].astype(F32), 0.0).astype(BF16)
    by_expert = dot(pick, spread)
    extras = extra_ref[...].astype(F32)
    lane = iota((tokens, LANES), 1)
    expert_lane = jnp.where(lane < NEAR, lane + base_ref[0], -1).astype(F32)
    result = jnp.zeros((tokens, LANES), F32)
    for k in range(TOP):
        hit = extras[:, k : k + 1] == expert_lane
        value = jnp.sum(jnp.where(hit, by_expert, 0.0), axis=1, keepdims=True)
        value = value / extras[:, TOP + k : TOP + k + 1]
        result = jnp.where(lane == k, value, result)
    sum_ref[:, width:] = result.astype(BF16)


def finish_kernel(sums_ref, part_ref, in_ref, prob_ref, gate_ref, up_ref, down_ref):
    width = in_ref.shape[1]
    total = sums_ref[0].astype(F32)
    for s in range(1, FAR):
        total = total + sums_ref[s].astype(F32)
    in_ref[...] = total[:, :width].astype(BF16)
    prob_ref[...] = total[:, width : width + TOP].astype(BF16)
    share, hidden_width = gate_ref.shape
    down_share = down_ref.shape[0]
    gate_ref[...] = part_ref[:share, :hidden_width].astype(F32)
    up_ref[...] = part_ref[:share, hidden_width:].astype(F32)
    half = width // 2
    down_ref[:, :half] = part_ref[share : share + down_share, :].astype(F32)
    down_ref[:, half:] = part_ref[share + down_share :, :].astype(F32)


def params(mib):
    return pltpu.CompilerParams(vmem_limit_bytes=mib * MIB)


def per_device(layer_in, grad_out, expert_ids, gate_probs, gate_weight, up_weight, down_weight):
    block, width = layer_in.shape
    hidden_width = gate_weight.shape[2]
    groups = lax.axis_size("group")
    tokens = FAR * block
    slots = NEAR * FAR * CAP
    share = width // groups
    down_share = hidden_width // groups
    part_rows = share + 2 * down_share
    base = (lax.axis_index("far") * NEAR).astype(jnp.int32).reshape(1)
    scalar = pl.BlockSpec(memory_space=pltpu.SMEM)

    extras = jnp.concatenate([expert_ids.astype(BF16), gate_probs], axis=1)
    extras = jnp.pad(extras, ((0, 0), (0, LANES - 2 * TOP)))
    packed = jnp.concatenate([layer_in, grad_out, extras], axis=1)
    near_tokens = lax.all_gather(packed, "far", tiled=True)

    send, pick = pl.pallas_call(
        select_kernel,
        out_shape=(
            jax.ShapeDtypeStruct((slots, 2 * width), BF16),
            jax.ShapeDtypeStruct((tokens, slots), BF16),
        ),
        in_specs=[scalar] + whole(1),
        out_specs=tuple(whole(2)),
        compiler_params=params(24),
        name="select_rows",
    )(base, near_tokens)

    near = ("near", "y")
    exchange = functools.partial(lax.all_to_all, split_axis=0, concat_axis=0, tiled=True)
    rows = exchange(send.reshape(NEAR, FAR * CAP, 2 * width), near).reshape(slots, 2 * width)

    back, parts = pl.pallas_call(
        expert_kernel,
        out_shape=(
            jax.ShapeDtypeStruct((slots, width + LANES), BF16),
            jax.ShapeDtypeStruct((groups, part_rows, 2 * hidden_width), BF16),
        ),
        in_specs=whole(4),
        out_specs=tuple(whole(2)),
        compiler_params=params(40),
        name="expert_rows",
    )(rows, gate_weight[0], up_weight[0], down_weight[0])

    part_sum = lax.psum_scatter(
        parts.reshape(groups * part_rows, 2 * hidden_width), "group", scatter_dimension=0, tiled=True
    )
    back = exchange(back.reshape(NEAR, FAR * CAP, width + LANES), near).reshape(slots, width + LANES)

    sums = pl.pallas_call(
        combine_kernel,
        out_shape=jax.ShapeDtypeStruct((tokens, width + LANES), BF16),
        in_specs=[scalar] + whole(3),
        out_specs=whole(1)[0],
        compiler_params=params(24),
        name="combine_rows",
    )(base, back, pick, near_tokens[:, 2 * width :])
    sums = exchange(sums.reshape(FAR, block, width + LANES), "far")

    grad_in, grad_probs, grad_gate, grad_up, grad_down = pl.pallas_call(
        finish_kernel,
        out_shape=(
            jax.ShapeDtypeStruct((block, width), BF16),
            jax.ShapeDtypeStruct((block, TOP), BF16),
            jax.ShapeDtypeStruct((share, hidden_width), F32),
            jax.ShapeDtypeStruct((share, hidden_width), F32),
            jax.ShapeDtypeStruct((down_share, width), F32),
        ),
        in_specs=whole(2),
        out_specs=tuple(whole(5)),
        compiler_params=params(24),
        name="finish",
    )(sums, part_sum)
    return grad_in, grad_probs, grad_gate[None], grad_up[None], grad_down[None]


def solution(mesh):
    groups, experts = mesh.devices.shape
    split = Mesh(mesh.devices.reshape(groups, FAR, 4, experts // NEAR), ("group", "far", "near", "y"))
    everywhere = ("group", "far", "near", "y")
    expert = ("far", "near", "y")
    token_spec = P(everywhere, None)
    weight_spec = P(expert, None, None)
    grad_spec = P(expert, "group", None)
    return jax.shard_map(
        per_device,
        mesh=split,
        in_specs=(token_spec,) * 4 + (weight_spec,) * 3,
        out_specs=(token_spec,) * 2 + (grad_spec,) * 3,
        check_vma=False,
    )
```

```python
import functools

import jax
import jax.numpy as jnp
from jax import lax
from jax.experimental import pallas as pl
from jax.experimental.pallas import tpu as pltpu
from jax.sharding import Mesh, PartitionSpec as P

F32 = jnp.float32
BF16 = jnp.bfloat16
LANES = 128
CAP = 6
FAR = 4
NEAR = 16
TOP = 8
EXPERTS = 64
MIB = 1 << 20


def iota(shape, dim):
    return lax.broadcasted_iota(jnp.int32, shape, dim)


def dot(a, b, contract=((1,), (0,))):
    return lax.dot_general(a, b, (contract, ((), ())), preferred_element_type=F32)


def whole(n):
    return [pl.BlockSpec(memory_space=pltpu.VMEM)] * n


def slot_parts(i):
    sixth = lax.shift_right_logical(i * 10923, 16)
    expert = lax.shift_right_logical(i * 2731, 16)
    return expert, sixth - FAR * expert, i - CAP * sixth


def served(lane, base):
    return jnp.where(lane < NEAR, (lane + base) & (EXPERTS - 1), -1).astype(F32)


def windows(groups, experts):
    lists = []
    for g in range(groups):
        for far in range(FAR):
            start = far * NEAR + (g % 2) * (NEAR // 2)
            lists.append([g * experts + (start + j) % experts for j in range(NEAR)])
    return lists


def select_kernel(base_ref, tok_ref, send_ref, pick_ref):
    tokens = tok_ref.shape[0]
    slots = send_ref.shape[0]
    width = send_ref.shape[1] // 2
    block = tokens // FAR
    extras = tok_ref[:, 2 * width :].astype(F32)
    lane = iota((tokens, LANES), 1)
    expert_lane = served(lane, base_ref[0])
    member = jnp.zeros((tokens, LANES), F32)
    prob = jnp.zeros((tokens, LANES), F32)
    for k in range(TOP):
        hit = extras[:, k : k + 1] == expert_lane
        member = jnp.where(hit, 1.0, member)
        prob = jnp.where(hit, extras[:, TOP + k : TOP + k + 1], prob)
    row, col = iota((tokens, tokens), 0), iota((tokens, tokens), 1)
    shift = block.bit_length() - 1
    same = lax.shift_right_logical(row, shift) == lax.shift_right_logical(col, shift)
    earlier = jnp.where(same & (col < row), 1.0, 0.0).astype(BF16)
    rank = dot(earlier, member.astype(BF16))
    code = jnp.where(member > 0.0, rank, -1.0).astype(BF16)
    eye = jnp.where(row == col, 1.0, 0.0).astype(BF16)
    code_t = dot(code, eye, ((0,), (0,))).astype(BF16)
    prob_t = dot(prob.astype(BF16), eye, ((0,), (0,))).astype(BF16)

    expert, home, place = slot_parts(iota((slots, LANES), 0))
    spread = jnp.where(iota((slots, LANES), 1) == expert, 1.0, 0.0).astype(BF16)
    code_row = dot(spread, code_t)
    token_block = lax.shift_right_logical(iota((slots, tokens), 1), shift)
    chosen = (code_row == place.astype(F32)) & (token_block == home)
    select = jnp.where(chosen, 1.0, 0.0).astype(BF16)
    prob_row = jnp.sum(jnp.where(chosen, dot(spread, prob_t), 0.0), axis=1, keepdims=True)
    send_ref[:, :width] = dot(select, tok_ref[:, :width]).astype(BF16)
    grads = dot(select, tok_ref[:, width : 2 * width])
    send_ref[:, width:] = (prob_row * grads).astype(BF16)

    expert, home, place = slot_parts(iota((LANES, slots), 1))
    spread = jnp.where(iota((LANES, slots), 0) == expert, 1.0, 0.0).astype(BF16)
    code_col = dot(code, spread)
    token_block = lax.shift_right_logical(iota((tokens, slots), 0), shift)
    chosen = (code_col == place.astype(F32)) & (token_block == home)
    pick_ref[...] = jnp.where(chosen, 1.0, 0.0).astype(BF16)


def expert_kernel(rows_ref, gate_ref, up_ref, down_ref, ret_ref, part_ref):
    width, hidden_width = gate_ref.shape
    groups = part_ref.shape[0]
    share = width // groups
    down_share = hidden_width // groups
    rows = rows_ref[:, :width]
    scaled = rows_ref[:, width:]
    gate, up, down = gate_ref[...], up_ref[...], down_ref[...]
    pre_gate = dot(rows, gate)
    pre_up = dot(rows, up)
    grad_hidden = dot(scaled, down, ((1,), (1,)))
    sig = jax.nn.sigmoid(pre_gate)
    silu = pre_gate * sig
    hidden = (silu * pre_up).astype(BF16)
    prob_grad = jnp.sum(hidden.astype(F32) * grad_hidden, axis=1, keepdims=True)
    gate_grad = (grad_hidden * pre_up * sig * (1.0 + pre_gate * (1.0 - sig))).astype(BF16)
    up_grad = (grad_hidden * silu).astype(BF16)
    back = dot(gate_grad, gate, ((1,), (1,))) + dot(up_grad, up, ((1,), (1,)))
    ret_ref[:, :width] = back.astype(BF16)
    ret_ref[:, width:] = jnp.broadcast_to(prob_grad, (rows.shape[0], LANES)).astype(BF16)
    both = jnp.concatenate([gate_grad, up_grad], axis=1)
    for pair in range(groups // 2):
        columns = rows_ref[:, pair * 2 * share : (pair + 1) * 2 * share]
        part = dot(columns, both, ((0,), (0,))).astype(BF16)
        part_ref[2 * pair, :share, :] = part[:share]
        part_ref[2 * pair + 1, :share, :] = part[share:]
    half = width // 2
    for side in range(2):
        part = dot(hidden, scaled[:, side * half : (side + 1) * half], ((0,), (0,))).astype(BF16)
        for g in range(groups):
            low = share + side * down_share
            part_ref[g, low : low + down_share, :] = part[g * down_share : (g + 1) * down_share]


def combine_kernel(base_ref, back_ref, pick_ref, extra_ref, sum_ref):
    slots = back_ref.shape[0]
    width = back_ref.shape[1] - LANES
    tokens = sum_ref.shape[0]
    pick = pick_ref[...]
    sum_ref[:, :width] = dot(pick, back_ref[:, :width]).astype(BF16)
    expert, _, _ = slot_parts(iota((slots, LANES), 0))
    own = iota((slots, LANES), 1) == expert
    spread = jnp.where(own, back_ref[:, width:].astype(F32), 0.0).astype(BF16)
    by_expert = dot(pick, spread)
    extras = extra_ref[...].astype(F32)
    lane = iota((tokens, LANES), 1)
    expert_lane = served(lane, base_ref[0])
    result = jnp.zeros((tokens, LANES), F32)
    for k in range(TOP):
        hit = extras[:, k : k + 1] == expert_lane
        value = jnp.sum(jnp.where(hit, by_expert, 0.0), axis=1, keepdims=True)
        value = value / extras[:, TOP + k : TOP + k + 1]
        result = jnp.where(lane == k, value, result)
    sum_ref[:, width:] = result.astype(BF16)


def finish_kernel(sums_ref, part_ref, in_ref, prob_ref, gate_ref, up_ref, down_ref):
    width = in_ref.shape[1]
    total = sums_ref[0].astype(F32)
    for s in range(1, FAR):
        total = total + sums_ref[s].astype(F32)
    in_ref[...] = total[:, :width].astype(BF16)
    prob_ref[...] = total[:, width : width + TOP].astype(BF16)
    share, hidden_width = gate_ref.shape
    down_share = down_ref.shape[0]
    gate_ref[...] = part_ref[:share, :hidden_width].astype(F32)
    up_ref[...] = part_ref[:share, hidden_width:].astype(F32)
    half = width // 2
    down_ref[:, :half] = part_ref[share : share + down_share, :].astype(F32)
    down_ref[:, half:] = part_ref[share + down_share :, :].astype(F32)


def params(mib):
    return pltpu.CompilerParams(vmem_limit_bytes=mib * MIB)


def per_device(layer_in, grad_out, expert_ids, gate_probs, gate_weight, up_weight, down_weight):
    block, width = layer_in.shape
    hidden_width = gate_weight.shape[2]
    groups = lax.axis_size("group")
    tokens = FAR * block
    slots = NEAR * FAR * CAP
    share = width // groups
    down_share = hidden_width // groups
    part_rows = share + 2 * down_share
    moved = (lax.axis_index("group") & 1) * (NEAR // 2)
    place = lax.axis_index(("far", "near", "y")) - moved + EXPERTS
    base = (place // NEAR * NEAR + moved).astype(jnp.int32).reshape(1)
    scalar = pl.BlockSpec(memory_space=pltpu.SMEM)

    extras = jnp.concatenate([expert_ids.astype(BF16), gate_probs], axis=1)
    extras = jnp.pad(extras, ((0, 0), (0, LANES - 2 * TOP)))
    packed = jnp.concatenate([layer_in, grad_out, extras], axis=1)
    near_tokens = lax.all_gather(packed, "far", tiled=True)

    send, pick = pl.pallas_call(
        select_kernel,
        out_shape=(
            jax.ShapeDtypeStruct((slots, 2 * width), BF16),
            jax.ShapeDtypeStruct((tokens, slots), BF16),
        ),
        in_specs=[scalar] + whole(1),
        out_specs=tuple(whole(2)),
        compiler_params=params(24),
        name="select_rows",
    )(base, near_tokens)

    exchange = functools.partial(lax.all_to_all, split_axis=0, concat_axis=0, tiled=True)
    near_exchange = functools.partial(
        exchange,
        axis_name=("group", "far", "near", "y"),
        axis_index_groups=windows(groups, EXPERTS),
    )
    rows = near_exchange(send.reshape(NEAR, FAR * CAP, 2 * width)).reshape(slots, 2 * width)

    back, parts = pl.pallas_call(
        expert_kernel,
        out_shape=(
            jax.ShapeDtypeStruct((slots, width + LANES), BF16),
            jax.ShapeDtypeStruct((groups, part_rows, 2 * hidden_width), BF16),
        ),
        in_specs=whole(4),
        out_specs=tuple(whole(2)),
        compiler_params=params(40),
        name="expert_rows",
    )(rows, gate_weight[0], up_weight[0], down_weight[0])

    part_sum = lax.psum_scatter(
        parts.reshape(groups * part_rows, 2 * hidden_width), "group", scatter_dimension=0, tiled=True
    )
    back = near_exchange(back.reshape(NEAR, FAR * CAP, width + LANES)).reshape(slots, width + LANES)

    sums = pl.pallas_call(
        combine_kernel,
        out_shape=jax.ShapeDtypeStruct((tokens, width + LANES), BF16),
        in_specs=[scalar] + whole(3),
        out_specs=whole(1)[0],
        compiler_params=params(24),
        name="combine_rows",
    )(base, back, pick, near_tokens[:, 2 * width :])
    sums = exchange(sums.reshape(FAR, block, width + LANES), "far")

    grad_in, grad_probs, grad_gate, grad_up, grad_down = pl.pallas_call(
        finish_kernel,
        out_shape=(
            jax.ShapeDtypeStruct((block, width), BF16),
            jax.ShapeDtypeStruct((block, TOP), BF16),
            jax.ShapeDtypeStruct((share, hidden_width), F32),
            jax.ShapeDtypeStruct((share, hidden_width), F32),
            jax.ShapeDtypeStruct((down_share, width), F32),
        ),
        in_specs=whole(2),
        out_specs=tuple(whole(5)),
        compiler_params=params(24),
        name="finish",
    )(sums, part_sum)
    return grad_in, grad_probs, grad_gate[None], grad_up[None], grad_down[None]


def solution(mesh):
    groups, experts = mesh.devices.shape
    split = Mesh(mesh.devices.reshape(groups, FAR, 4, experts // NEAR), ("group", "far", "near", "y"))
    everywhere = ("group", "far", "near", "y")
    expert = ("far", "near", "y")
    token_spec = P(everywhere, None)
    weight_spec = P(expert, None, None)
    grad_spec = P(expert, "group", None)
    return jax.shard_map(
        per_device,
        mesh=split,
        in_specs=(token_spec,) * 4 + (weight_spec,) * 3,
        out_specs=(token_spec,) * 2 + (grad_spec,) * 3,
        check_vma=False,
    )
```

```python
import functools

import jax
import jax.numpy as jnp
from jax import lax
from jax.experimental import pallas as pl
from jax.experimental.pallas import tpu as pltpu
from jax.sharding import Mesh, PartitionSpec as P

F32 = jnp.float32
BF16 = jnp.bfloat16
LANES = 128
CAP = 6
FAR = 4
NEAR = 16
TOP = 8
EXPERTS = 64
MIB = 1 << 20


def iota(shape, dim):
    return lax.broadcasted_iota(jnp.int32, shape, dim)


def dot(a, b, contract=((1,), (0,))):
    return lax.dot_general(a, b, (contract, ((), ())), preferred_element_type=F32)


def whole(n):
    return [pl.BlockSpec(memory_space=pltpu.VMEM)] * n


def slot_parts(i):
    sixth = lax.shift_right_logical(i * 10923, 16)
    expert = lax.shift_right_logical(i * 2731, 16)
    return expert, sixth - FAR * expert, i - CAP * sixth


def served(lane, base):
    return jnp.where(lane < NEAR, (lane + base) & (EXPERTS - 1), -1).astype(F32)


def windows(groups, experts):
    lists = []
    for g in range(groups):
        for far in range(FAR):
            start = far * NEAR + (g % 2) * (NEAR // 2)
            lists.append([g * experts + (start + j) % experts for j in range(NEAR)])
    return lists


def pack_kernel(layer_ref, grad_ref, ids_ref, probs_ref, out_ref):
    width = layer_ref.shape[1]
    out_ref[:, :width] = layer_ref[...]
    out_ref[:, width : 2 * width] = grad_ref[...]
    choice, lane = iota((TOP, LANES), 0), iota((TOP, LANES), 1)
    ids_lane = jnp.where(lane == choice, 1.0, 0.0).astype(BF16)
    probs_lane = jnp.where(lane == choice + TOP, 1.0, 0.0).astype(BF16)
    ids = ids_ref[...].astype(F32).astype(BF16)
    extras = dot(ids, ids_lane, ((0,), (0,))) + dot(probs_ref[...], probs_lane, ((0,), (0,)))
    out_ref[:, 2 * width :] = extras.astype(BF16)


def select_kernel(base_ref, tok_ref, send_ref, pick_ref):
    tokens = tok_ref.shape[0]
    slots = send_ref.shape[0]
    width = send_ref.shape[1] // 2
    block = tokens // FAR
    extras = tok_ref[:, 2 * width :].astype(F32)
    lane = iota((tokens, LANES), 1)
    expert_lane = served(lane, base_ref[0])
    member = jnp.zeros((tokens, LANES), F32)
    prob = jnp.zeros((tokens, LANES), F32)
    for k in range(TOP):
        hit = extras[:, k : k + 1] == expert_lane
        member = jnp.where(hit, 1.0, member)
        prob = jnp.where(hit, extras[:, TOP + k : TOP + k + 1], prob)
    row, col = iota((tokens, tokens), 0), iota((tokens, tokens), 1)
    shift = block.bit_length() - 1
    same = lax.shift_right_logical(row, shift) == lax.shift_right_logical(col, shift)
    earlier = jnp.where(same & (col < row), 1.0, 0.0).astype(BF16)
    rank = dot(earlier, member.astype(BF16))
    code = jnp.where(member > 0.0, rank, -1.0).astype(BF16)
    eye = jnp.where(row == col, 1.0, 0.0).astype(BF16)
    code_t = dot(code, eye, ((0,), (0,))).astype(BF16)
    prob_t = dot(prob.astype(BF16), eye, ((0,), (0,))).astype(BF16)

    expert, home, place = slot_parts(iota((slots, LANES), 0))
    spread = jnp.where(iota((slots, LANES), 1) == expert, 1.0, 0.0).astype(BF16)
    code_row = dot(spread, code_t)
    token_block = lax.shift_right_logical(iota((slots, tokens), 1), shift)
    chosen = (code_row == place.astype(F32)) & (token_block == home)
    select = jnp.where(chosen, 1.0, 0.0).astype(BF16)
    prob_row = jnp.sum(jnp.where(chosen, dot(spread, prob_t), 0.0), axis=1, keepdims=True)
    send_ref[:, :width] = dot(select, tok_ref[:, :width]).astype(BF16)
    grads = dot(select, tok_ref[:, width : 2 * width])
    send_ref[:, width:] = (prob_row * grads).astype(BF16)

    expert, home, place = slot_parts(iota((LANES, slots), 1))
    spread = jnp.where(iota((LANES, slots), 0) == expert, 1.0, 0.0).astype(BF16)
    code_col = dot(code, spread)
    token_block = lax.shift_right_logical(iota((tokens, slots), 0), shift)
    chosen = (code_col == place.astype(F32)) & (token_block == home)
    pick_ref[...] = jnp.where(chosen, 1.0, 0.0).astype(BF16)


def expert_kernel(rows_ref, gate_ref, up_ref, down_ref, ret_ref, both_ref, hidden_ref):
    width, hidden_width = gate_ref.shape
    scaled = rows_ref[:, width:]
    rows = rows_ref[:, :width]
    gate, up, down = gate_ref[...], up_ref[...], down_ref[...]
    pre_gate = dot(rows, gate)
    pre_up = dot(rows, up)
    grad_hidden = dot(scaled, down, ((1,), (1,)))
    sig = jax.nn.sigmoid(pre_gate)
    silu = pre_gate * sig
    hidden = (silu * pre_up).astype(BF16)
    prob_grad = jnp.sum(hidden.astype(F32) * grad_hidden, axis=1, keepdims=True)
    gate_grad = (grad_hidden * pre_up * sig * (1.0 + pre_gate * (1.0 - sig))).astype(BF16)
    up_grad = (grad_hidden * silu).astype(BF16)
    back = dot(gate_grad, gate, ((1,), (1,))) + dot(up_grad, up, ((1,), (1,)))
    ret_ref[:, :width] = back.astype(BF16)
    ret_ref[:, width:] = jnp.broadcast_to(prob_grad, (rows.shape[0], LANES)).astype(BF16)
    both_ref[:, :hidden_width] = gate_grad
    both_ref[:, hidden_width:] = up_grad
    hidden_ref[...] = hidden


def part_kernel(core_ref, rows_ref, both_ref, hidden_ref, keep_ref, give_ref):
    chips, part_rows, columns = keep_ref.shape
    hidden_width = hidden_ref.shape[1]
    width = rows_ref.shape[1] // 2
    share = width // (2 * chips)
    down_share = hidden_width // (2 * chips)
    first = core_ref[0] == 0

    def put(chip, low, pair):
        size = pair.shape[0] // 2
        keep_ref[chip, low : low + size, :] = jnp.where(first, pair[:size], pair[size:]).astype(BF16)
        give_ref[chip, low : low + size, :] = jnp.where(first, pair[size:], pair[:size]).astype(BF16)

    both = both_ref[...]
    for chip in range(chips):
        rows = rows_ref[:, chip * 2 * share : (chip + 1) * 2 * share]
        put(chip, 0, dot(rows, both, ((0,), (0,))))
    hidden = hidden_ref[...]
    half = width // 2
    for side in range(2):
        part = dot(hidden, rows_ref[:, width + side * half : width + (side + 1) * half], ((0,), (0,)))
        for chip in range(chips):
            put(chip, share + side * down_share, part[chip * 2 * down_share : (chip + 1) * 2 * down_share])


def chip_sum_kernel(chip_ref, keep_ref, got_ref, *out_refs):
    chips = keep_ref.shape[0]
    for s, out_ref in enumerate(out_refs):
        chip = (chip_ref[0] + s) & (chips - 1)
        out_ref[...] = (keep_ref[chip].astype(F32) + got_ref[chip].astype(F32)).astype(BF16)


def combine_kernel(base_ref, back_ref, pick_ref, extra_ref, sum_ref):
    slots = back_ref.shape[0]
    width = back_ref.shape[1] - LANES
    tokens = sum_ref.shape[0]
    pick = pick_ref[...]
    sum_ref[:, :width] = dot(pick, back_ref[:, :width]).astype(BF16)
    expert, _, _ = slot_parts(iota((slots, LANES), 0))
    own = iota((slots, LANES), 1) == expert
    spread = jnp.where(own, back_ref[:, width:].astype(F32), 0.0).astype(BF16)
    by_expert = dot(pick, spread)
    extras = extra_ref[...].astype(F32)
    lane = iota((tokens, LANES), 1)
    expert_lane = served(lane, base_ref[0])
    result = jnp.zeros((tokens, LANES), F32)
    for k in range(TOP):
        hit = extras[:, k : k + 1] == expert_lane
        value = jnp.sum(jnp.where(hit, by_expert, 0.0), axis=1, keepdims=True)
        value = value / extras[:, TOP + k : TOP + k + 1]
        result = jnp.where(lane == k, value, result)
    sum_ref[:, width:] = result.astype(BF16)


def finish_kernel(*refs):
    sums_ref, part_refs = refs[0], refs[1:-5]
    in_ref, prob_ref, gate_ref, up_ref, down_ref = refs[-5:]
    width = in_ref.shape[1]
    total = sums_ref[0].astype(F32)
    for s in range(1, FAR):
        total = total + sums_ref[s].astype(F32)
    in_ref[...] = total[:, :width].astype(BF16)
    pick = jnp.where(iota((TOP, LANES), 0) == iota((TOP, LANES), 1), 1.0, 0.0).astype(BF16)
    prob_ref[...] = dot(pick, total[:, width:].astype(BF16), ((1,), (1,))).astype(BF16)
    share, hidden_width = gate_ref.shape
    down_share = down_ref.shape[0]
    half = width // 2

    def part(low, size):
        result = part_refs[0][low : low + size, :].astype(F32)
        for ref in part_refs[1:]:
            result = result + ref[low : low + size, :].astype(F32)
        return result

    gate_up = part(0, share)
    gate_ref[...] = gate_up[:, :hidden_width]
    up_ref[...] = gate_up[:, hidden_width:]
    down_ref[:, :half] = part(share, down_share)
    down_ref[:, half:] = part(share + down_share, down_share)


def params(mib):
    return pltpu.CompilerParams(vmem_limit_bytes=mib * MIB)


def cost(flops, nbytes):
    return pl.CostEstimate(flops=flops, bytes_accessed=nbytes, transcendentals=0)


def per_device(layer_in, grad_out, expert_ids, gate_probs, gate_weight, up_weight, down_weight):
    block, width = layer_in.shape
    hidden_width = gate_weight.shape[2]
    chips = lax.axis_size("x")
    groups = 2 * chips
    tokens = FAR * block
    slots = NEAR * FAR * CAP
    share = width // groups
    down_share = hidden_width // groups
    part_rows = share + 2 * down_share
    core = lax.axis_index("core").astype(jnp.int32)
    chip = lax.axis_index("x").astype(jnp.int32)
    moved = core * (NEAR // 2)
    place = lax.axis_index(("far", "near", "y")) - moved + EXPERTS
    base = ((place & -NEAR) + moved).astype(jnp.int32).reshape(1)
    scalar = pl.BlockSpec(memory_space=pltpu.SMEM)

    def shape(*dims):
        return jax.ShapeDtypeStruct(dims, BF16)

    packed = pl.pallas_call(
        pack_kernel,
        out_shape=shape(block, 2 * width + LANES),
        in_specs=whole(4),
        out_specs=whole(1)[0],
        compiler_params=params(8),
        name="pack_tokens",
    )(layer_in, grad_out, expert_ids.T, gate_probs.T)
    near_tokens = lax.all_gather(packed, "far", tiled=True)

    send, pick = pl.pallas_call(
        select_kernel,
        out_shape=(shape(slots, 2 * width), shape(tokens, slots)),
        in_specs=[scalar] + whole(1),
        out_specs=tuple(whole(2)),
        compiler_params=params(24),
        name="select_rows",
    )(base, near_tokens)

    exchange = functools.partial(lax.all_to_all, split_axis=0, concat_axis=0, tiled=True)
    near_exchange = functools.partial(
        exchange,
        axis_name=("x", "core", "far", "near", "y"),
        axis_index_groups=windows(groups, EXPERTS),
    )
    rows = near_exchange(send.reshape(NEAR, FAR * CAP, 2 * width)).reshape(slots, 2 * width)

    matmul = 2 * slots * width * hidden_width
    back, both, hidden = pl.pallas_call(
        expert_kernel,
        out_shape=(shape(slots, width + LANES), shape(slots, 2 * hidden_width), shape(slots, hidden_width)),
        in_specs=whole(4),
        out_specs=tuple(whole(3)),
        compiler_params=params(32),
        cost_estimate=cost(5 * matmul, 8 * MIB),
        name="expert_rows",
    )(rows, gate_weight[0], up_weight[0], down_weight[0])
    back = near_exchange(back.reshape(NEAR, FAR * CAP, width + LANES)).reshape(slots, width + LANES)

    keep, give = pl.pallas_call(
        part_kernel,
        out_shape=(shape(chips, part_rows, 2 * hidden_width),) * 2,
        in_specs=[scalar] + whole(3),
        out_specs=tuple(whole(2)),
        compiler_params=params(32),
        cost_estimate=cost(3 * matmul, 8 * MIB),
        name="weight_parts",
    )(core.reshape(1), rows, both, hidden)
    got = lax.ppermute(give, "core", [(0, 1), (1, 0)])
    chip_sums = pl.pallas_call(
        chip_sum_kernel,
        out_shape=(shape(part_rows, 2 * hidden_width),) * chips,
        in_specs=[scalar] + whole(2),
        out_specs=tuple(whole(chips)),
        compiler_params=params(16),
        cost_estimate=cost(MIB, 6 * MIB),
        name="chip_sums",
    )(chip.reshape(1), keep, got)
    parts = [chip_sums[0]] + [
        lax.ppermute(chip_sums[s], "x", [(i, (i + s) % chips) for i in range(chips)]) for s in range(1, chips)
    ]

    sums = pl.pallas_call(
        combine_kernel,
        out_shape=shape(tokens, width + LANES),
        in_specs=[scalar] + whole(3),
        out_specs=whole(1)[0],
        compiler_params=params(24),
        name="combine_rows",
    )(base, back, pick, near_tokens[:, 2 * width :])
    sums = exchange(sums.reshape(FAR, block, width + LANES), "far")

    grad_in, grad_probs, grad_gate, grad_up, grad_down = pl.pallas_call(
        finish_kernel,
        out_shape=(
            shape(block, width),
            shape(TOP, block),
            jax.ShapeDtypeStruct((share, hidden_width), F32),
            jax.ShapeDtypeStruct((share, hidden_width), F32),
            jax.ShapeDtypeStruct((down_share, width), F32),
        ),
        in_specs=whole(1 + chips),
        out_specs=tuple(whole(5)),
        compiler_params=params(24),
        name="finish",
    )(sums, *parts)
    return grad_in, grad_probs.T, grad_gate[None], grad_up[None], grad_down[None]


def solution(mesh):
    groups, experts = mesh.devices.shape
    split = Mesh(
        mesh.devices.reshape(groups // 2, 2, FAR, 4, experts // NEAR), ("x", "core", "far", "near", "y")
    )
    expert = ("far", "near", "y")
    token_spec = P(("x", "core") + expert, None)
    weight_spec = P(expert, None, None)
    grad_spec = P(expert, ("x", "core"), None)
    return jax.shard_map(
        per_device,
        mesh=split,
        in_specs=(token_spec,) * 4 + (weight_spec,) * 3,
        out_specs=(token_spec,) * 2 + (grad_spec,) * 3,
        check_vma=False,
    )
```

```python
import functools

import jax
import jax.numpy as jnp
from jax import lax
from jax.experimental import pallas as pl
from jax.experimental.pallas import tpu as pltpu
from jax.sharding import Mesh, PartitionSpec as P

F32 = jnp.float32
BF16 = jnp.bfloat16
LANES = 128
CAP = 6
FAR = 4
NEAR = 16
TOP = 8
EXPERTS = 64
MIB = 1 << 20


def iota(shape, dim):
    return lax.broadcasted_iota(jnp.int32, shape, dim)


def dot(a, b, contract=((1,), (0,))):
    return lax.dot_general(a, b, (contract, ((), ())), preferred_element_type=F32)


def whole(n):
    return [pl.BlockSpec(memory_space=pltpu.VMEM)] * n


def slot_parts(i):
    sixth = lax.shift_right_logical(i * 10923, 16)
    expert = lax.shift_right_logical(i * 2731, 16)
    return expert, sixth - FAR * expert, i - CAP * sixth


def served(lane, base):
    return jnp.where(lane < NEAR, (lane + base) & (EXPERTS - 1), -1).astype(F32)


def windows(groups, experts):
    lists = []
    for g in range(groups):
        for far in range(FAR):
            start = far * NEAR + (g % 2) * (NEAR // 2)
            lists.append([g * experts + (start + j) % experts for j in range(NEAR)])
    return lists


def pack_kernel(layer_ref, grad_ref, ids_ref, probs_ref, out_ref, ids_vmem, sems):
    width = layer_ref.shape[1]
    copies = [
        pltpu.make_async_copy(ids_ref, ids_vmem, sems.at[0]),
        pltpu.make_async_copy(layer_ref, out_ref.at[:, :width], sems.at[1]),
        pltpu.make_async_copy(grad_ref, out_ref.at[:, width : 2 * width], sems.at[2]),
    ]
    for copy in copies:
        copy.start()
    choice, lane = iota((TOP, LANES), 0), iota((TOP, LANES), 1)
    ids_lane = jnp.where(lane == choice, 1.0, 0.0).astype(BF16)
    probs_lane = jnp.where(lane == choice + TOP, 1.0, 0.0).astype(BF16)
    copies[0].wait()
    ids = ids_vmem[...].astype(F32).astype(BF16)
    extras = dot(ids, ids_lane, ((0,), (0,))) + dot(probs_ref[...], probs_lane, ((0,), (0,)))
    out_ref[:, 2 * width :] = extras.astype(BF16)
    copies[1].wait()
    copies[2].wait()


def select_kernel(base_ref, tok_ref, send_ref, pick_ref):
    tokens = tok_ref.shape[0]
    slots = send_ref.shape[0]
    width = send_ref.shape[1] // 2
    block = tokens // FAR
    extras = tok_ref[:, 2 * width :].astype(F32)
    lane = iota((tokens, LANES), 1)
    expert_lane = served(lane, base_ref[0])
    member = jnp.zeros((tokens, LANES), F32)
    prob = jnp.zeros((tokens, LANES), F32)
    for k in range(TOP):
        hit = extras[:, k : k + 1] == expert_lane
        member = jnp.where(hit, 1.0, member)
        prob = jnp.where(hit, extras[:, TOP + k : TOP + k + 1], prob)
    row, col = iota((tokens, tokens), 0), iota((tokens, tokens), 1)
    shift = block.bit_length() - 1
    same = lax.shift_right_logical(row, shift) == lax.shift_right_logical(col, shift)
    earlier = jnp.where(same & (col < row), 1.0, 0.0).astype(BF16)
    rank = dot(earlier, member.astype(BF16))
    code = jnp.where(member > 0.0, rank, -1.0).astype(BF16)
    eye = jnp.where(row == col, 1.0, 0.0).astype(BF16)
    code_t = dot(code, eye, ((0,), (0,))).astype(BF16)
    prob_t = dot(prob.astype(BF16), eye, ((0,), (0,))).astype(BF16)

    expert, home, place = slot_parts(iota((slots, LANES), 0))
    spread = jnp.where(iota((slots, LANES), 1) == expert, 1.0, 0.0).astype(BF16)
    code_row = dot(spread, code_t)
    token_block = lax.shift_right_logical(iota((slots, tokens), 1), shift)
    chosen = (code_row == place.astype(F32)) & (token_block == home)
    select = jnp.where(chosen, 1.0, 0.0).astype(BF16)
    prob_row = jnp.sum(jnp.where(chosen, dot(spread, prob_t), 0.0), axis=1, keepdims=True)
    send_ref[:, :width] = dot(select, tok_ref[:, :width]).astype(BF16)
    grads = dot(select, tok_ref[:, width : 2 * width])
    send_ref[:, width:] = (prob_row * grads).astype(BF16)

    expert, home, place = slot_parts(iota((LANES, slots), 1))
    spread = jnp.where(iota((LANES, slots), 0) == expert, 1.0, 0.0).astype(BF16)
    code_col = dot(code, spread)
    token_block = lax.shift_right_logical(iota((tokens, slots), 0), shift)
    chosen = (code_col == place.astype(F32)) & (token_block == home)
    pick_ref[...] = jnp.where(chosen, 1.0, 0.0).astype(BF16)


def expert_kernel(rows_ref, gate_ref, up_ref, down_ref, ret_ref, both_ref, hidden_ref):
    width, hidden_width = gate_ref.shape
    scaled = rows_ref[:, width:]
    rows = rows_ref[:, :width]
    gate, up, down = gate_ref[...], up_ref[...], down_ref[...]
    pre_gate = dot(rows, gate)
    pre_up = dot(rows, up)
    grad_hidden = dot(scaled, down, ((1,), (1,)))
    sig = jax.nn.sigmoid(pre_gate)
    silu = pre_gate * sig
    hidden = (silu * pre_up).astype(BF16)
    prob_grad = jnp.sum(hidden.astype(F32) * grad_hidden, axis=1, keepdims=True)
    gate_grad = (grad_hidden * pre_up * sig * (1.0 + pre_gate * (1.0 - sig))).astype(BF16)
    up_grad = (grad_hidden * silu).astype(BF16)
    back = dot(gate_grad, gate, ((1,), (1,))) + dot(up_grad, up, ((1,), (1,)))
    ret_ref[:, :width] = back.astype(BF16)
    ret_ref[:, width:] = jnp.broadcast_to(prob_grad, (rows.shape[0], LANES)).astype(BF16)
    both_ref[:, :hidden_width] = gate_grad
    both_ref[:, hidden_width:] = up_grad
    hidden_ref[...] = hidden


def part_kernel(core_ref, rows_ref, both_ref, hidden_ref, keep_ref, give_ref):
    chips, part_rows, columns = keep_ref.shape
    hidden_width = hidden_ref.shape[1]
    width = rows_ref.shape[1] // 2
    share = width // (2 * chips)
    down_share = hidden_width // (2 * chips)
    first = core_ref[0] == 0

    def put(chip, low, pair):
        size = pair.shape[0] // 2
        keep_ref[chip, low : low + size, :] = jnp.where(first, pair[:size], pair[size:]).astype(BF16)
        give_ref[chip, low : low + size, :] = jnp.where(first, pair[size:], pair[:size]).astype(BF16)

    both = both_ref[...]
    for chip in range(chips):
        rows = rows_ref[:, chip * 2 * share : (chip + 1) * 2 * share]
        put(chip, 0, dot(rows, both, ((0,), (0,))))
    hidden = hidden_ref[...]
    half = width // 2
    for side in range(2):
        part = dot(hidden, rows_ref[:, width + side * half : width + (side + 1) * half], ((0,), (0,)))
        for chip in range(chips):
            put(chip, share + side * down_share, part[chip * 2 * down_share : (chip + 1) * 2 * down_share])


def chip_sum_kernel(chip_ref, keep_ref, got_ref, *out_refs):
    chips = keep_ref.shape[0]
    for s, out_ref in enumerate(out_refs):
        chip = (chip_ref[0] + s) & (chips - 1)
        out_ref[...] = (keep_ref[chip].astype(F32) + got_ref[chip].astype(F32)).astype(BF16)


def combine_kernel(base_ref, back_ref, pick_ref, extra_ref, sum_ref):
    slots = back_ref.shape[0]
    width = back_ref.shape[1] - LANES
    tokens = sum_ref.shape[0]
    pick = pick_ref[...]
    sum_ref[:, :width] = dot(pick, back_ref[:, :width]).astype(BF16)
    expert, _, _ = slot_parts(iota((slots, LANES), 0))
    own = iota((slots, LANES), 1) == expert
    spread = jnp.where(own, back_ref[:, width:].astype(F32), 0.0).astype(BF16)
    by_expert = dot(pick, spread)
    extras = extra_ref[...].astype(F32)
    lane = iota((tokens, LANES), 1)
    expert_lane = served(lane, base_ref[0])
    result = jnp.zeros((tokens, LANES), F32)
    for k in range(TOP):
        hit = extras[:, k : k + 1] == expert_lane
        value = jnp.sum(jnp.where(hit, by_expert, 0.0), axis=1, keepdims=True)
        value = value / extras[:, TOP + k : TOP + k + 1]
        result = jnp.where(lane == k, value, result)
    sum_ref[:, width:] = result.astype(BF16)


def finish_kernel(*refs):
    sums_ref, part_refs = refs[0], refs[1:-5]
    in_ref, prob_ref, gate_ref, up_ref, down_ref = refs[-5:]
    width = in_ref.shape[1]
    total = sums_ref[0].astype(F32)
    for s in range(1, FAR):
        total = total + sums_ref[s].astype(F32)
    in_ref[...] = total[:, :width].astype(BF16)
    pick = jnp.where(iota((TOP, LANES), 0) == iota((TOP, LANES), 1), 1.0, 0.0).astype(BF16)
    prob_ref[...] = dot(pick, total[:, width:].astype(BF16), ((1,), (1,))).astype(BF16)
    share, hidden_width = gate_ref.shape
    down_share = down_ref.shape[0]
    half = width // 2

    def part(low, size):
        result = part_refs[0][low : low + size, :].astype(F32)
        for ref in part_refs[1:]:
            result = result + ref[low : low + size, :].astype(F32)
        return result

    gate_up = part(0, share)
    gate_ref[...] = gate_up[:, :hidden_width]
    up_ref[...] = gate_up[:, hidden_width:]
    down_ref[:, :half] = part(share, down_share)
    down_ref[:, half:] = part(share + down_share, down_share)


def params(mib):
    return pltpu.CompilerParams(vmem_limit_bytes=mib * MIB)


def cost(flops, nbytes):
    return pl.CostEstimate(flops=flops, bytes_accessed=nbytes, transcendentals=0)


def per_device(layer_in, grad_out, expert_ids, gate_probs, gate_weight, up_weight, down_weight):
    block, width = layer_in.shape
    hidden_width = gate_weight.shape[2]
    chips = lax.axis_size("x")
    groups = 2 * chips
    tokens = FAR * block
    slots = NEAR * FAR * CAP
    share = width // groups
    down_share = hidden_width // groups
    part_rows = share + 2 * down_share
    core = lax.axis_index("core").astype(jnp.int32)
    chip = lax.axis_index("x").astype(jnp.int32)
    moved = core * (NEAR // 2)
    place = lax.axis_index(("far", "near", "y")) - moved + EXPERTS
    base = ((place & -NEAR) + moved).astype(jnp.int32).reshape(1)
    scalar = pl.BlockSpec(memory_space=pltpu.SMEM)

    def shape(*dims):
        return jax.ShapeDtypeStruct(dims, BF16)

    packed = pl.pallas_call(
        pack_kernel,
        out_shape=shape(block, 2 * width + LANES),
        in_specs=[pl.BlockSpec(memory_space=pltpu.HBM)] * 3 + whole(1),
        out_specs=whole(1)[0],
        scratch_shapes=[pltpu.VMEM((TOP, block), jnp.int32), pltpu.SemaphoreType.DMA((3,))],
        compiler_params=params(8),
        name="pack_tokens",
    )(layer_in, grad_out, expert_ids.T, gate_probs.T)
    near_tokens = lax.all_gather(packed, "far", tiled=True)

    send, pick = pl.pallas_call(
        select_kernel,
        out_shape=(shape(slots, 2 * width), shape(tokens, slots)),
        in_specs=[scalar] + whole(1),
        out_specs=tuple(whole(2)),
        compiler_params=params(24),
        name="select_rows",
    )(base, near_tokens)

    exchange = functools.partial(lax.all_to_all, split_axis=0, concat_axis=0, tiled=True)
    near_exchange = functools.partial(
        exchange,
        axis_name=("x", "core", "far", "near", "y"),
        axis_index_groups=windows(groups, EXPERTS),
    )
    rows = near_exchange(send.reshape(NEAR, FAR * CAP, 2 * width)).reshape(slots, 2 * width)

    matmul = 2 * slots * width * hidden_width
    back, both, hidden = pl.pallas_call(
        expert_kernel,
        out_shape=(shape(slots, width + LANES), shape(slots, 2 * hidden_width), shape(slots, hidden_width)),
        in_specs=whole(4),
        out_specs=tuple(whole(3)),
        compiler_params=params(32),
        cost_estimate=cost(5 * matmul, 8 * MIB),
        name="expert_rows",
    )(rows, gate_weight[0], up_weight[0], down_weight[0])
    back = near_exchange(back.reshape(NEAR, FAR * CAP, width + LANES)).reshape(slots, width + LANES)

    keep, give = pl.pallas_call(
        part_kernel,
        out_shape=(shape(chips, part_rows, 2 * hidden_width),) * 2,
        in_specs=[scalar] + whole(3),
        out_specs=tuple(whole(2)),
        compiler_params=params(32),
        cost_estimate=cost(3 * matmul, 8 * MIB),
        name="weight_parts",
    )(core.reshape(1), rows, both, hidden)
    got = lax.ppermute(give, "core", [(0, 1), (1, 0)])
    chip_sums = pl.pallas_call(
        chip_sum_kernel,
        out_shape=(shape(part_rows, 2 * hidden_width),) * chips,
        in_specs=[scalar] + whole(2),
        out_specs=tuple(whole(chips)),
        compiler_params=params(16),
        cost_estimate=cost(MIB, 6 * MIB),
        name="chip_sums",
    )(chip.reshape(1), keep, got)
    parts = [chip_sums[0]] + [
        lax.ppermute(chip_sums[s], "x", [(i, (i + s) % chips) for i in range(chips)]) for s in range(1, chips)
    ]

    back, _ = lax.optimization_barrier((back, chip_sums[0]))
    sums = pl.pallas_call(
        combine_kernel,
        out_shape=shape(tokens, width + LANES),
        in_specs=[scalar] + whole(3),
        out_specs=whole(1)[0],
        compiler_params=params(24),
        name="combine_rows",
    )(base, back, pick, near_tokens[:, 2 * width :])
    sums = exchange(sums.reshape(FAR, block, width + LANES), "far")

    grad_in, grad_probs, grad_gate, grad_up, grad_down = pl.pallas_call(
        finish_kernel,
        out_shape=(
            shape(block, width),
            shape(TOP, block),
            jax.ShapeDtypeStruct((share, hidden_width), F32),
            jax.ShapeDtypeStruct((share, hidden_width), F32),
            jax.ShapeDtypeStruct((down_share, width), F32),
        ),
        in_specs=whole(1 + chips),
        out_specs=tuple(whole(5)),
        compiler_params=params(24),
        name="finish",
    )(sums, *parts)
    return grad_in, grad_probs.T, grad_gate[None], grad_up[None], grad_down[None]


def solution(mesh):
    groups, experts = mesh.devices.shape
    split = Mesh(
        mesh.devices.reshape(groups // 2, 2, FAR, 4, experts // NEAR), ("x", "core", "far", "near", "y")
    )
    expert = ("far", "near", "y")
    token_spec = P(("x", "core") + expert, None)
    weight_spec = P(expert, None, None)
    grad_spec = P(expert, ("x", "core"), None)
    return jax.shard_map(
        per_device,
        mesh=split,
        in_specs=(token_spec,) * 4 + (weight_spec,) * 3,
        out_specs=(token_spec,) * 2 + (grad_spec,) * 3,
        check_vma=False,
    )
```

```python
import functools

import jax
import jax.numpy as jnp
from jax import lax
from jax.experimental import pallas as pl
from jax.experimental.pallas import tpu as pltpu
from jax.sharding import Mesh, PartitionSpec as P

F32 = jnp.float32
BF16 = jnp.bfloat16
LANES = 128
CAP = 6
FAR = 4
NEAR = 16
TOP = 8
EXPERTS = 64
MIB = 1 << 20


def iota(shape, dim):
    return lax.broadcasted_iota(jnp.int32, shape, dim)


def dot(a, b, contract=((1,), (0,))):
    return lax.dot_general(a, b, (contract, ((), ())), preferred_element_type=F32)


def whole(n):
    return [pl.BlockSpec(memory_space=pltpu.VMEM)] * n


def slot_parts(i):
    sixth = lax.shift_right_logical(i * 10923, 16)
    expert = lax.shift_right_logical(i * 2731, 16)
    return expert, sixth - FAR * expert, i - CAP * sixth


def served(lane, base):
    return jnp.where(lane < NEAR, (lane + base) & (EXPERTS - 1), -1).astype(F32)


def windows(groups, experts):
    lists = []
    for g in range(groups):
        for far in range(FAR):
            start = far * NEAR + (g % 2) * (NEAR // 2)
            lists.append([g * experts + (start + j) % experts for j in range(NEAR)])
    return lists


def pack_kernel(layer_ref, grad_ref, ids_ref, probs_ref, out_ref, ids_vmem, sems):
    width = layer_ref.shape[1]
    copies = [
        pltpu.make_async_copy(ids_ref, ids_vmem, sems.at[0]),
        pltpu.make_async_copy(layer_ref, out_ref.at[:, :width], sems.at[1]),
        pltpu.make_async_copy(grad_ref, out_ref.at[:, width : 2 * width], sems.at[2]),
    ]
    for copy in copies:
        copy.start()
    choice, lane = iota((TOP, LANES), 0), iota((TOP, LANES), 1)
    ids_lane = jnp.where(lane == choice, 1.0, 0.0).astype(BF16)
    probs_lane = jnp.where(lane == choice + TOP, 1.0, 0.0).astype(BF16)
    copies[0].wait()
    ids = ids_vmem[...].astype(F32).astype(BF16)
    extras = dot(ids, ids_lane, ((0,), (0,))) + dot(probs_ref[...], probs_lane, ((0,), (0,)))
    out_ref[:, 2 * width :] = extras.astype(BF16)
    copies[1].wait()
    copies[2].wait()


def select_kernel(base_ref, tok_ref, send_ref, pick_ref):
    tokens = tok_ref.shape[0]
    slots = send_ref.shape[0]
    width = send_ref.shape[1] // 2
    block = tokens // FAR
    extras = tok_ref[:, 2 * width :].astype(F32)
    lane = iota((tokens, LANES), 1)
    expert_lane = served(lane, base_ref[0])
    member = jnp.zeros((tokens, LANES), F32)
    prob = jnp.zeros((tokens, LANES), F32)
    for k in range(TOP):
        hit = extras[:, k : k + 1] == expert_lane
        member = jnp.where(hit, 1.0, member)
        prob = jnp.where(hit, extras[:, TOP + k : TOP + k + 1], prob)
    row, col = iota((tokens, tokens), 0), iota((tokens, tokens), 1)
    shift = block.bit_length() - 1
    same = lax.shift_right_logical(row, shift) == lax.shift_right_logical(col, shift)
    earlier = jnp.where(same & (col < row), 1.0, 0.0).astype(BF16)
    rank = dot(earlier, member.astype(BF16))
    code = jnp.where(member > 0.0, rank, -1.0).astype(BF16)
    eye = jnp.where(row == col, 1.0, 0.0).astype(BF16)
    code_t = dot(code, eye, ((0,), (0,))).astype(BF16)
    prob_t = dot(prob.astype(BF16), eye, ((0,), (0,))).astype(BF16)

    expert, home, place = slot_parts(iota((slots, LANES), 0))
    spread = jnp.where(iota((slots, LANES), 1) == expert, 1.0, 0.0).astype(BF16)
    code_row = dot(spread, code_t)
    token_block = lax.shift_right_logical(iota((slots, tokens), 1), shift)
    chosen = (code_row == place.astype(F32)) & (token_block == home)
    select = jnp.where(chosen, 1.0, 0.0).astype(BF16)
    prob_row = jnp.sum(jnp.where(chosen, dot(spread, prob_t), 0.0), axis=1, keepdims=True)
    send_ref[:, :width] = dot(select, tok_ref[:, :width]).astype(BF16)
    grads = dot(select, tok_ref[:, width : 2 * width])
    send_ref[:, width:] = (prob_row * grads).astype(BF16)

    expert, home, place = slot_parts(iota((LANES, slots), 1))
    spread = jnp.where(iota((LANES, slots), 0) == expert, 1.0, 0.0).astype(BF16)
    code_col = dot(code, spread)
    token_block = lax.shift_right_logical(iota((tokens, slots), 0), shift)
    chosen = (code_col == place.astype(F32)) & (token_block == home)
    pick_ref[...] = jnp.where(chosen, 1.0, 0.0).astype(BF16)


def expert_kernel(rows_ref, gate_ref, up_ref, down_ref, ret_ref, both_ref, hidden_ref):
    width, hidden_width = gate_ref.shape
    scaled = rows_ref[:, width:]
    rows = rows_ref[:, :width]
    gate, up, down = gate_ref[...], up_ref[...], down_ref[...]
    pre_gate = dot(rows, gate)
    pre_up = dot(rows, up)
    grad_hidden = dot(scaled, down, ((1,), (1,)))
    sig = jax.nn.sigmoid(pre_gate)
    silu = pre_gate * sig
    hidden = (silu * pre_up).astype(BF16)
    prob_grad = jnp.sum(hidden.astype(F32) * grad_hidden, axis=1, keepdims=True)
    gate_grad = (grad_hidden * pre_up * sig * (1.0 + pre_gate * (1.0 - sig))).astype(BF16)
    up_grad = (grad_hidden * silu).astype(BF16)
    back = dot(gate_grad, gate, ((1,), (1,))) + dot(up_grad, up, ((1,), (1,)))
    ret_ref[:, :width] = back.astype(BF16)
    ret_ref[:, width:] = jnp.broadcast_to(prob_grad, (rows.shape[0], LANES)).astype(BF16)
    both_ref[:, :hidden_width] = gate_grad
    both_ref[:, hidden_width:] = up_grad
    hidden_ref[...] = hidden


def part_kernel(core_ref, rows_ref, both_ref, hidden_ref, keep_ref, give_ref):
    chips, part_rows, columns = keep_ref.shape
    hidden_width = hidden_ref.shape[1]
    width = rows_ref.shape[1] // 2
    share = width // (2 * chips)
    down_share = hidden_width // (2 * chips)
    first = core_ref[0] == 0

    def put(chip, low, pair):
        size = pair.shape[0] // 2
        keep_ref[chip, low : low + size, :] = jnp.where(first, pair[:size], pair[size:]).astype(BF16)
        give_ref[chip, low : low + size, :] = jnp.where(first, pair[size:], pair[:size]).astype(BF16)

    both = both_ref[...]
    for chip in range(chips):
        rows = rows_ref[:, chip * 2 * share : (chip + 1) * 2 * share]
        put(chip, 0, dot(rows, both, ((0,), (0,))))
    hidden = hidden_ref[...]
    half = width // 2
    for side in range(2):
        part = dot(hidden, rows_ref[:, width + side * half : width + (side + 1) * half], ((0,), (0,)))
        for chip in range(chips):
            put(chip, share + side * down_share, part[chip * 2 * down_share : (chip + 1) * 2 * down_share])


def chip_sum_kernel(chip_ref, keep_ref, got_ref, own_ref, right_ref, left_ref, far_low_ref, far_high_ref):
    chips, part_rows, _ = keep_ref.shape
    half = part_rows // 2

    def total(s, low, size):
        chip = (chip_ref[0] + s) & (chips - 1)
        rows = pl.ds(low, size)
        return (keep_ref[chip, rows].astype(F32) + got_ref[chip, rows].astype(F32)).astype(BF16)

    far_low_ref[...] = total(2, 0, half)
    far_high_ref[...] = total(2, half, half)
    own_ref[...] = total(0, 0, part_rows)
    right_ref[...] = total(1, 0, part_rows)
    left_ref[...] = total(3, 0, part_rows)


def relay_kernel(right_ref, left_ref, low_ref, high_ref, to_right_ref, to_left_ref):
    half = low_ref.shape[0]
    to_right_ref[:half] = (right_ref[:half].astype(F32) + low_ref[...].astype(F32)).astype(BF16)
    to_right_ref[half:] = right_ref[half:]
    to_left_ref[:half] = left_ref[:half]
    to_left_ref[half:] = (left_ref[half:].astype(F32) + high_ref[...].astype(F32)).astype(BF16)


def combine_kernel(base_ref, back_ref, pick_ref, extra_ref, sum_ref):
    slots = back_ref.shape[0]
    width = back_ref.shape[1] - LANES
    tokens = sum_ref.shape[0]
    pick = pick_ref[...]
    sum_ref[:, :width] = dot(pick, back_ref[:, :width]).astype(BF16)
    expert, _, _ = slot_parts(iota((slots, LANES), 0))
    own = iota((slots, LANES), 1) == expert
    spread = jnp.where(own, back_ref[:, width:].astype(F32), 0.0).astype(BF16)
    by_expert = dot(pick, spread)
    extras = extra_ref[...].astype(F32)
    lane = iota((tokens, LANES), 1)
    expert_lane = served(lane, base_ref[0])
    result = jnp.zeros((tokens, LANES), F32)
    for k in range(TOP):
        hit = extras[:, k : k + 1] == expert_lane
        value = jnp.sum(jnp.where(hit, by_expert, 0.0), axis=1, keepdims=True)
        value = value / extras[:, TOP + k : TOP + k + 1]
        result = jnp.where(lane == k, value, result)
    sum_ref[:, width:] = result.astype(BF16)


def finish_kernel(*refs):
    sums_ref, part_refs = refs[0], refs[1:-5]
    in_ref, prob_ref, gate_ref, up_ref, down_ref = refs[-5:]
    width = in_ref.shape[1]
    total = sums_ref[0].astype(F32)
    for s in range(1, FAR):
        total = total + sums_ref[s].astype(F32)
    in_ref[...] = total[:, :width].astype(BF16)
    pick = jnp.where(iota((TOP, LANES), 0) == iota((TOP, LANES), 1), 1.0, 0.0).astype(BF16)
    prob_ref[...] = dot(pick, total[:, width:].astype(BF16), ((1,), (1,))).astype(BF16)
    share, hidden_width = gate_ref.shape
    down_share = down_ref.shape[0]
    half = width // 2

    def part(low, size):
        result = part_refs[0][low : low + size, :].astype(F32)
        for ref in part_refs[1:]:
            result = result + ref[low : low + size, :].astype(F32)
        return result

    gate_up = part(0, share)
    gate_ref[...] = gate_up[:, :hidden_width]
    up_ref[...] = gate_up[:, hidden_width:]
    down_ref[:, :half] = part(share, down_share)
    down_ref[:, half:] = part(share + down_share, down_share)


def params(mib):
    return pltpu.CompilerParams(vmem_limit_bytes=mib * MIB)


def cost(flops, nbytes):
    return pl.CostEstimate(flops=flops, bytes_accessed=nbytes, transcendentals=0)


def per_device(layer_in, grad_out, expert_ids, gate_probs, gate_weight, up_weight, down_weight):
    block, width = layer_in.shape
    hidden_width = gate_weight.shape[2]
    chips = lax.axis_size("x")
    groups = 2 * chips
    tokens = FAR * block
    slots = NEAR * FAR * CAP
    share = width // groups
    down_share = hidden_width // groups
    part_rows = share + 2 * down_share
    core = lax.axis_index("core").astype(jnp.int32)
    chip = lax.axis_index("x").astype(jnp.int32)
    moved = core * (NEAR // 2)
    place = lax.axis_index(("far", "near", "y")) - moved + EXPERTS
    base = ((place & -NEAR) + moved).astype(jnp.int32).reshape(1)
    scalar = pl.BlockSpec(memory_space=pltpu.SMEM)

    def shape(*dims):
        return jax.ShapeDtypeStruct(dims, BF16)

    packed = pl.pallas_call(
        pack_kernel,
        out_shape=shape(block, 2 * width + LANES),
        in_specs=[pl.BlockSpec(memory_space=pltpu.HBM)] * 3 + whole(1),
        out_specs=whole(1)[0],
        scratch_shapes=[pltpu.VMEM((TOP, block), jnp.int32), pltpu.SemaphoreType.DMA((3,))],
        compiler_params=params(60),
        name="pack_tokens",
    )(layer_in, grad_out, expert_ids.T, gate_probs.T)
    near_tokens = lax.all_gather(packed, "far", tiled=True)

    send, pick = pl.pallas_call(
        select_kernel,
        out_shape=(shape(slots, 2 * width), shape(tokens, slots)),
        in_specs=[scalar] + whole(1),
        out_specs=tuple(whole(2)),
        compiler_params=params(24),
        name="select_rows",
    )(base, near_tokens)

    exchange = functools.partial(lax.all_to_all, split_axis=0, concat_axis=0, tiled=True)
    near_exchange = functools.partial(
        exchange,
        axis_name=("x", "core", "far", "near", "y"),
        axis_index_groups=windows(groups, EXPERTS),
    )
    rows = near_exchange(send.reshape(NEAR, FAR * CAP, 2 * width)).reshape(slots, 2 * width)

    matmul = 2 * slots * width * hidden_width
    back, both, hidden = pl.pallas_call(
        expert_kernel,
        out_shape=(shape(slots, width + LANES), shape(slots, 2 * hidden_width), shape(slots, hidden_width)),
        in_specs=whole(4),
        out_specs=tuple(whole(3)),
        compiler_params=params(32),
        cost_estimate=cost(5 * matmul, 8 * MIB),
        name="expert_rows",
    )(rows, gate_weight[0], up_weight[0], down_weight[0])
    back = near_exchange(back.reshape(NEAR, FAR * CAP, width + LANES)).reshape(slots, width + LANES)

    keep, give = pl.pallas_call(
        part_kernel,
        out_shape=(shape(chips, part_rows, 2 * hidden_width),) * 2,
        in_specs=[scalar] + whole(3),
        out_specs=tuple(whole(2)),
        compiler_params=params(32),
        cost_estimate=cost(3 * matmul, 8 * MIB),
        name="weight_parts",
    )(core.reshape(1), rows, both, hidden)
    got = lax.ppermute(give, "core", [(0, 1), (1, 0)])
    share_shape, half_shape = shape(part_rows, 2 * hidden_width), shape(part_rows // 2, 2 * hidden_width)
    own, right, left, far_low, far_high = pl.pallas_call(
        chip_sum_kernel,
        out_shape=(share_shape,) * 3 + (half_shape,) * 2,
        in_specs=[scalar] + whole(2),
        out_specs=tuple(whole(5)),
        compiler_params=params(16),
        cost_estimate=cost(MIB, 6 * MIB),
        name="chip_sums",
    )(chip.reshape(1), keep, got)
    to_right = [(i, (i + 1) % chips) for i in range(chips)]
    to_left = [(i, (i - 1) % chips) for i in range(chips)]
    right, left = pl.pallas_call(
        relay_kernel,
        out_shape=(share_shape,) * 2,
        in_specs=whole(4),
        out_specs=tuple(whole(2)),
        compiler_params=params(8),
        cost_estimate=cost(MIB, 2 * MIB),
        name="relay_sums",
    )(right, left, lax.ppermute(far_low, "x", to_right), lax.ppermute(far_high, "x", to_left))
    parts = [own, lax.ppermute(right, "x", to_right), lax.ppermute(left, "x", to_left)]

    back, _ = lax.optimization_barrier((back, right))
    sums = pl.pallas_call(
        combine_kernel,
        out_shape=shape(tokens, width + LANES),
        in_specs=[scalar] + whole(3),
        out_specs=whole(1)[0],
        compiler_params=params(24),
        name="combine_rows",
    )(base, back, pick, near_tokens[:, 2 * width :])
    sums = exchange(sums.reshape(FAR, block, width + LANES), "far")

    grad_in, grad_probs, grad_gate, grad_up, grad_down = pl.pallas_call(
        finish_kernel,
        out_shape=(
            shape(block, width),
            shape(TOP, block),
            jax.ShapeDtypeStruct((share, hidden_width), F32),
            jax.ShapeDtypeStruct((share, hidden_width), F32),
            jax.ShapeDtypeStruct((down_share, width), F32),
        ),
        in_specs=whole(1 + len(parts)),
        out_specs=tuple(whole(5)),
        compiler_params=params(24),
        name="finish",
    )(sums, *parts)
    return grad_in, grad_probs.T, grad_gate[None], grad_up[None], grad_down[None]


def solution(mesh):
    groups, experts = mesh.devices.shape
    split = Mesh(
        mesh.devices.reshape(groups // 2, 2, FAR, 4, experts // NEAR), ("x", "core", "far", "near", "y")
    )
    expert = ("far", "near", "y")
    token_spec = P(("x", "core") + expert, None)
    weight_spec = P(expert, None, None)
    grad_spec = P(expert, ("x", "core"), None)
    return jax.shard_map(
        per_device,
        mesh=split,
        in_specs=(token_spec,) * 4 + (weight_spec,) * 3,
        out_specs=(token_spec,) * 2 + (grad_spec,) * 3,
        check_vma=False,
    )
```

```python
import functools

import jax
import jax.numpy as jnp
from jax import lax
from jax.experimental import pallas as pl
from jax.experimental.pallas import tpu as pltpu
from jax.sharding import Mesh, PartitionSpec as P

F32 = jnp.float32
BF16 = jnp.bfloat16
LANES = 128
CAP = 6
FAR = 4
NEAR = 16
TOP = 8
EXPERTS = 64
MIB = 1 << 20


def iota(shape, dim):
    return lax.broadcasted_iota(jnp.int32, shape, dim)


def dot(a, b, contract=((1,), (0,))):
    return lax.dot_general(a, b, (contract, ((), ())), preferred_element_type=F32)


def whole(n):
    return [pl.BlockSpec(memory_space=pltpu.VMEM)] * n


def slot_parts(i):
    sixth = lax.shift_right_logical(i * 10923, 16)
    expert = lax.shift_right_logical(i * 2731, 16)
    return expert, sixth - FAR * expert, i - CAP * sixth


def served(lane, base):
    return jnp.where(lane < NEAR, (lane + base) & (EXPERTS - 1), -1).astype(F32)


def windows(groups, experts):
    lists = []
    for g in range(groups):
        for far in range(FAR):
            start = far * NEAR + (g % 2) * (NEAR // 2)
            lists.append([g * experts + (start + j) % experts for j in range(NEAR)])
    return lists


def pack_kernel(layer_ref, grad_ref, ids_ref, probs_ref, out_ref, ids_vmem, sems):
    width = layer_ref.shape[1]
    copies = [
        pltpu.make_async_copy(ids_ref, ids_vmem, sems.at[0]),
        pltpu.make_async_copy(layer_ref, out_ref.at[:, :width], sems.at[1]),
        pltpu.make_async_copy(grad_ref, out_ref.at[:, width : 2 * width], sems.at[2]),
    ]
    for copy in copies:
        copy.start()
    choice, lane = iota((TOP, LANES), 0), iota((TOP, LANES), 1)
    ids_lane = jnp.where(lane == choice, 1.0, 0.0).astype(BF16)
    probs_lane = jnp.where(lane == choice + TOP, 1.0, 0.0).astype(BF16)
    copies[0].wait()
    ids = ids_vmem[...].astype(F32).astype(BF16)
    extras = dot(ids, ids_lane, ((0,), (0,))) + dot(probs_ref[...], probs_lane, ((0,), (0,)))
    out_ref[:, 2 * width :] = extras.astype(BF16)
    copies[1].wait()
    copies[2].wait()


def select_kernel(base_ref, tok_ref, send_ref, pick_ref):
    tokens = tok_ref.shape[0]
    slots = send_ref.shape[0]
    width = send_ref.shape[1] // 2
    block = tokens // FAR
    extras = tok_ref[:, 2 * width :].astype(F32)
    lane = iota((tokens, LANES), 1)
    expert_lane = served(lane, base_ref[0])
    member = jnp.zeros((tokens, LANES), F32)
    prob = jnp.zeros((tokens, LANES), F32)
    for k in range(TOP):
        hit = extras[:, k : k + 1] == expert_lane
        member = jnp.where(hit, 1.0, member)
        prob = jnp.where(hit, extras[:, TOP + k : TOP + k + 1], prob)
    row, col = iota((tokens, tokens), 0), iota((tokens, tokens), 1)
    shift = block.bit_length() - 1
    same = lax.shift_right_logical(row, shift) == lax.shift_right_logical(col, shift)
    earlier = jnp.where(same & (col < row), 1.0, 0.0).astype(BF16)
    rank = dot(earlier, member.astype(BF16))
    code = jnp.where(member > 0.0, rank, -1.0).astype(BF16)
    eye = jnp.where(row == col, 1.0, 0.0).astype(BF16)
    code_t = dot(code, eye, ((0,), (0,))).astype(BF16)
    prob_t = dot(prob.astype(BF16), eye, ((0,), (0,))).astype(BF16)

    expert, home, place = slot_parts(iota((slots, LANES), 0))
    spread = jnp.where(iota((slots, LANES), 1) == expert, 1.0, 0.0).astype(BF16)
    code_row = dot(spread, code_t)
    token_block = lax.shift_right_logical(iota((slots, tokens), 1), shift)
    chosen = (code_row == place.astype(F32)) & (token_block == home)
    select = jnp.where(chosen, 1.0, 0.0).astype(BF16)
    prob_row = jnp.sum(jnp.where(chosen, dot(spread, prob_t), 0.0), axis=1, keepdims=True)
    send_ref[:, :width] = dot(select, tok_ref[:, :width]).astype(BF16)
    grads = dot(select, tok_ref[:, width : 2 * width])
    send_ref[:, width:] = (prob_row * grads).astype(BF16)

    expert, home, place = slot_parts(iota((LANES, slots), 1))
    spread = jnp.where(iota((LANES, slots), 0) == expert, 1.0, 0.0).astype(BF16)
    code_col = dot(code, spread)
    token_block = lax.shift_right_logical(iota((tokens, slots), 0), shift)
    chosen = (code_col == place.astype(F32)) & (token_block == home)
    pick_ref[...] = jnp.where(chosen, 1.0, 0.0).astype(BF16)


def expert_kernel(rows_ref, gate_ref, up_ref, down_ref, ret_ref, both_ref, hidden_ref):
    width, hidden_width = gate_ref.shape
    scaled = rows_ref[:, width:]
    rows = rows_ref[:, :width]
    gate, up, down = gate_ref[...], up_ref[...], down_ref[...]
    pre_gate = dot(rows, gate)
    pre_up = dot(rows, up)
    grad_hidden = dot(scaled, down, ((1,), (1,)))
    sig = jax.nn.sigmoid(pre_gate)
    silu = pre_gate * sig
    hidden = (silu * pre_up).astype(BF16)
    prob_grad = jnp.sum(hidden.astype(F32) * grad_hidden, axis=1, keepdims=True)
    gate_grad = (grad_hidden * pre_up * sig * (1.0 + pre_gate * (1.0 - sig))).astype(BF16)
    up_grad = (grad_hidden * silu).astype(BF16)
    back = dot(gate_grad, gate, ((1,), (1,))) + dot(up_grad, up, ((1,), (1,)))
    ret_ref[:, :width] = back.astype(BF16)
    ret_ref[:, width:] = jnp.broadcast_to(prob_grad, (rows.shape[0], LANES)).astype(BF16)
    both_ref[:, :hidden_width] = gate_grad
    both_ref[:, hidden_width:] = up_grad
    hidden_ref[...] = hidden


def part_kernel(core_ref, rows_hbm, both_ref, hidden_ref, keep_hbm, give_hbm, rows, keep, give, in_sems, out_sems):
    chips, part_rows, columns = keep.shape
    hidden_width = hidden_ref.shape[1]
    width = rows.shape[1] // 2
    share = width // (2 * chips)
    down_share = hidden_width // (2 * chips)
    half = width // 2
    first = core_ref[0] == 0

    spans = [(width + side * half, half) for side in range(2)]
    spans += [(chip * 2 * share, 2 * share) for chip in range(chips)]
    loads = [
        pltpu.make_async_copy(rows_hbm.at[:, pl.ds(*span)], rows.at[:, pl.ds(*span)], in_sems.at[i])
        for i, span in enumerate(spans)
    ]
    for load in loads:
        load.start()

    def put(chip, low, pair):
        size = pair.shape[0] // 2
        keep[chip, low : low + size, :] = jnp.where(first, pair[:size], pair[size:]).astype(BF16)
        give[chip, low : low + size, :] = jnp.where(first, pair[size:], pair[:size]).astype(BF16)

    hidden = hidden_ref[...]
    for side in range(2):
        loads[side].wait()
        part = dot(hidden, rows[:, width + side * half : width + (side + 1) * half], ((0,), (0,)))
        for chip in range(chips):
            put(chip, share + side * down_share, part[chip * 2 * down_share : (chip + 1) * 2 * down_share])
    both = both_ref[...]
    stores = []
    for chip in range(chips):
        loads[2 + chip].wait()
        put(chip, 0, dot(rows[:, chip * 2 * share : (chip + 1) * 2 * share], both, ((0,), (0,))))
        stores.append(pltpu.make_async_copy(give.at[chip], give_hbm.at[chip], out_sems.at[2 * chip]))
        stores.append(pltpu.make_async_copy(keep.at[chip], keep_hbm.at[chip], out_sems.at[2 * chip + 1]))
        stores[-2].start()
        stores[-1].start()
    for store in stores:
        store.wait()


def chip_sum_kernel(
    chip_ref, keep_hbm, got_hbm, own_ref, right_ref, left_ref, far_low_ref, far_high_ref, keep, got, sems
):
    chips, part_rows, _ = keep.shape
    half = part_rows // 2
    loads = []
    for s in (2, 1, 3, 0):
        chip = (chip_ref[0] + s) & (chips - 1)
        loads.append(pltpu.make_async_copy(keep_hbm.at[chip], keep.at[s], sems.at[2 * s]))
        loads.append(pltpu.make_async_copy(got_hbm.at[chip], got.at[s], sems.at[2 * s + 1]))
    for load in loads:
        load.start()

    def total(s, low, size):
        rows = pl.ds(low, size)
        return (keep[s, rows].astype(F32) + got[s, rows].astype(F32)).astype(BF16)

    loads[0].wait()
    loads[1].wait()
    far_low_ref[...] = total(2, 0, half)
    far_high_ref[...] = total(2, half, half)
    for i, (s, ref) in enumerate(((1, right_ref), (3, left_ref), (0, own_ref))):
        loads[2 * i + 2].wait()
        loads[2 * i + 3].wait()
        ref[...] = total(s, 0, part_rows)


def relay_kernel(right_ref, left_ref, low_ref, high_ref, to_right_ref, to_left_ref):
    half = low_ref.shape[0]
    to_right_ref[:half] = (right_ref[:half].astype(F32) + low_ref[...].astype(F32)).astype(BF16)
    to_right_ref[half:] = right_ref[half:]
    to_left_ref[:half] = left_ref[:half]
    to_left_ref[half:] = (left_ref[half:].astype(F32) + high_ref[...].astype(F32)).astype(BF16)


def combine_kernel(base_ref, back_ref, pick_ref, extra_ref, sum_ref):
    slots = back_ref.shape[0]
    width = back_ref.shape[1] - LANES
    tokens = sum_ref.shape[0]
    pick = pick_ref[...]
    sum_ref[:, :width] = dot(pick, back_ref[:, :width]).astype(BF16)
    expert, _, _ = slot_parts(iota((slots, LANES), 0))
    own = iota((slots, LANES), 1) == expert
    spread = jnp.where(own, back_ref[:, width:].astype(F32), 0.0).astype(BF16)
    by_expert = dot(pick, spread)
    extras = extra_ref[...].astype(F32)
    lane = iota((tokens, LANES), 1)
    expert_lane = served(lane, base_ref[0])
    result = jnp.zeros((tokens, LANES), F32)
    for k in range(TOP):
        hit = extras[:, k : k + 1] == expert_lane
        value = jnp.sum(jnp.where(hit, by_expert, 0.0), axis=1, keepdims=True)
        value = value / extras[:, TOP + k : TOP + k + 1]
        result = jnp.where(lane == k, value, result)
    sum_ref[:, width:] = result.astype(BF16)


def finish_kernel(*refs):
    sums_ref, part_refs = refs[0], refs[1:-5]
    in_ref, prob_ref, gate_ref, up_ref, down_ref = refs[-5:]
    width = in_ref.shape[1]
    total = sums_ref[0].astype(F32)
    for s in range(1, FAR):
        total = total + sums_ref[s].astype(F32)
    in_ref[...] = total[:, :width].astype(BF16)
    pick = jnp.where(iota((TOP, LANES), 0) == iota((TOP, LANES), 1), 1.0, 0.0).astype(BF16)
    prob_ref[...] = dot(pick, total[:, width:].astype(BF16), ((1,), (1,))).astype(BF16)
    share, hidden_width = gate_ref.shape
    down_share = down_ref.shape[0]
    half = width // 2

    def part(low, size):
        result = part_refs[0][low : low + size, :].astype(F32)
        for ref in part_refs[1:]:
            result = result + ref[low : low + size, :].astype(F32)
        return result

    gate_up = part(0, share)
    gate_ref[...] = gate_up[:, :hidden_width]
    up_ref[...] = gate_up[:, hidden_width:]
    down_ref[:, :half] = part(share, down_share)
    down_ref[:, half:] = part(share + down_share, down_share)


def params(mib):
    return pltpu.CompilerParams(vmem_limit_bytes=mib * MIB)


def cost(flops, nbytes):
    return pl.CostEstimate(flops=flops, bytes_accessed=nbytes, transcendentals=0)


def per_device(layer_in, grad_out, expert_ids, gate_probs, gate_weight, up_weight, down_weight):
    block, width = layer_in.shape
    hidden_width = gate_weight.shape[2]
    chips = lax.axis_size("x")
    groups = 2 * chips
    tokens = FAR * block
    slots = NEAR * FAR * CAP
    share = width // groups
    down_share = hidden_width // groups
    part_rows = share + 2 * down_share
    core = lax.axis_index("core").astype(jnp.int32)
    chip = lax.axis_index("x").astype(jnp.int32)
    moved = core * (NEAR // 2)
    place = lax.axis_index(("far", "near", "y")) - moved + EXPERTS
    base = ((place & -NEAR) + moved).astype(jnp.int32).reshape(1)
    scalar = pl.BlockSpec(memory_space=pltpu.SMEM)
    hbm = pl.BlockSpec(memory_space=pltpu.HBM)

    def shape(*dims):
        return jax.ShapeDtypeStruct(dims, BF16)

    packed = pl.pallas_call(
        pack_kernel,
        out_shape=shape(block, 2 * width + LANES),
        in_specs=[hbm] * 3 + whole(1),
        out_specs=whole(1)[0],
        scratch_shapes=[pltpu.VMEM((TOP, block), jnp.int32), pltpu.SemaphoreType.DMA((3,))],
        compiler_params=params(60),
        name="pack_tokens",
    )(layer_in, grad_out, expert_ids.T, gate_probs.T)
    near_tokens = lax.all_gather(packed, "far", tiled=True)

    send, pick = pl.pallas_call(
        select_kernel,
        out_shape=(shape(slots, 2 * width), shape(tokens, slots)),
        in_specs=[scalar] + whole(1),
        out_specs=tuple(whole(2)),
        compiler_params=params(24),
        name="select_rows",
    )(base, near_tokens)

    exchange = functools.partial(lax.all_to_all, split_axis=0, concat_axis=0, tiled=True)
    near_exchange = functools.partial(
        exchange,
        axis_name=("x", "core", "far", "near", "y"),
        axis_index_groups=windows(groups, EXPERTS),
    )
    rows = near_exchange(send.reshape(NEAR, FAR * CAP, 2 * width)).reshape(slots, 2 * width)

    matmul = 2 * slots * width * hidden_width
    back, both, hidden = pl.pallas_call(
        expert_kernel,
        out_shape=(shape(slots, width + LANES), shape(slots, 2 * hidden_width), shape(slots, hidden_width)),
        in_specs=whole(4),
        out_specs=tuple(whole(3)),
        compiler_params=params(32),
        cost_estimate=cost(5 * matmul, 8 * MIB),
        name="expert_rows",
    )(rows, gate_weight[0], up_weight[0], down_weight[0])
    back = near_exchange(back.reshape(NEAR, FAR * CAP, width + LANES)).reshape(slots, width + LANES)

    keep, give = pl.pallas_call(
        part_kernel,
        out_shape=(shape(chips, part_rows, 2 * hidden_width),) * 2,
        in_specs=[scalar, hbm] + whole(2),
        out_specs=(hbm, hbm),
        scratch_shapes=[
            pltpu.VMEM((slots, 2 * width), BF16),
            pltpu.VMEM((chips, part_rows, 2 * hidden_width), BF16),
            pltpu.VMEM((chips, part_rows, 2 * hidden_width), BF16),
            pltpu.SemaphoreType.DMA((chips + 2,)),
            pltpu.SemaphoreType.DMA((2 * chips,)),
        ],
        compiler_params=params(52),
        cost_estimate=cost(3 * matmul, 8 * MIB),
        name="weight_parts",
    )(core.reshape(1), rows, both, hidden)
    got = lax.ppermute(give, "core", [(0, 1), (1, 0)])
    share_shape, half_shape = shape(part_rows, 2 * hidden_width), shape(part_rows // 2, 2 * hidden_width)
    own, right, left, far_low, far_high = pl.pallas_call(
        chip_sum_kernel,
        out_shape=(share_shape,) * 3 + (half_shape,) * 2,
        in_specs=[scalar, hbm, hbm],
        out_specs=tuple(whole(5)),
        scratch_shapes=[
            pltpu.VMEM((chips, part_rows, 2 * hidden_width), BF16),
            pltpu.VMEM((chips, part_rows, 2 * hidden_width), BF16),
            pltpu.SemaphoreType.DMA((2 * chips,)),
        ],
        compiler_params=params(52),
        cost_estimate=cost(MIB, 6 * MIB),
        name="chip_sums",
    )(chip.reshape(1), keep, got)
    to_right = [(i, (i + 1) % chips) for i in range(chips)]
    to_left = [(i, (i - 1) % chips) for i in range(chips)]
    right, left = pl.pallas_call(
        relay_kernel,
        out_shape=(share_shape,) * 2,
        in_specs=whole(4),
        out_specs=tuple(whole(2)),
        compiler_params=params(8),
        cost_estimate=cost(MIB, 2 * MIB),
        name="relay_sums",
    )(right, left, lax.ppermute(far_low, "x", to_right), lax.ppermute(far_high, "x", to_left))
    parts = [own, lax.ppermute(right, "x", to_right), lax.ppermute(left, "x", to_left)]

    back, _ = lax.optimization_barrier((back, right))
    sums = pl.pallas_call(
        combine_kernel,
        out_shape=shape(tokens, width + LANES),
        in_specs=[scalar] + whole(3),
        out_specs=whole(1)[0],
        compiler_params=params(24),
        name="combine_rows",
    )(base, back, pick, near_tokens[:, 2 * width :])
    sums = exchange(sums.reshape(FAR, block, width + LANES), "far")

    grad_in, grad_probs, grad_gate, grad_up, grad_down = pl.pallas_call(
        finish_kernel,
        out_shape=(
            shape(block, width),
            shape(TOP, block),
            jax.ShapeDtypeStruct((share, hidden_width), F32),
            jax.ShapeDtypeStruct((share, hidden_width), F32),
            jax.ShapeDtypeStruct((down_share, width), F32),
        ),
        in_specs=whole(1 + len(parts)),
        out_specs=tuple(whole(5)),
        compiler_params=params(24),
        name="finish",
    )(sums, *parts)
    return grad_in, grad_probs.T, grad_gate[None], grad_up[None], grad_down[None]


def solution(mesh):
    groups, experts = mesh.devices.shape
    split = Mesh(
        mesh.devices.reshape(groups // 2, 2, FAR, 4, experts // NEAR), ("x", "core", "far", "near", "y")
    )
    expert = ("far", "near", "y")
    token_spec = P(("x", "core") + expert, None)
    weight_spec = P(expert, None, None)
    grad_spec = P(expert, ("x", "core"), None)
    return jax.shard_map(
        per_device,
        mesh=split,
        in_specs=(token_spec,) * 4 + (weight_spec,) * 3,
        out_specs=(token_spec,) * 2 + (grad_spec,) * 3,
        check_vma=False,
    )
```

```python
import functools

import jax
import jax.numpy as jnp
from jax import lax
from jax.experimental import pallas as pl
from jax.experimental.pallas import tpu as pltpu
from jax.sharding import Mesh, PartitionSpec as P

F32 = jnp.float32
BF16 = jnp.bfloat16
LANES = 128
CAP = 6
FAR = 4
NEAR = 16
TOP = 8
EXPERTS = 64
MIB = 1 << 20


def iota(shape, dim):
    return lax.broadcasted_iota(jnp.int32, shape, dim)


def dot(a, b, contract=((1,), (0,))):
    return lax.dot_general(a, b, (contract, ((), ())), preferred_element_type=F32)


def whole(n):
    return [pl.BlockSpec(memory_space=pltpu.VMEM)] * n


def slot_parts(i):
    sixth = lax.shift_right_logical(i * 10923, 16)
    expert = lax.shift_right_logical(i * 2731, 16)
    return expert, sixth - FAR * expert, i - CAP * sixth


def served(lane, base):
    return jnp.where(lane < NEAR, (lane + base) & (EXPERTS - 1), -1).astype(F32)


def windows(groups, experts):
    lists = []
    for g in range(groups):
        for far in range(FAR):
            start = far * NEAR + (g % 2) * (NEAR // 2)
            lists.append([g * experts + (start + j) % experts for j in range(NEAR)])
    return lists


def pack_kernel(layer_ref, grad_ref, ids_ref, probs_ref, out_ref, ids_vmem, sems):
    width = layer_ref.shape[1]
    copies = [
        pltpu.make_async_copy(ids_ref, ids_vmem, sems.at[0]),
        pltpu.make_async_copy(layer_ref, out_ref.at[:, :width], sems.at[1]),
        pltpu.make_async_copy(grad_ref, out_ref.at[:, width : 2 * width], sems.at[2]),
    ]
    for copy in copies:
        copy.start()
    choice, lane = iota((TOP, LANES), 0), iota((TOP, LANES), 1)
    ids_lane = jnp.where(lane == choice, 1.0, 0.0).astype(BF16)
    probs_lane = jnp.where(lane == choice + TOP, 1.0, 0.0).astype(BF16)
    copies[0].wait()
    ids = ids_vmem[...].astype(F32).astype(BF16)
    extras = dot(ids, ids_lane, ((0,), (0,))) + dot(probs_ref[...], probs_lane, ((0,), (0,)))
    out_ref[:, 2 * width :] = extras.astype(BF16)
    copies[1].wait()
    copies[2].wait()


def select_kernel(base_ref, tok_ref, send_ref, pick_ref):
    tokens = tok_ref.shape[0]
    slots = send_ref.shape[0]
    width = send_ref.shape[1] // 2
    block = tokens // FAR
    extras = tok_ref[:, 2 * width :].astype(F32)
    lane = iota((tokens, LANES), 1)
    expert_lane = served(lane, base_ref[0])
    member = jnp.zeros((tokens, LANES), F32)
    prob = jnp.zeros((tokens, LANES), F32)
    for k in range(TOP):
        hit = extras[:, k : k + 1] == expert_lane
        member = jnp.where(hit, 1.0, member)
        prob = jnp.where(hit, extras[:, TOP + k : TOP + k + 1], prob)
    row, col = iota((tokens, tokens), 0), iota((tokens, tokens), 1)
    shift = block.bit_length() - 1
    same = lax.shift_right_logical(row, shift) == lax.shift_right_logical(col, shift)
    earlier = jnp.where(same & (col < row), 1.0, 0.0).astype(BF16)
    rank = dot(earlier, member.astype(BF16))
    code = jnp.where(member > 0.0, rank, -1.0).astype(BF16)
    eye = jnp.where(row == col, 1.0, 0.0).astype(BF16)
    code_t = dot(code, eye, ((0,), (0,))).astype(BF16)
    prob_t = dot(prob.astype(BF16), eye, ((0,), (0,))).astype(BF16)

    expert, home, place = slot_parts(iota((slots, LANES), 0))
    spread = jnp.where(iota((slots, LANES), 1) == expert, 1.0, 0.0).astype(BF16)
    code_row = dot(spread, code_t)
    token_block = lax.shift_right_logical(iota((slots, tokens), 1), shift)
    chosen = (code_row == place.astype(F32)) & (token_block == home)
    select = jnp.where(chosen, 1.0, 0.0).astype(BF16)
    prob_row = jnp.sum(jnp.where(chosen, dot(spread, prob_t), 0.0), axis=1, keepdims=True)
    send_ref[:, :width] = dot(select, tok_ref[:, :width]).astype(BF16)
    grads = dot(select, tok_ref[:, width : 2 * width])
    send_ref[:, width:] = (prob_row * grads).astype(BF16)

    expert, home, place = slot_parts(iota((LANES, slots), 1))
    spread = jnp.where(iota((LANES, slots), 0) == expert, 1.0, 0.0).astype(BF16)
    code_col = dot(code, spread)
    token_block = lax.shift_right_logical(iota((tokens, slots), 0), shift)
    chosen = (code_col == place.astype(F32)) & (token_block == home)
    pick_ref[...] = jnp.where(chosen, 1.0, 0.0).astype(BF16)


def expert_kernel(rows_ref, gate_ref, up_ref, down_ref, ret_ref, both_ref, hidden_ref):
    width, hidden_width = gate_ref.shape
    scaled = rows_ref[:, width:]
    rows = rows_ref[:, :width]
    gate, up, down = gate_ref[...], up_ref[...], down_ref[...]
    pre_gate = dot(rows, gate)
    pre_up = dot(rows, up)
    grad_hidden = dot(scaled, down, ((1,), (1,)))
    sig = jax.nn.sigmoid(pre_gate)
    silu = pre_gate * sig
    hidden = (silu * pre_up).astype(BF16)
    prob_grad = jnp.sum(hidden.astype(F32) * grad_hidden, axis=1, keepdims=True)
    gate_grad = (grad_hidden * pre_up * sig * (1.0 + pre_gate * (1.0 - sig))).astype(BF16)
    up_grad = (grad_hidden * silu).astype(BF16)
    back = dot(gate_grad, gate, ((1,), (1,))) + dot(up_grad, up, ((1,), (1,)))
    ret_ref[:, :width] = back.astype(BF16)
    ret_ref[:, width:] = jnp.broadcast_to(prob_grad, (rows.shape[0], LANES)).astype(BF16)
    both_ref[:, :hidden_width] = gate_grad
    both_ref[:, hidden_width:] = up_grad
    hidden_ref[...] = hidden


def part_kernel(core_ref, rows_hbm, both_ref, hidden_ref, keep_hbm, give_hbm, rows, keep, give, in_sems, out_sems):
    chips, part_rows, columns = keep.shape
    hidden_width = hidden_ref.shape[1]
    width = rows.shape[1] // 2
    share = width // (2 * chips)
    down_share = hidden_width // (2 * chips)
    half = width // 2
    first = core_ref[0] == 0

    spans = [(width + side * half, half) for side in range(2)]
    spans += [(chip * 2 * share, 2 * share) for chip in range(chips)]
    loads = [
        pltpu.make_async_copy(rows_hbm.at[:, pl.ds(*span)], rows.at[:, pl.ds(*span)], in_sems.at[i])
        for i, span in enumerate(spans)
    ]
    for load in loads:
        load.start()

    def put(chip, low, pair):
        size = pair.shape[0] // 2
        keep[chip, low : low + size, :] = jnp.where(first, pair[:size], pair[size:]).astype(BF16)
        give[chip, low : low + size, :] = jnp.where(first, pair[size:], pair[:size]).astype(BF16)

    hidden = hidden_ref[...]
    for side in range(2):
        loads[side].wait()
        part = dot(hidden, rows[:, width + side * half : width + (side + 1) * half], ((0,), (0,)))
        for chip in range(chips):
            put(chip, share + side * down_share, part[chip * 2 * down_share : (chip + 1) * 2 * down_share])
    both = both_ref[...]
    stores = []
    for chip in range(chips):
        loads[2 + chip].wait()
        put(chip, 0, dot(rows[:, chip * 2 * share : (chip + 1) * 2 * share], both, ((0,), (0,))))
        stores.append(pltpu.make_async_copy(give.at[chip], give_hbm.at[chip], out_sems.at[2 * chip]))
        stores.append(pltpu.make_async_copy(keep.at[chip], keep_hbm.at[chip], out_sems.at[2 * chip + 1]))
        stores[-2].start()
        stores[-1].start()
    for store in stores:
        store.wait()


def chip_sum_kernel(chip_ref, keep_hbm, got_hbm, *refs):
    out_refs, (keep, got, sems) = refs[:-3], refs[-3:]
    chips = keep.shape[0]
    order = (2, 1, 3, 0)
    loads = []
    for s in order:
        chip = (chip_ref[0] + s) & (chips - 1)
        loads.append(pltpu.make_async_copy(keep_hbm.at[chip], keep.at[s], sems.at[2 * s]))
        loads.append(pltpu.make_async_copy(got_hbm.at[chip], got.at[s], sems.at[2 * s + 1]))
    for load in loads:
        load.start()
    for i, s in enumerate(order):
        loads[2 * i].wait()
        loads[2 * i + 1].wait()
        out_refs[s][...] = (keep[s].astype(F32) + got[s].astype(F32)).astype(BF16)


def combine_kernel(base_ref, far_ref, back_ref, pick_ref, extra_ref, *refs):
    out_refs, sum_ref = refs[:-1], refs[-1]
    slots = back_ref.shape[0]
    width = back_ref.shape[1] - LANES
    tokens = pick_ref.shape[0]
    block = tokens // FAR
    pick = pick_ref[...]
    sum_ref[:, :, :width] = dot(pick, back_ref[:, :width]).astype(BF16).reshape(FAR, block, width)
    expert, _, _ = slot_parts(iota((slots, LANES), 0))
    own = iota((slots, LANES), 1) == expert
    spread = jnp.where(own, back_ref[:, width:].astype(F32), 0.0).astype(BF16)
    by_expert = dot(pick, spread)
    extras = extra_ref[...].astype(F32)
    lane = iota((tokens, LANES), 1)
    expert_lane = served(lane, base_ref[0])
    result = jnp.zeros((tokens, LANES), F32)
    for k in range(TOP):
        hit = extras[:, k : k + 1] == expert_lane
        value = jnp.sum(jnp.where(hit, by_expert, 0.0), axis=1, keepdims=True)
        value = value / extras[:, TOP + k : TOP + k + 1]
        result = jnp.where(lane == k, value, result)
    sum_ref[:, :, width:] = result.astype(BF16).reshape(FAR, block, LANES)
    for s, out_ref in enumerate(out_refs):
        out_ref[...] = sum_ref[(far_ref[0] + s) & (FAR - 1)]


def finish_kernel(*refs):
    sum_refs, part_refs = refs[:FAR], refs[FAR:-5]
    in_ref, prob_ref, gate_ref, up_ref, down_ref = refs[-5:]
    width = in_ref.shape[1]
    total = sum_refs[0][...].astype(F32)
    for ref in sum_refs[1:]:
        total = total + ref[...].astype(F32)
    in_ref[...] = total[:, :width].astype(BF16)
    pick = jnp.where(iota((TOP, LANES), 0) == iota((TOP, LANES), 1), 1.0, 0.0).astype(BF16)
    prob_ref[...] = dot(pick, total[:, width:].astype(BF16), ((1,), (1,))).astype(BF16)
    share, hidden_width = gate_ref.shape
    down_share = down_ref.shape[0]
    half = width // 2

    def part(low, size):
        result = part_refs[0][low : low + size, :].astype(F32)
        for ref in part_refs[1:]:
            result = result + ref[low : low + size, :].astype(F32)
        return result

    gate_up = part(0, share)
    gate_ref[...] = gate_up[:, :hidden_width]
    up_ref[...] = gate_up[:, hidden_width:]
    down_ref[:, :half] = part(share, down_share)
    down_ref[:, half:] = part(share + down_share, down_share)


def params(mib):
    return pltpu.CompilerParams(vmem_limit_bytes=mib * MIB)


def cost(flops, nbytes):
    return pl.CostEstimate(flops=flops, bytes_accessed=nbytes, transcendentals=0)


def per_device(layer_in, grad_out, expert_ids, gate_probs, gate_weight, up_weight, down_weight):
    block, width = layer_in.shape
    hidden_width = gate_weight.shape[2]
    chips = lax.axis_size("x")
    groups = 2 * chips
    tokens = FAR * block
    slots = NEAR * FAR * CAP
    share = width // groups
    down_share = hidden_width // groups
    part_rows = share + 2 * down_share
    core = lax.axis_index("core").astype(jnp.int32)
    chip = lax.axis_index("x").astype(jnp.int32)
    far = lax.axis_index("far").astype(jnp.int32)
    moved = core * (NEAR // 2)
    place = lax.axis_index(("far", "near", "y")) - moved + EXPERTS
    base = ((place & -NEAR) + moved).astype(jnp.int32).reshape(1)
    scalar = pl.BlockSpec(memory_space=pltpu.SMEM)
    hbm = pl.BlockSpec(memory_space=pltpu.HBM)

    def shape(*dims):
        return jax.ShapeDtypeStruct(dims, BF16)

    packed = pl.pallas_call(
        pack_kernel,
        out_shape=shape(block, 2 * width + LANES),
        in_specs=[hbm] * 3 + whole(1),
        out_specs=whole(1)[0],
        scratch_shapes=[pltpu.VMEM((TOP, block), jnp.int32), pltpu.SemaphoreType.DMA((3,))],
        compiler_params=params(60),
        name="pack_tokens",
    )(layer_in, grad_out, expert_ids.T, gate_probs.T)
    near_tokens = lax.all_gather(packed, "far", tiled=True)

    send, pick = pl.pallas_call(
        select_kernel,
        out_shape=(shape(slots, 2 * width), shape(tokens, slots)),
        in_specs=[scalar] + whole(1),
        out_specs=tuple(whole(2)),
        compiler_params=params(24),
        name="select_rows",
    )(base, near_tokens)

    exchange = functools.partial(lax.all_to_all, split_axis=0, concat_axis=0, tiled=True)
    near_exchange = functools.partial(
        exchange,
        axis_name=("x", "core", "far", "near", "y"),
        axis_index_groups=windows(groups, EXPERTS),
    )
    rows = near_exchange(send.reshape(NEAR, FAR * CAP, 2 * width)).reshape(slots, 2 * width)

    matmul = 2 * slots * width * hidden_width
    back, both, hidden = pl.pallas_call(
        expert_kernel,
        out_shape=(shape(slots, width + LANES), shape(slots, 2 * hidden_width), shape(slots, hidden_width)),
        in_specs=whole(4),
        out_specs=tuple(whole(3)),
        compiler_params=params(32),
        cost_estimate=cost(5 * matmul, 8 * MIB),
        name="expert_rows",
    )(rows, gate_weight[0], up_weight[0], down_weight[0])
    back = near_exchange(back.reshape(NEAR, FAR * CAP, width + LANES)).reshape(slots, width + LANES)

    keep, give = pl.pallas_call(
        part_kernel,
        out_shape=(shape(chips, part_rows, 2 * hidden_width),) * 2,
        in_specs=[scalar, hbm] + whole(2),
        out_specs=(hbm, hbm),
        scratch_shapes=[
            pltpu.VMEM((slots, 2 * width), BF16),
            pltpu.VMEM((chips, part_rows, 2 * hidden_width), BF16),
            pltpu.VMEM((chips, part_rows, 2 * hidden_width), BF16),
            pltpu.SemaphoreType.DMA((chips + 2,)),
            pltpu.SemaphoreType.DMA((2 * chips,)),
        ],
        compiler_params=params(52),
        cost_estimate=cost(3 * matmul, 8 * MIB),
        name="weight_parts",
    )(core.reshape(1), rows, both, hidden)
    got = lax.ppermute(give, "core", [(0, 1), (1, 0)])
    chip_sums = pl.pallas_call(
        chip_sum_kernel,
        out_shape=(shape(part_rows, 2 * hidden_width),) * chips,
        in_specs=[scalar, hbm, hbm],
        out_specs=tuple(whole(chips)),
        scratch_shapes=[
            pltpu.VMEM((chips, part_rows, 2 * hidden_width), BF16),
            pltpu.VMEM((chips, part_rows, 2 * hidden_width), BF16),
            pltpu.SemaphoreType.DMA((2 * chips,)),
        ],
        compiler_params=params(52),
        cost_estimate=cost(MIB, 6 * MIB),
        name="chip_sums",
    )(chip.reshape(1), keep, got)
    parts = [
        lax.ppermute(chip_sums[s], "x", [(i, (i + s) % chips) for i in range(chips)]) for s in range(1, chips)
    ] + [chip_sums[0]]

    back, _ = lax.optimization_barrier((back, chip_sums[0]))
    sums = pl.pallas_call(
        combine_kernel,
        out_shape=(shape(block, width + LANES),) * FAR,
        in_specs=[scalar] * 2 + whole(3),
        out_specs=tuple(whole(FAR)),
        scratch_shapes=[pltpu.VMEM((FAR, block, width + LANES), BF16)],
        compiler_params=params(24),
        name="combine_rows",
    )(base, far.reshape(1), back, pick, near_tokens[:, 2 * width :])
    sums = [sums[0]] + [
        lax.ppermute(sums[s], "far", [(i, (i + s) % FAR) for i in range(FAR)]) for s in range(1, FAR)
    ]

    grad_in, grad_probs, grad_gate, grad_up, grad_down = pl.pallas_call(
        finish_kernel,
        out_shape=(
            shape(block, width),
            shape(TOP, block),
            jax.ShapeDtypeStruct((share, hidden_width), F32),
            jax.ShapeDtypeStruct((share, hidden_width), F32),
            jax.ShapeDtypeStruct((down_share, width), F32),
        ),
        in_specs=whole(FAR + len(parts)),
        out_specs=tuple(whole(5)),
        compiler_params=params(24),
        name="finish",
    )(*sums, *parts)
    return grad_in, grad_probs.T, grad_gate[None], grad_up[None], grad_down[None]


def solution(mesh):
    groups, experts = mesh.devices.shape
    split = Mesh(
        mesh.devices.reshape(groups // 2, 2, FAR, 4, experts // NEAR), ("x", "core", "far", "near", "y")
    )
    expert = ("far", "near", "y")
    token_spec = P(("x", "core") + expert, None)
    weight_spec = P(expert, None, None)
    grad_spec = P(expert, ("x", "core"), None)
    return jax.shard_map(
        per_device,
        mesh=split,
        in_specs=(token_spec,) * 4 + (weight_spec,) * 3,
        out_specs=(token_spec,) * 2 + (grad_spec,) * 3,
        check_vma=False,
    )
```

```python
import functools

import jax
import jax.numpy as jnp
from jax import lax
from jax.experimental import pallas as pl
from jax.experimental.pallas import tpu as pltpu
from jax.sharding import Mesh, PartitionSpec as P

F32 = jnp.float32
BF16 = jnp.bfloat16
LANES = 128
CAP = 6
FAR = 4
NEAR = 16
TOP = 8
EXPERTS = 64
MIB = 1 << 20


def iota(shape, dim):
    return lax.broadcasted_iota(jnp.int32, shape, dim)


def dot(a, b, contract=((1,), (0,))):
    return lax.dot_general(a, b, (contract, ((), ())), preferred_element_type=F32)


def whole(n):
    return [pl.BlockSpec(memory_space=pltpu.VMEM)] * n


def slot_parts(i):
    sixth = lax.shift_right_logical(i * 10923, 16)
    expert = lax.shift_right_logical(i * 2731, 16)
    return expert, sixth - FAR * expert, i - CAP * sixth


def served(lane, base):
    return jnp.where(lane < NEAR, (lane + base) & (EXPERTS - 1), -1).astype(F32)


def windows(groups, experts):
    lists = []
    for g in range(groups):
        for far in range(FAR):
            start = far * NEAR + (g % 2) * (NEAR // 2)
            lists.append([g * experts + (start + j) % experts for j in range(NEAR)])
    return lists


def pack_kernel(layer_hbm, grad_hbm, ids_ref, probs_ref, out_hbm, extras, sems):
    width = layer_hbm.shape[1]
    copies = [
        pltpu.make_async_copy(layer_hbm, out_hbm.at[:, :width], sems.at[0]),
        pltpu.make_async_copy(grad_hbm, out_hbm.at[:, width : 2 * width], sems.at[1]),
        pltpu.make_async_copy(extras, out_hbm.at[:, 2 * width :], sems.at[2]),
    ]
    copies[0].start()
    copies[1].start()
    choice, lane = iota((TOP, LANES), 0), iota((TOP, LANES), 1)
    ids_lane = jnp.where(lane == choice, 1.0, 0.0).astype(BF16)
    probs_lane = jnp.where(lane == choice + TOP, 1.0, 0.0).astype(BF16)
    ids = ids_ref[...].astype(F32).astype(BF16)
    both = dot(ids, ids_lane, ((0,), (0,))) + dot(probs_ref[...], probs_lane, ((0,), (0,)))
    extras[...] = both.astype(BF16)
    copies[2].start()
    for copy in copies:
        copy.wait()


def select_kernel(base_ref, tok_ref, send_ref, pick_ref):
    tokens = tok_ref.shape[0]
    slots = send_ref.shape[0]
    width = send_ref.shape[1] // 2
    block = tokens // FAR
    extras = tok_ref[:, 2 * width :].astype(F32)
    lane = iota((tokens, LANES), 1)
    expert_lane = served(lane, base_ref[0])
    member = jnp.zeros((tokens, LANES), F32)
    prob = jnp.zeros((tokens, LANES), F32)
    for k in range(TOP):
        hit = extras[:, k : k + 1] == expert_lane
        member = jnp.where(hit, 1.0, member)
        prob = jnp.where(hit, extras[:, TOP + k : TOP + k + 1], prob)
    row, col = iota((tokens, tokens), 0), iota((tokens, tokens), 1)
    shift = block.bit_length() - 1
    same = lax.shift_right_logical(row, shift) == lax.shift_right_logical(col, shift)
    earlier = jnp.where(same & (col < row), 1.0, 0.0).astype(BF16)
    rank = dot(earlier, member.astype(BF16))
    code = jnp.where(member > 0.0, rank, -1.0).astype(BF16)
    eye = jnp.where(row == col, 1.0, 0.0).astype(BF16)
    code_t = dot(code, eye, ((0,), (0,))).astype(BF16)
    prob_t = dot(prob.astype(BF16), eye, ((0,), (0,))).astype(BF16)

    expert, home, place = slot_parts(iota((slots, LANES), 0))
    spread = jnp.where(iota((slots, LANES), 1) == expert, 1.0, 0.0).astype(BF16)
    code_row = dot(spread, code_t)
    token_block = lax.shift_right_logical(iota((slots, tokens), 1), shift)
    chosen = (code_row == place.astype(F32)) & (token_block == home)
    select = jnp.where(chosen, 1.0, 0.0).astype(BF16)
    prob_row = jnp.sum(jnp.where(chosen, dot(spread, prob_t), 0.0), axis=1, keepdims=True)
    send_ref[:, :width] = dot(select, tok_ref[:, :width]).astype(BF16)
    grads = dot(select, tok_ref[:, width : 2 * width])
    send_ref[:, width:] = (prob_row * grads).astype(BF16)

    expert, home, place = slot_parts(iota((LANES, slots), 1))
    spread = jnp.where(iota((LANES, slots), 0) == expert, 1.0, 0.0).astype(BF16)
    code_col = dot(code, spread)
    token_block = lax.shift_right_logical(iota((tokens, slots), 0), shift)
    chosen = (code_col == place.astype(F32)) & (token_block == home)
    pick_ref[...] = jnp.where(chosen, 1.0, 0.0).astype(BF16)


def expert_kernel(rows_ref, gate_ref, up_ref, down_ref, ret_ref, both_ref, hidden_ref):
    width, hidden_width = gate_ref.shape
    scaled = rows_ref[:, width:]
    rows = rows_ref[:, :width]
    gate, up, down = gate_ref[...], up_ref[...], down_ref[...]
    pre_gate = dot(rows, gate)
    pre_up = dot(rows, up)
    grad_hidden = dot(scaled, down, ((1,), (1,)))
    sig = jax.nn.sigmoid(pre_gate)
    silu = pre_gate * sig
    hidden = (silu * pre_up).astype(BF16)
    prob_grad = jnp.sum(hidden.astype(F32) * grad_hidden, axis=1, keepdims=True)
    gate_grad = (grad_hidden * pre_up * sig * (1.0 + pre_gate * (1.0 - sig))).astype(BF16)
    up_grad = (grad_hidden * silu).astype(BF16)
    back = dot(gate_grad, gate, ((1,), (1,))) + dot(up_grad, up, ((1,), (1,)))
    ret_ref[:, :width] = back.astype(BF16)
    ret_ref[:, width:] = jnp.broadcast_to(prob_grad, (rows.shape[0], LANES)).astype(BF16)
    both_ref[:, :hidden_width] = gate_grad
    both_ref[:, hidden_width:] = up_grad
    hidden_ref[...] = hidden


def part_kernel(core_ref, rows_hbm, both_ref, hidden_ref, keep_hbm, give_hbm, rows, keep, give, in_sems, out_sems):
    chips, part_rows, columns = keep.shape
    hidden_width = hidden_ref.shape[1]
    width = rows.shape[1] // 2
    share = width // (2 * chips)
    down_share = hidden_width // (2 * chips)
    half = width // 2
    first = core_ref[0] == 0

    spans = [(width + side * half, half) for side in range(2)]
    spans += [(chip * 2 * share, 2 * share) for chip in range(chips)]
    loads = [
        pltpu.make_async_copy(rows_hbm.at[:, pl.ds(*span)], rows.at[:, pl.ds(*span)], in_sems.at[i])
        for i, span in enumerate(spans)
    ]
    for load in loads:
        load.start()

    def put(chip, low, pair):
        size = pair.shape[0] // 2
        keep[chip, low : low + size, :] = jnp.where(first, pair[:size], pair[size:]).astype(BF16)
        give[chip, low : low + size, :] = jnp.where(first, pair[size:], pair[:size]).astype(BF16)

    hidden = hidden_ref[...]
    for side in range(2):
        loads[side].wait()
        part = dot(hidden, rows[:, width + side * half : width + (side + 1) * half], ((0,), (0,)))
        for chip in range(chips):
            put(chip, share + side * down_share, part[chip * 2 * down_share : (chip + 1) * 2 * down_share])
    both = both_ref[...]
    stores = []
    for chip in range(chips):
        loads[2 + chip].wait()
        put(chip, 0, dot(rows[:, chip * 2 * share : (chip + 1) * 2 * share], both, ((0,), (0,))))
        stores.append(pltpu.make_async_copy(give.at[chip], give_hbm.at[chip], out_sems.at[2 * chip]))
        stores.append(pltpu.make_async_copy(keep.at[chip], keep_hbm.at[chip], out_sems.at[2 * chip + 1]))
        stores[-2].start()
        stores[-1].start()
    for store in stores:
        store.wait()


def chip_sum_kernel(
    chip_ref, keep_hbm, got_hbm, own_ref, right_ref, left_ref, far_low_ref, far_high_ref, keep, got, sems
):
    chips, part_rows, _ = keep.shape
    half = part_rows // 2
    loads = []
    for s in (2, 1, 3, 0):
        chip = (chip_ref[0] + s) & (chips - 1)
        loads.append(pltpu.make_async_copy(keep_hbm.at[chip], keep.at[s], sems.at[2 * s]))
        loads.append(pltpu.make_async_copy(got_hbm.at[chip], got.at[s], sems.at[2 * s + 1]))
    for load in loads:
        load.start()

    def total(s, low, size):
        rows = pl.ds(low, size)
        return (keep[s, rows].astype(F32) + got[s, rows].astype(F32)).astype(BF16)

    loads[0].wait()
    loads[1].wait()
    far_low_ref[...] = total(2, 0, half)
    far_high_ref[...] = total(2, half, half)
    for i, (s, ref) in enumerate(((1, right_ref), (3, left_ref), (0, own_ref))):
        loads[2 * i + 2].wait()
        loads[2 * i + 3].wait()
        ref[...] = total(s, 0, part_rows)


def relay_kernel(right_ref, left_ref, low_ref, high_ref, to_right_ref, to_left_ref):
    half = low_ref.shape[0]
    to_right_ref[:half] = (right_ref[:half].astype(F32) + low_ref[...].astype(F32)).astype(BF16)
    to_right_ref[half:] = right_ref[half:]
    to_left_ref[:half] = left_ref[:half]
    to_left_ref[half:] = (left_ref[half:].astype(F32) + high_ref[...].astype(F32)).astype(BF16)


def combine_kernel(base_ref, back_ref, pick_ref, extra_ref, sum_ref):
    slots = back_ref.shape[0]
    width = back_ref.shape[1] - LANES
    tokens = sum_ref.shape[0]
    pick = pick_ref[...]
    sum_ref[:, :width] = dot(pick, back_ref[:, :width]).astype(BF16)
    expert, _, _ = slot_parts(iota((slots, LANES), 0))
    own = iota((slots, LANES), 1) == expert
    spread = jnp.where(own, back_ref[:, width:].astype(F32), 0.0).astype(BF16)
    by_expert = dot(pick, spread)
    extras = extra_ref[...].astype(F32)
    lane = iota((tokens, LANES), 1)
    expert_lane = served(lane, base_ref[0])
    result = jnp.zeros((tokens, LANES), F32)
    for k in range(TOP):
        hit = extras[:, k : k + 1] == expert_lane
        value = jnp.sum(jnp.where(hit, by_expert, 0.0), axis=1, keepdims=True)
        value = value / extras[:, TOP + k : TOP + k + 1]
        result = jnp.where(lane == k, value, result)
    sum_ref[:, width:] = result.astype(BF16)


def finish_kernel(*refs):
    sums_ref, part_refs = refs[0], refs[1:-5]
    in_ref, prob_ref, gate_ref, up_ref, down_ref = refs[-5:]
    width = in_ref.shape[1]
    total = sums_ref[0].astype(F32)
    for s in range(1, FAR):
        total = total + sums_ref[s].astype(F32)
    in_ref[...] = total[:, :width].astype(BF16)
    pick = jnp.where(iota((TOP, LANES), 0) == iota((TOP, LANES), 1), 1.0, 0.0).astype(BF16)
    prob_ref[...] = dot(pick, total[:, width:].astype(BF16), ((1,), (1,))).astype(BF16)
    share, hidden_width = gate_ref.shape
    down_share = down_ref.shape[0]
    half = width // 2

    def part(low, size):
        result = part_refs[0][low : low + size, :].astype(F32)
        for ref in part_refs[1:]:
            result = result + ref[low : low + size, :].astype(F32)
        return result

    gate_up = part(0, share)
    gate_ref[...] = gate_up[:, :hidden_width]
    up_ref[...] = gate_up[:, hidden_width:]
    down_ref[:, :half] = part(share, down_share)
    down_ref[:, half:] = part(share + down_share, down_share)


def params(mib):
    return pltpu.CompilerParams(vmem_limit_bytes=mib * MIB)


def cost(flops, nbytes):
    return pl.CostEstimate(flops=flops, bytes_accessed=nbytes, transcendentals=0)


def per_device(layer_in, grad_out, expert_ids, gate_probs, gate_weight, up_weight, down_weight):
    block, width = layer_in.shape
    hidden_width = gate_weight.shape[2]
    chips = lax.axis_size("x")
    groups = 2 * chips
    tokens = FAR * block
    slots = NEAR * FAR * CAP
    share = width // groups
    down_share = hidden_width // groups
    part_rows = share + 2 * down_share
    core = lax.axis_index("core").astype(jnp.int32)
    chip = lax.axis_index("x").astype(jnp.int32)
    moved = core * (NEAR // 2)
    place = lax.axis_index(("far", "near", "y")) - moved + EXPERTS
    base = ((place & -NEAR) + moved).astype(jnp.int32).reshape(1)
    scalar = pl.BlockSpec(memory_space=pltpu.SMEM)
    hbm = pl.BlockSpec(memory_space=pltpu.HBM)

    def shape(*dims):
        return jax.ShapeDtypeStruct(dims, BF16)

    packed = pl.pallas_call(
        pack_kernel,
        out_shape=shape(block, 2 * width + LANES),
        in_specs=[hbm] * 2 + whole(2),
        out_specs=hbm,
        scratch_shapes=[pltpu.VMEM((block, LANES), BF16), pltpu.SemaphoreType.DMA((3,))],
        compiler_params=params(60),
        name="pack_tokens",
    )(layer_in, grad_out, expert_ids.T, gate_probs.T)
    near_tokens = lax.all_gather(packed, "far", tiled=True)

    send, pick = pl.pallas_call(
        select_kernel,
        out_shape=(shape(slots, 2 * width), shape(tokens, slots)),
        in_specs=[scalar] + whole(1),
        out_specs=tuple(whole(2)),
        compiler_params=params(24),
        name="select_rows",
    )(base, near_tokens)

    exchange = functools.partial(lax.all_to_all, split_axis=0, concat_axis=0, tiled=True)
    near_exchange = functools.partial(
        exchange,
        axis_name=("x", "core", "far", "near", "y"),
        axis_index_groups=windows(groups, EXPERTS),
    )
    rows = near_exchange(send.reshape(NEAR, FAR * CAP, 2 * width)).reshape(slots, 2 * width)

    matmul = 2 * slots * width * hidden_width
    back, both, hidden = pl.pallas_call(
        expert_kernel,
        out_shape=(shape(slots, width + LANES), shape(slots, 2 * hidden_width), shape(slots, hidden_width)),
        in_specs=whole(4),
        out_specs=tuple(whole(3)),
        compiler_params=params(32),
        cost_estimate=cost(5 * matmul, 8 * MIB),
        name="expert_rows",
    )(rows, gate_weight[0], up_weight[0], down_weight[0])
    back = near_exchange(back.reshape(NEAR, FAR * CAP, width + LANES)).reshape(slots, width + LANES)

    keep, give = pl.pallas_call(
        part_kernel,
        out_shape=(shape(chips, part_rows, 2 * hidden_width),) * 2,
        in_specs=[scalar, hbm] + whole(2),
        out_specs=(hbm, hbm),
        scratch_shapes=[
            pltpu.VMEM((slots, 2 * width), BF16),
            pltpu.VMEM((chips, part_rows, 2 * hidden_width), BF16),
            pltpu.VMEM((chips, part_rows, 2 * hidden_width), BF16),
            pltpu.SemaphoreType.DMA((chips + 2,)),
            pltpu.SemaphoreType.DMA((2 * chips,)),
        ],
        compiler_params=params(52),
        cost_estimate=cost(3 * matmul, 8 * MIB),
        name="weight_parts",
    )(core.reshape(1), rows, both, hidden)
    got = lax.ppermute(give, "core", [(0, 1), (1, 0)])
    share_shape, half_shape = shape(part_rows, 2 * hidden_width), shape(part_rows // 2, 2 * hidden_width)
    own, right, left, far_low, far_high = pl.pallas_call(
        chip_sum_kernel,
        out_shape=(share_shape,) * 3 + (half_shape,) * 2,
        in_specs=[scalar, hbm, hbm],
        out_specs=tuple(whole(5)),
        scratch_shapes=[
            pltpu.VMEM((chips, part_rows, 2 * hidden_width), BF16),
            pltpu.VMEM((chips, part_rows, 2 * hidden_width), BF16),
            pltpu.SemaphoreType.DMA((2 * chips,)),
        ],
        compiler_params=params(52),
        cost_estimate=cost(MIB, 6 * MIB),
        name="chip_sums",
    )(chip.reshape(1), keep, got)
    to_right = [(i, (i + 1) % chips) for i in range(chips)]
    to_left = [(i, (i - 1) % chips) for i in range(chips)]
    got_low = lax.ppermute(far_low, "x", to_right)
    got_high = lax.ppermute(far_high, "x", to_left)
    sums = pl.pallas_call(
        combine_kernel,
        out_shape=shape(tokens, width + LANES),
        in_specs=[scalar] + whole(3),
        out_specs=whole(1)[0],
        compiler_params=params(24),
        name="combine_rows",
    )(base, back, pick, near_tokens[:, 2 * width :])
    right, left, sums = lax.optimization_barrier((right, left, sums))
    right, left = pl.pallas_call(
        relay_kernel,
        out_shape=(share_shape,) * 2,
        in_specs=whole(4),
        out_specs=tuple(whole(2)),
        compiler_params=params(8),
        cost_estimate=cost(MIB, 2 * MIB),
        name="relay_sums",
    )(right, left, got_low, got_high)
    parts = [own, lax.ppermute(right, "x", to_right), lax.ppermute(left, "x", to_left)]

    sums, _ = lax.optimization_barrier((sums, right))
    sums = exchange(sums.reshape(FAR, block, width + LANES), "far")

    grad_in, grad_probs, grad_gate, grad_up, grad_down = pl.pallas_call(
        finish_kernel,
        out_shape=(
            shape(block, width),
            shape(TOP, block),
            jax.ShapeDtypeStruct((share, hidden_width), F32),
            jax.ShapeDtypeStruct((share, hidden_width), F32),
            jax.ShapeDtypeStruct((down_share, width), F32),
        ),
        in_specs=whole(1 + len(parts)),
        out_specs=tuple(whole(5)),
        compiler_params=params(24),
        name="finish",
    )(sums, *parts)
    return grad_in, grad_probs.T, grad_gate[None], grad_up[None], grad_down[None]


def solution(mesh):
    groups, experts = mesh.devices.shape
    split = Mesh(
        mesh.devices.reshape(groups // 2, 2, FAR, 4, experts // NEAR), ("x", "core", "far", "near", "y")
    )
    expert = ("far", "near", "y")
    token_spec = P(("x", "core") + expert, None)
    weight_spec = P(expert, None, None)
    grad_spec = P(expert, ("x", "core"), None)
    return jax.shard_map(
        per_device,
        mesh=split,
        in_specs=(token_spec,) * 4 + (weight_spec,) * 3,
        out_specs=(token_spec,) * 2 + (grad_spec,) * 3,
        check_vma=False,
    )
```

```python
import functools

import jax
import jax.numpy as jnp
from jax import lax
from jax.experimental import pallas as pl
from jax.experimental.pallas import tpu as pltpu
from jax.sharding import Mesh, PartitionSpec as P

F32 = jnp.float32
BF16 = jnp.bfloat16
LANES = 128
CAP = 6
FAR = 4
NEAR = 16
TOP = 8
EXPERTS = 64
MIB = 1 << 20


def iota(shape, dim):
    return lax.broadcasted_iota(jnp.int32, shape, dim)


def dot(a, b, contract=((1,), (0,))):
    return lax.dot_general(a, b, (contract, ((), ())), preferred_element_type=F32)


def whole(n):
    return [pl.BlockSpec(memory_space=pltpu.VMEM)] * n


def slot_parts(i):
    sixth = lax.shift_right_logical(i * 10923, 16)
    expert = lax.shift_right_logical(i * 2731, 16)
    return expert, sixth - FAR * expert, i - CAP * sixth


def served(lane, base):
    return jnp.where(lane < NEAR, (lane + base) & (EXPERTS - 1), -1).astype(F32)


def windows(groups, experts):
    lists = []
    for g in range(groups):
        for far in range(FAR):
            start = far * NEAR + (g % 2) * (NEAR // 2)
            lists.append([g * experts + (start + j) % experts for j in range(NEAR)])
    return lists


def pack_kernel(layer_ref, grad_ref, ids_ref, probs_ref, out_ref, ids_vmem, sems):
    width = layer_ref.shape[1]
    copies = [
        pltpu.make_async_copy(ids_ref, ids_vmem, sems.at[0]),
        pltpu.make_async_copy(layer_ref, out_ref.at[:, :width], sems.at[1]),
        pltpu.make_async_copy(grad_ref, out_ref.at[:, width : 2 * width], sems.at[2]),
    ]
    for copy in copies:
        copy.start()
    choice, lane = iota((TOP, LANES), 0), iota((TOP, LANES), 1)
    ids_lane = jnp.where(lane == choice, 1.0, 0.0).astype(BF16)
    probs_lane = jnp.where(lane == choice + TOP, 1.0, 0.0).astype(BF16)
    copies[0].wait()
    ids = ids_vmem[...].astype(F32).astype(BF16)
    extras = dot(ids, ids_lane, ((0,), (0,))) + dot(probs_ref[...], probs_lane, ((0,), (0,)))
    out_ref[:, 2 * width :] = extras.astype(BF16)
    copies[1].wait()
    copies[2].wait()


def select_kernel(base_ref, tok_ref, send_ref, pick_ref):
    tokens = tok_ref.shape[0]
    slots = send_ref.shape[0]
    width = send_ref.shape[1] // 2
    block = tokens // FAR
    extras = tok_ref[:, 2 * width :].astype(F32)
    lane = iota((tokens, LANES), 1)
    expert_lane = served(lane, base_ref[0])
    member = jnp.zeros((tokens, LANES), F32)
    prob = jnp.zeros((tokens, LANES), F32)
    for k in range(TOP):
        hit = extras[:, k : k + 1] == expert_lane
        member = jnp.where(hit, 1.0, member)
        prob = jnp.where(hit, extras[:, TOP + k : TOP + k + 1], prob)
    row, col = iota((tokens, tokens), 0), iota((tokens, tokens), 1)
    shift = block.bit_length() - 1
    same = lax.shift_right_logical(row, shift) == lax.shift_right_logical(col, shift)
    earlier = jnp.where(same & (col < row), 1.0, 0.0).astype(BF16)
    rank = dot(earlier, member.astype(BF16))
    code = jnp.where(member > 0.0, rank, -1.0).astype(BF16)
    eye = jnp.where(row == col, 1.0, 0.0).astype(BF16)
    code_t = dot(code, eye, ((0,), (0,))).astype(BF16)
    prob_t = dot(prob.astype(BF16), eye, ((0,), (0,))).astype(BF16)

    expert, home, place = slot_parts(iota((slots, LANES), 0))
    spread = jnp.where(iota((slots, LANES), 1) == expert, 1.0, 0.0).astype(BF16)
    code_row = dot(spread, code_t)
    token_block = lax.shift_right_logical(iota((slots, tokens), 1), shift)
    chosen = (code_row == place.astype(F32)) & (token_block == home)
    select = jnp.where(chosen, 1.0, 0.0).astype(BF16)
    prob_row = jnp.sum(jnp.where(chosen, dot(spread, prob_t), 0.0), axis=1, keepdims=True)
    send_ref[:, :width] = dot(select, tok_ref[:, :width]).astype(BF16)
    grads = dot(select, tok_ref[:, width : 2 * width])
    send_ref[:, width:] = (prob_row * grads).astype(BF16)

    expert, home, place = slot_parts(iota((LANES, slots), 1))
    spread = jnp.where(iota((LANES, slots), 0) == expert, 1.0, 0.0).astype(BF16)
    code_col = dot(code, spread)
    token_block = lax.shift_right_logical(iota((tokens, slots), 0), shift)
    chosen = (code_col == place.astype(F32)) & (token_block == home)
    pick_ref[...] = jnp.where(chosen, 1.0, 0.0).astype(BF16)


def expert_kernel(rows_ref, gate_ref, up_ref, down_ref, ret_ref, both_ref, hidden_ref):
    width, hidden_width = gate_ref.shape
    scaled = rows_ref[:, width:]
    rows = rows_ref[:, :width]
    gate, up, down = gate_ref[...], up_ref[...], down_ref[...]
    pre_gate = dot(rows, gate)
    pre_up = dot(rows, up)
    grad_hidden = dot(scaled, down, ((1,), (1,)))
    sig = jax.nn.sigmoid(pre_gate)
    silu = pre_gate * sig
    hidden = (silu * pre_up).astype(BF16)
    prob_grad = jnp.sum(hidden.astype(F32) * grad_hidden, axis=1, keepdims=True)
    gate_grad = (grad_hidden * pre_up * sig * (1.0 + pre_gate * (1.0 - sig))).astype(BF16)
    up_grad = (grad_hidden * silu).astype(BF16)
    back = dot(gate_grad, gate, ((1,), (1,))) + dot(up_grad, up, ((1,), (1,)))
    ret_ref[:, :width] = back.astype(BF16)
    ret_ref[:, width:] = jnp.broadcast_to(prob_grad, (rows.shape[0], LANES)).astype(BF16)
    both_ref[:, :hidden_width] = gate_grad
    both_ref[:, hidden_width:] = up_grad
    hidden_ref[...] = hidden


def part_kernel(core_ref, rows_hbm, both_ref, hidden_ref, keep_hbm, give_hbm, rows, keep, give, in_sems, out_sems):
    chips, part_rows, columns = keep.shape
    hidden_width = hidden_ref.shape[1]
    width = rows.shape[1] // 2
    share = width // (2 * chips)
    down_share = hidden_width // (2 * chips)
    half = width // 2
    first = core_ref[0] == 0

    spans = [(width + side * half, half) for side in range(2)]
    spans += [(chip * 2 * share, 2 * share) for chip in range(chips)]
    loads = [
        pltpu.make_async_copy(rows_hbm.at[:, pl.ds(*span)], rows.at[:, pl.ds(*span)], in_sems.at[i])
        for i, span in enumerate(spans)
    ]
    for load in loads:
        load.start()

    def put(chip, low, pair):
        size = pair.shape[0] // 2
        keep[chip, low : low + size, :] = jnp.where(first, pair[:size], pair[size:]).astype(BF16)
        give[chip, low : low + size, :] = jnp.where(first, pair[size:], pair[:size]).astype(BF16)

    hidden = hidden_ref[...]
    for side in range(2):
        loads[side].wait()
        part = dot(hidden, rows[:, width + side * half : width + (side + 1) * half], ((0,), (0,)))
        for chip in range(chips):
            put(chip, share + side * down_share, part[chip * 2 * down_share : (chip + 1) * 2 * down_share])
    both = both_ref[...]
    stores = []
    for chip in range(chips):
        loads[2 + chip].wait()
        put(chip, 0, dot(rows[:, chip * 2 * share : (chip + 1) * 2 * share], both, ((0,), (0,))))
        stores.append(pltpu.make_async_copy(give.at[chip], give_hbm.at[chip], out_sems.at[2 * chip]))
        stores.append(pltpu.make_async_copy(keep.at[chip], keep_hbm.at[chip], out_sems.at[2 * chip + 1]))
        stores[-2].start()
        stores[-1].start()
    for store in stores:
        store.wait()


def chip_sum_kernel(chip_ref, keep_hbm, got_hbm, *refs):
    out_refs, (keep, got, sems) = refs[:-3], refs[-3:]
    chips = keep.shape[0]
    order = (2, 1, 3, 0)
    loads = []
    for s in order:
        chip = (chip_ref[0] + s) & (chips - 1)
        loads.append(pltpu.make_async_copy(keep_hbm.at[chip], keep.at[s], sems.at[2 * s]))
        loads.append(pltpu.make_async_copy(got_hbm.at[chip], got.at[s], sems.at[2 * s + 1]))
    for load in loads:
        load.start()
    for i, s in enumerate(order):
        loads[2 * i].wait()
        loads[2 * i + 1].wait()
        out_refs[s][...] = (keep[s].astype(F32) + got[s].astype(F32)).astype(BF16)


def combine_kernel(base_ref, back_ref, pick_ref, extra_ref, sum_ref):
    slots = back_ref.shape[0]
    width = back_ref.shape[1] - LANES
    tokens = sum_ref.shape[0]
    pick = pick_ref[...]
    sum_ref[:, :width] = dot(pick, back_ref[:, :width]).astype(BF16)
    expert, _, _ = slot_parts(iota((slots, LANES), 0))
    own = iota((slots, LANES), 1) == expert
    spread = jnp.where(own, back_ref[:, width:].astype(F32), 0.0).astype(BF16)
    by_expert = dot(pick, spread)
    extras = extra_ref[...].astype(F32)
    lane = iota((tokens, LANES), 1)
    expert_lane = served(lane, base_ref[0])
    result = jnp.zeros((tokens, LANES), F32)
    for k in range(TOP):
        hit = extras[:, k : k + 1] == expert_lane
        value = jnp.sum(jnp.where(hit, by_expert, 0.0), axis=1, keepdims=True)
        value = value / extras[:, TOP + k : TOP + k + 1]
        result = jnp.where(lane == k, value, result)
    sum_ref[:, width:] = result.astype(BF16)


def finish_kernel(*refs):
    sums_ref, part_refs = refs[0], refs[1:-5]
    in_ref, prob_ref, gate_ref, up_ref, down_ref = refs[-5:]
    width = in_ref.shape[1]
    total = sums_ref[0].astype(F32)
    for s in range(1, FAR):
        total = total + sums_ref[s].astype(F32)
    in_ref[...] = total[:, :width].astype(BF16)
    pick = jnp.where(iota((TOP, LANES), 0) == iota((TOP, LANES), 1), 1.0, 0.0).astype(BF16)
    prob_ref[...] = dot(pick, total[:, width:].astype(BF16), ((1,), (1,))).astype(BF16)
    share, hidden_width = gate_ref.shape
    down_share = down_ref.shape[0]
    half = width // 2

    def part(low, size):
        result = part_refs[0][low : low + size, :].astype(F32)
        for ref in part_refs[1:]:
            result = result + ref[low : low + size, :].astype(F32)
        return result

    gate_up = part(0, share)
    gate_ref[...] = gate_up[:, :hidden_width]
    up_ref[...] = gate_up[:, hidden_width:]
    down_ref[:, :half] = part(share, down_share)
    down_ref[:, half:] = part(share + down_share, down_share)


def params(mib):
    return pltpu.CompilerParams(vmem_limit_bytes=mib * MIB)


def cost(flops, nbytes):
    return pl.CostEstimate(flops=flops, bytes_accessed=nbytes, transcendentals=0)


def per_device(layer_in, grad_out, expert_ids, gate_probs, gate_weight, up_weight, down_weight):
    block, width = layer_in.shape
    hidden_width = gate_weight.shape[2]
    chips = lax.axis_size("x")
    groups = 2 * chips
    tokens = FAR * block
    slots = NEAR * FAR * CAP
    share = width // groups
    down_share = hidden_width // groups
    part_rows = share + 2 * down_share
    core = lax.axis_index("core").astype(jnp.int32)
    chip = lax.axis_index("x").astype(jnp.int32)
    moved = core * (NEAR // 2)
    place = lax.axis_index(("far", "near", "y")) - moved + EXPERTS
    base = ((place & -NEAR) + moved).astype(jnp.int32).reshape(1)
    scalar = pl.BlockSpec(memory_space=pltpu.SMEM)
    hbm = pl.BlockSpec(memory_space=pltpu.HBM)

    def shape(*dims):
        return jax.ShapeDtypeStruct(dims, BF16)

    packed = pl.pallas_call(
        pack_kernel,
        out_shape=shape(block, 2 * width + LANES),
        in_specs=[hbm] * 3 + whole(1),
        out_specs=whole(1)[0],
        scratch_shapes=[pltpu.VMEM((TOP, block), jnp.int32), pltpu.SemaphoreType.DMA((3,))],
        compiler_params=params(60),
        name="pack_tokens",
    )(layer_in, grad_out, expert_ids.T, gate_probs.T)
    near_tokens = lax.all_gather(packed, "far", tiled=True)

    send, pick = pl.pallas_call(
        select_kernel,
        out_shape=(shape(slots, 2 * width), shape(tokens, slots)),
        in_specs=[scalar] + whole(1),
        out_specs=tuple(whole(2)),
        compiler_params=params(24),
        name="select_rows",
    )(base, near_tokens)

    exchange = functools.partial(lax.all_to_all, split_axis=0, concat_axis=0, tiled=True)
    near_exchange = functools.partial(
        exchange,
        axis_name=("x", "core", "far", "near", "y"),
        axis_index_groups=windows(groups, EXPERTS),
    )
    rows = near_exchange(send.reshape(NEAR, FAR * CAP, 2 * width)).reshape(slots, 2 * width)

    matmul = 2 * slots * width * hidden_width
    back, both, hidden = pl.pallas_call(
        expert_kernel,
        out_shape=(shape(slots, width + LANES), shape(slots, 2 * hidden_width), shape(slots, hidden_width)),
        in_specs=whole(4),
        out_specs=tuple(whole(3)),
        compiler_params=params(32),
        cost_estimate=cost(5 * matmul, 8 * MIB),
        name="expert_rows",
    )(rows, gate_weight[0], up_weight[0], down_weight[0])
    back = near_exchange(back.reshape(NEAR, FAR * CAP, width + LANES)).reshape(slots, width + LANES)

    keep, give = pl.pallas_call(
        part_kernel,
        out_shape=(shape(chips, part_rows, 2 * hidden_width),) * 2,
        in_specs=[scalar, hbm] + whole(2),
        out_specs=(hbm, hbm),
        scratch_shapes=[
            pltpu.VMEM((slots, 2 * width), BF16),
            pltpu.VMEM((chips, part_rows, 2 * hidden_width), BF16),
            pltpu.VMEM((chips, part_rows, 2 * hidden_width), BF16),
            pltpu.SemaphoreType.DMA((chips + 2,)),
            pltpu.SemaphoreType.DMA((2 * chips,)),
        ],
        compiler_params=params(52),
        cost_estimate=cost(3 * matmul, 8 * MIB),
        name="weight_parts",
    )(core.reshape(1), rows, both, hidden)
    got = lax.ppermute(give, "core", [(0, 1), (1, 0)])
    chip_sums = pl.pallas_call(
        chip_sum_kernel,
        out_shape=(shape(part_rows, 2 * hidden_width),) * chips,
        in_specs=[scalar, hbm, hbm],
        out_specs=tuple(whole(chips)),
        scratch_shapes=[
            pltpu.VMEM((chips, part_rows, 2 * hidden_width), BF16),
            pltpu.VMEM((chips, part_rows, 2 * hidden_width), BF16),
            pltpu.SemaphoreType.DMA((2 * chips,)),
        ],
        compiler_params=params(52),
        cost_estimate=cost(MIB, 6 * MIB),
        name="chip_sums",
    )(chip.reshape(1), keep, got)
    parts = [
        lax.ppermute(chip_sums[s], "x", [(i, (i + s) % chips) for i in range(chips)]) for s in (2, 1, 3)
    ] + [chip_sums[0]]

    back, _ = lax.optimization_barrier((back, chip_sums[0]))
    sums = pl.pallas_call(
        combine_kernel,
        out_shape=shape(tokens, width + LANES),
        in_specs=[scalar] + whole(3),
        out_specs=whole(1)[0],
        compiler_params=params(24),
        name="combine_rows",
    )(base, back, pick, near_tokens[:, 2 * width :])
    sums = exchange(sums.reshape(FAR, block, width + LANES), "far")

    grad_in, grad_probs, grad_gate, grad_up, grad_down = pl.pallas_call(
        finish_kernel,
        out_shape=(
            shape(block, width),
            shape(TOP, block),
            jax.ShapeDtypeStruct((share, hidden_width), F32),
            jax.ShapeDtypeStruct((share, hidden_width), F32),
            jax.ShapeDtypeStruct((down_share, width), F32),
        ),
        in_specs=whole(1 + len(parts)),
        out_specs=tuple(whole(5)),
        compiler_params=params(24),
        name="finish",
    )(sums, *parts)
    return grad_in, grad_probs.T, grad_gate[None], grad_up[None], grad_down[None]


def solution(mesh):
    groups, experts = mesh.devices.shape
    split = Mesh(
        mesh.devices.reshape(groups // 2, 2, FAR, 4, experts // NEAR), ("x", "core", "far", "near", "y")
    )
    expert = ("far", "near", "y")
    token_spec = P(("x", "core") + expert, None)
    weight_spec = P(expert, None, None)
    grad_spec = P(expert, ("x", "core"), None)
    return jax.shard_map(
        per_device,
        mesh=split,
        in_specs=(token_spec,) * 4 + (weight_spec,) * 3,
        out_specs=(token_spec,) * 2 + (grad_spec,) * 3,
        check_vma=False,
    )
```

```python
import functools

import jax
import jax.numpy as jnp
from jax import lax
from jax.experimental import pallas as pl
from jax.experimental.pallas import tpu as pltpu
from jax.sharding import Mesh, PartitionSpec as P

F32 = jnp.float32
BF16 = jnp.bfloat16
LANES = 128
CAP = 6
FAR = 4
NEAR = 16
TOP = 8
EXPERTS = 64
MIB = 1 << 20


def iota(shape, dim):
    return lax.broadcasted_iota(jnp.int32, shape, dim)


def dot(a, b, contract=((1,), (0,))):
    return lax.dot_general(a, b, (contract, ((), ())), preferred_element_type=F32)


def whole(n):
    return [pl.BlockSpec(memory_space=pltpu.VMEM)] * n


def slot_parts(i):
    sixth = lax.shift_right_logical(i * 10923, 16)
    expert = lax.shift_right_logical(i * 2731, 16)
    return expert, sixth - FAR * expert, i - CAP * sixth


def served(lane, base):
    return jnp.where(lane < NEAR, (lane + base) & (EXPERTS - 1), -1).astype(F32)


def windows(groups, experts):
    lists = []
    for g in range(groups):
        for far in range(FAR):
            start = far * NEAR + (g % 2) * (NEAR // 2)
            lists.append([g * experts + (start + j) % experts for j in range(NEAR)])
    return lists


def pack_kernel(layer_ref, grad_ref, ids_ref, probs_ref, out_ref, ids_vmem, sems):
    width = layer_ref.shape[1]
    copies = [
        pltpu.make_async_copy(ids_ref, ids_vmem, sems.at[0]),
        pltpu.make_async_copy(layer_ref, out_ref.at[:, :width], sems.at[1]),
        pltpu.make_async_copy(grad_ref, out_ref.at[:, width : 2 * width], sems.at[2]),
    ]
    for copy in copies:
        copy.start()
    choice, lane = iota((TOP, LANES), 0), iota((TOP, LANES), 1)
    ids_lane = jnp.where(lane == choice, 1.0, 0.0).astype(BF16)
    probs_lane = jnp.where(lane == choice + TOP, 1.0, 0.0).astype(BF16)
    copies[0].wait()
    ids = ids_vmem[...].astype(F32).astype(BF16)
    extras = dot(ids, ids_lane, ((0,), (0,))) + dot(probs_ref[...], probs_lane, ((0,), (0,)))
    out_ref[:, 2 * width :] = extras.astype(BF16)
    copies[1].wait()
    copies[2].wait()


def select_kernel(base_ref, tok_ref, send_ref, pick_ref):
    tokens = tok_ref.shape[0]
    slots = send_ref.shape[0]
    width = send_ref.shape[1] // 2
    block = tokens // FAR
    extras = tok_ref[:, 2 * width :].astype(F32)
    lane = iota((tokens, LANES), 1)
    expert_lane = served(lane, base_ref[0])
    member = jnp.zeros((tokens, LANES), F32)
    prob = jnp.zeros((tokens, LANES), F32)
    for k in range(TOP):
        hit = extras[:, k : k + 1] == expert_lane
        member = jnp.where(hit, 1.0, member)
        prob = jnp.where(hit, extras[:, TOP + k : TOP + k + 1], prob)
    row, col = iota((tokens, tokens), 0), iota((tokens, tokens), 1)
    shift = block.bit_length() - 1
    same = lax.shift_right_logical(row, shift) == lax.shift_right_logical(col, shift)
    earlier = jnp.where(same & (col < row), 1.0, 0.0).astype(BF16)
    rank = dot(earlier, member.astype(BF16))
    code = jnp.where(member > 0.0, rank, -1.0).astype(BF16)
    eye = jnp.where(row == col, 1.0, 0.0).astype(BF16)
    code_t = dot(code, eye, ((0,), (0,))).astype(BF16)
    prob_t = dot(prob.astype(BF16), eye, ((0,), (0,))).astype(BF16)

    expert, home, place = slot_parts(iota((slots, LANES), 0))
    spread = jnp.where(iota((slots, LANES), 1) == expert, 1.0, 0.0).astype(BF16)
    code_row = dot(spread, code_t)
    token_block = lax.shift_right_logical(iota((slots, tokens), 1), shift)
    chosen = (code_row == place.astype(F32)) & (token_block == home)
    select = jnp.where(chosen, 1.0, 0.0).astype(BF16)
    prob_row = jnp.sum(jnp.where(chosen, dot(spread, prob_t), 0.0), axis=1, keepdims=True)
    send_ref[:, :width] = dot(select, tok_ref[:, :width]).astype(BF16)
    grads = dot(select, tok_ref[:, width : 2 * width])
    send_ref[:, width:] = (prob_row * grads).astype(BF16)

    expert, home, place = slot_parts(iota((LANES, slots), 1))
    spread = jnp.where(iota((LANES, slots), 0) == expert, 1.0, 0.0).astype(BF16)
    code_col = dot(code, spread)
    token_block = lax.shift_right_logical(iota((tokens, slots), 0), shift)
    chosen = (code_col == place.astype(F32)) & (token_block == home)
    pick_ref[...] = jnp.where(chosen, 1.0, 0.0).astype(BF16)


def expert_kernel(rows_ref, gate_ref, up_ref, down_ref, ret_ref, both_ref, hidden_ref):
    width, hidden_width = gate_ref.shape
    scaled = rows_ref[:, width:]
    rows = rows_ref[:, :width]
    gate, up, down = gate_ref[...], up_ref[...], down_ref[...]
    pre_gate = dot(rows, gate)
    pre_up = dot(rows, up)
    grad_hidden = dot(scaled, down, ((1,), (1,)))
    sig = jax.nn.sigmoid(pre_gate)
    silu = pre_gate * sig
    hidden = (silu * pre_up).astype(BF16)
    prob_grad = jnp.sum(hidden.astype(F32) * grad_hidden, axis=1, keepdims=True)
    gate_grad = (grad_hidden * pre_up * sig * (1.0 + pre_gate * (1.0 - sig))).astype(BF16)
    up_grad = (grad_hidden * silu).astype(BF16)
    back = dot(gate_grad, gate, ((1,), (1,))) + dot(up_grad, up, ((1,), (1,)))
    ret_ref[:, :width] = back.astype(BF16)
    ret_ref[:, width:] = jnp.broadcast_to(prob_grad, (rows.shape[0], LANES)).astype(BF16)
    both_ref[:, :hidden_width] = gate_grad
    both_ref[:, hidden_width:] = up_grad
    hidden_ref[...] = hidden


def part_kernel(core_ref, rows_hbm, both_ref, hidden_ref, keep_hbm, give_hbm, rows, keep, give, in_sems, out_sems):
    chips, part_rows, columns = keep.shape
    hidden_width = hidden_ref.shape[1]
    width = rows.shape[1] // 2
    share = width // (2 * chips)
    down_share = hidden_width // (2 * chips)
    half = width // 2
    first = core_ref[0] == 0

    spans = [(width + side * half, half) for side in range(2)]
    spans += [(chip * 2 * share, 2 * share) for chip in range(chips)]
    loads = [
        pltpu.make_async_copy(rows_hbm.at[:, pl.ds(*span)], rows.at[:, pl.ds(*span)], in_sems.at[i])
        for i, span in enumerate(spans)
    ]
    for load in loads:
        load.start()

    def put(chip, low, pair):
        size = pair.shape[0] // 2
        keep[chip, low : low + size, :] = jnp.where(first, pair[:size], pair[size:]).astype(BF16)
        give[chip, low : low + size, :] = jnp.where(first, pair[size:], pair[:size]).astype(BF16)

    hidden = hidden_ref[...]
    for side in range(2):
        loads[side].wait()
        part = dot(hidden, rows[:, width + side * half : width + (side + 1) * half], ((0,), (0,)))
        for chip in range(chips):
            put(chip, share + side * down_share, part[chip * 2 * down_share : (chip + 1) * 2 * down_share])
    both = both_ref[...]
    stores = []
    for chip in range(chips):
        loads[2 + chip].wait()
        put(chip, 0, dot(rows[:, chip * 2 * share : (chip + 1) * 2 * share], both, ((0,), (0,))))
        stores.append(pltpu.make_async_copy(give.at[chip], give_hbm.at[chip], out_sems.at[2 * chip]))
        stores.append(pltpu.make_async_copy(keep.at[chip], keep_hbm.at[chip], out_sems.at[2 * chip + 1]))
        stores[-2].start()
        stores[-1].start()
    for store in stores:
        store.wait()


def chip_sum_kernel(chip_ref, keep_hbm, got_hbm, *refs):
    out_refs, (keep, got, sems) = refs[:-3], refs[-3:]
    chips = keep.shape[0]
    order = (2, 1, 3, 0)
    loads = []
    for s in order:
        chip = (chip_ref[0] + s) & (chips - 1)
        loads.append(pltpu.make_async_copy(keep_hbm.at[chip], keep.at[s], sems.at[2 * s]))
        loads.append(pltpu.make_async_copy(got_hbm.at[chip], got.at[s], sems.at[2 * s + 1]))
    for load in loads:
        load.start()
    for i, s in enumerate(order):
        loads[2 * i].wait()
        loads[2 * i + 1].wait()
        out_refs[s][...] = (keep[s].astype(F32) + got[s].astype(F32)).astype(BF16)


def combine_kernel(base_ref, back_ref, pick_ref, extra_ref, sum_ref):
    slots = back_ref.shape[0]
    width = back_ref.shape[1] - LANES
    tokens = sum_ref.shape[0]
    pick = pick_ref[...]
    sum_ref[:, :width] = dot(pick, back_ref[:, :width]).astype(BF16)
    expert, _, _ = slot_parts(iota((slots, LANES), 0))
    own = iota((slots, LANES), 1) == expert
    spread = jnp.where(own, back_ref[:, width:].astype(F32), 0.0).astype(BF16)
    by_expert = dot(pick, spread)
    extras = extra_ref[...].astype(F32)
    lane = iota((tokens, LANES), 1)
    expert_lane = served(lane, base_ref[0])
    result = jnp.zeros((tokens, LANES), F32)
    for k in range(TOP):
        hit = extras[:, k : k + 1] == expert_lane
        value = jnp.sum(jnp.where(hit, by_expert, 0.0), axis=1, keepdims=True)
        value = value / extras[:, TOP + k : TOP + k + 1]
        result = jnp.where(lane == k, value, result)
    sum_ref[:, width:] = result.astype(BF16)


def finish_kernel(sums_ref, in_ref, prob_ref):
    width = in_ref.shape[1]
    total = sums_ref[0].astype(F32)
    for s in range(1, FAR):
        total = total + sums_ref[s].astype(F32)
    in_ref[...] = total[:, :width].astype(BF16)
    pick = jnp.where(iota((TOP, LANES), 0) == iota((TOP, LANES), 1), 1.0, 0.0).astype(BF16)
    prob_ref[...] = dot(pick, total[:, width:].astype(BF16), ((1,), (1,))).astype(BF16)


def weight_sum_kernel(*refs):
    part_refs, (gate_ref, up_ref, down_ref) = refs[:-3], refs[-3:]
    share, hidden_width = gate_ref.shape
    down_share, width = down_ref.shape
    half = width // 2

    def part(low, size):
        result = part_refs[0][low : low + size, :].astype(F32)
        for ref in part_refs[1:]:
            result = result + ref[low : low + size, :].astype(F32)
        return result

    gate_up = part(0, share)
    gate_ref[...] = gate_up[:, :hidden_width]
    up_ref[...] = gate_up[:, hidden_width:]
    down_ref[:, :half] = part(share, down_share)
    down_ref[:, half:] = part(share + down_share, down_share)


def params(mib):
    return pltpu.CompilerParams(vmem_limit_bytes=mib * MIB)


def cost(flops, nbytes):
    return pl.CostEstimate(flops=flops, bytes_accessed=nbytes, transcendentals=0)


def per_device(layer_in, grad_out, expert_ids, gate_probs, gate_weight, up_weight, down_weight):
    block, width = layer_in.shape
    hidden_width = gate_weight.shape[2]
    chips = lax.axis_size("x")
    groups = 2 * chips
    tokens = FAR * block
    slots = NEAR * FAR * CAP
    share = width // groups
    down_share = hidden_width // groups
    part_rows = share + 2 * down_share
    core = lax.axis_index("core").astype(jnp.int32)
    chip = lax.axis_index("x").astype(jnp.int32)
    moved = core * (NEAR // 2)
    place = lax.axis_index(("far", "near", "y")) - moved + EXPERTS
    base = ((place & -NEAR) + moved).astype(jnp.int32).reshape(1)
    scalar = pl.BlockSpec(memory_space=pltpu.SMEM)
    hbm = pl.BlockSpec(memory_space=pltpu.HBM)

    def shape(*dims):
        return jax.ShapeDtypeStruct(dims, BF16)

    packed = pl.pallas_call(
        pack_kernel,
        out_shape=shape(block, 2 * width + LANES),
        in_specs=[hbm] * 3 + whole(1),
        out_specs=whole(1)[0],
        scratch_shapes=[pltpu.VMEM((TOP, block), jnp.int32), pltpu.SemaphoreType.DMA((3,))],
        compiler_params=params(60),
        name="pack_tokens",
    )(layer_in, grad_out, expert_ids.T, gate_probs.T)
    near_tokens = lax.all_gather(packed, "far", tiled=True)

    send, pick = pl.pallas_call(
        select_kernel,
        out_shape=(shape(slots, 2 * width), shape(tokens, slots)),
        in_specs=[scalar] + whole(1),
        out_specs=tuple(whole(2)),
        compiler_params=params(24),
        name="select_rows",
    )(base, near_tokens)

    exchange = functools.partial(lax.all_to_all, split_axis=0, concat_axis=0, tiled=True)
    near_exchange = functools.partial(
        exchange,
        axis_name=("x", "core", "far", "near", "y"),
        axis_index_groups=windows(groups, EXPERTS),
    )
    rows = near_exchange(send.reshape(NEAR, FAR * CAP, 2 * width)).reshape(slots, 2 * width)

    matmul = 2 * slots * width * hidden_width
    back, both, hidden = pl.pallas_call(
        expert_kernel,
        out_shape=(shape(slots, width + LANES), shape(slots, 2 * hidden_width), shape(slots, hidden_width)),
        in_specs=whole(4),
        out_specs=tuple(whole(3)),
        compiler_params=params(32),
        cost_estimate=cost(5 * matmul, 8 * MIB),
        name="expert_rows",
    )(rows, gate_weight[0], up_weight[0], down_weight[0])
    back = near_exchange(back.reshape(NEAR, FAR * CAP, width + LANES)).reshape(slots, width + LANES)

    keep, give = pl.pallas_call(
        part_kernel,
        out_shape=(shape(chips, part_rows, 2 * hidden_width),) * 2,
        in_specs=[scalar, hbm] + whole(2),
        out_specs=(hbm, hbm),
        scratch_shapes=[
            pltpu.VMEM((slots, 2 * width), BF16),
            pltpu.VMEM((chips, part_rows, 2 * hidden_width), BF16),
            pltpu.VMEM((chips, part_rows, 2 * hidden_width), BF16),
            pltpu.SemaphoreType.DMA((chips + 2,)),
            pltpu.SemaphoreType.DMA((2 * chips,)),
        ],
        compiler_params=params(52),
        cost_estimate=cost(3 * matmul, 8 * MIB),
        name="weight_parts",
    )(core.reshape(1), rows, both, hidden)
    got = lax.ppermute(give, "core", [(0, 1), (1, 0)])
    chip_sums = pl.pallas_call(
        chip_sum_kernel,
        out_shape=(shape(part_rows, 2 * hidden_width),) * chips,
        in_specs=[scalar, hbm, hbm],
        out_specs=tuple(whole(chips)),
        scratch_shapes=[
            pltpu.VMEM((chips, part_rows, 2 * hidden_width), BF16),
            pltpu.VMEM((chips, part_rows, 2 * hidden_width), BF16),
            pltpu.SemaphoreType.DMA((2 * chips,)),
        ],
        compiler_params=params(52),
        cost_estimate=cost(MIB, 6 * MIB),
        name="chip_sums",
    )(chip.reshape(1), keep, got)
    parts = [
        lax.ppermute(chip_sums[s], "x", [(i, (i + s) % chips) for i in range(chips)]) for s in (2, 1, 3)
    ] + [chip_sums[0]]

    back, _ = lax.optimization_barrier((back, chip_sums[0]))
    sums = pl.pallas_call(
        combine_kernel,
        out_shape=shape(tokens, width + LANES),
        in_specs=[scalar] + whole(3),
        out_specs=whole(1)[0],
        compiler_params=params(24),
        name="combine_rows",
    )(base, back, pick, near_tokens[:, 2 * width :])
    sums = exchange(sums.reshape(FAR, block, width + LANES), "far")

    grad_gate, grad_up, grad_down = pl.pallas_call(
        weight_sum_kernel,
        out_shape=(
            jax.ShapeDtypeStruct((share, hidden_width), F32),
            jax.ShapeDtypeStruct((share, hidden_width), F32),
            jax.ShapeDtypeStruct((down_share, width), F32),
        ),
        in_specs=whole(chips),
        out_specs=tuple(whole(3)),
        compiler_params=params(24),
        cost_estimate=cost(MIB, 3 * MIB),
        name="weight_sums",
    )(*parts)
    grad_in, grad_probs = pl.pallas_call(
        finish_kernel,
        out_shape=(shape(block, width), shape(TOP, block)),
        in_specs=whole(1),
        out_specs=tuple(whole(2)),
        compiler_params=params(24),
        name="finish",
    )(sums)
    return grad_in, grad_probs.T, grad_gate[None], grad_up[None], grad_down[None]


def solution(mesh):
    groups, experts = mesh.devices.shape
    split = Mesh(
        mesh.devices.reshape(groups // 2, 2, FAR, 4, experts // NEAR), ("x", "core", "far", "near", "y")
    )
    expert = ("far", "near", "y")
    token_spec = P(("x", "core") + expert, None)
    weight_spec = P(expert, None, None)
    grad_spec = P(expert, ("x", "core"), None)
    return jax.shard_map(
        per_device,
        mesh=split,
        in_specs=(token_spec,) * 4 + (weight_spec,) * 3,
        out_specs=(token_spec,) * 2 + (grad_spec,) * 3,
        check_vma=False,
    )
```

```python
import functools

import jax
import jax.numpy as jnp
from jax import lax
from jax.experimental import pallas as pl
from jax.experimental.pallas import tpu as pltpu
from jax.sharding import Mesh, PartitionSpec as P

F32 = jnp.float32
BF16 = jnp.bfloat16
LANES = 128
CAP = 6
FAR = 4
NEAR = 16
TOP = 8
EXPERTS = 64
MIB = 1 << 20
PLACING_FLOPS = 10**11


def iota(shape, dim):
    return lax.broadcasted_iota(jnp.int32, shape, dim)


def dot(a, b, contract=((1,), (0,))):
    return lax.dot_general(a, b, (contract, ((), ())), preferred_element_type=F32)


def whole(n):
    return [pl.BlockSpec(memory_space=pltpu.VMEM)] * n


def slot_parts(i):
    sixth = lax.shift_right_logical(i * 10923, 16)
    expert = lax.shift_right_logical(i * 2731, 16)
    return expert, sixth - FAR * expert, i - CAP * sixth


def served(lane, base):
    return jnp.where(lane < NEAR, (lane + base) & (EXPERTS - 1), -1).astype(F32)


def windows(groups, experts):
    lists = []
    for g in range(groups):
        for far in range(FAR):
            start = far * NEAR + (g % 2) * (NEAR // 2)
            lists.append([g * experts + (start + j) % experts for j in range(NEAR)])
    return lists


def pack_kernel(layer_ref, grad_ref, ids_ref, probs_ref, out_ref, ids_vmem, sems):
    width = layer_ref.shape[1]
    copies = [
        pltpu.make_async_copy(ids_ref, ids_vmem, sems.at[0]),
        pltpu.make_async_copy(layer_ref, out_ref.at[:, :width], sems.at[1]),
        pltpu.make_async_copy(grad_ref, out_ref.at[:, width : 2 * width], sems.at[2]),
    ]
    for copy in copies:
        copy.start()
    choice, lane = iota((TOP, LANES), 0), iota((TOP, LANES), 1)
    ids_lane = jnp.where(lane == choice, 1.0, 0.0).astype(BF16)
    probs_lane = jnp.where(lane == choice + TOP, 1.0, 0.0).astype(BF16)
    copies[0].wait()
    ids = ids_vmem[...].astype(F32).astype(BF16)
    extras = dot(ids, ids_lane, ((0,), (0,))) + dot(probs_ref[...], probs_lane, ((0,), (0,)))
    out_ref[:, 2 * width :] = extras.astype(BF16)
    copies[1].wait()
    copies[2].wait()


def select_kernel(base_ref, tok_ref, send_ref, pick_ref):
    tokens = tok_ref.shape[0]
    slots = send_ref.shape[0]
    width = send_ref.shape[1] // 2
    block = tokens // FAR
    extras = tok_ref[:, 2 * width :].astype(F32)
    lane = iota((tokens, LANES), 1)
    expert_lane = served(lane, base_ref[0])
    member = jnp.zeros((tokens, LANES), F32)
    prob = jnp.zeros((tokens, LANES), F32)
    for k in range(TOP):
        hit = extras[:, k : k + 1] == expert_lane
        member = jnp.where(hit, 1.0, member)
        prob = jnp.where(hit, extras[:, TOP + k : TOP + k + 1], prob)
    row, col = iota((tokens, tokens), 0), iota((tokens, tokens), 1)
    shift = block.bit_length() - 1
    same = lax.shift_right_logical(row, shift) == lax.shift_right_logical(col, shift)
    earlier = jnp.where(same & (col < row), 1.0, 0.0).astype(BF16)
    rank = dot(earlier, member.astype(BF16))
    code = jnp.where(member > 0.0, rank, -1.0).astype(BF16)
    eye = jnp.where(row == col, 1.0, 0.0).astype(BF16)
    code_t = dot(code, eye, ((0,), (0,))).astype(BF16)
    prob_t = dot(prob.astype(BF16), eye, ((0,), (0,))).astype(BF16)

    expert, home, place = slot_parts(iota((slots, LANES), 0))
    spread = jnp.where(iota((slots, LANES), 1) == expert, 1.0, 0.0).astype(BF16)
    code_row = dot(spread, code_t)
    token_block = lax.shift_right_logical(iota((slots, tokens), 1), shift)
    chosen = (code_row == place.astype(F32)) & (token_block == home)
    select = jnp.where(chosen, 1.0, 0.0).astype(BF16)
    prob_row = jnp.sum(jnp.where(chosen, dot(spread, prob_t), 0.0), axis=1, keepdims=True)
    send_ref[:, :width] = dot(select, tok_ref[:, :width]).astype(BF16)
    grads = dot(select, tok_ref[:, width : 2 * width])
    send_ref[:, width:] = (prob_row * grads).astype(BF16)

    expert, home, place = slot_parts(iota((LANES, slots), 1))
    spread = jnp.where(iota((LANES, slots), 0) == expert, 1.0, 0.0).astype(BF16)
    code_col = dot(code, spread)
    token_block = lax.shift_right_logical(iota((tokens, slots), 0), shift)
    chosen = (code_col == place.astype(F32)) & (token_block == home)
    pick_ref[...] = jnp.where(chosen, 1.0, 0.0).astype(BF16)


def expert_kernel(rows_ref, gate_ref, up_ref, down_ref, ret_ref, both_ref, hidden_ref):
    width, hidden_width = gate_ref.shape
    scaled = rows_ref[:, width:]
    rows = rows_ref[:, :width]
    gate, up, down = gate_ref[...], up_ref[...], down_ref[...]
    pre_gate = dot(rows, gate)
    pre_up = dot(rows, up)
    grad_hidden = dot(scaled, down, ((1,), (1,)))
    sig = jax.nn.sigmoid(pre_gate)
    silu = pre_gate * sig
    hidden = (silu * pre_up).astype(BF16)
    prob_grad = jnp.sum(hidden.astype(F32) * grad_hidden, axis=1, keepdims=True)
    gate_grad = (grad_hidden * pre_up * sig * (1.0 + pre_gate * (1.0 - sig))).astype(BF16)
    up_grad = (grad_hidden * silu).astype(BF16)
    back = dot(gate_grad, gate, ((1,), (1,))) + dot(up_grad, up, ((1,), (1,)))
    ret_ref[:, :width] = back.astype(BF16)
    ret_ref[:, width:] = jnp.broadcast_to(prob_grad, (rows.shape[0], LANES)).astype(BF16)
    both_ref[:, :hidden_width] = gate_grad
    both_ref[:, hidden_width:] = up_grad
    hidden_ref[...] = hidden


def part_kernel(core_ref, rows_hbm, both_ref, hidden_ref, keep_hbm, give_hbm, rows, keep, give, in_sems, out_sems):
    chips, part_rows, columns = keep.shape
    hidden_width = hidden_ref.shape[1]
    width = rows.shape[1] // 2
    share = width // (2 * chips)
    down_share = hidden_width // (2 * chips)
    half = width // 2
    first = core_ref[0] == 0

    spans = [(width + side * half, half) for side in range(2)]
    spans += [(chip * 2 * share, 2 * share) for chip in range(chips)]
    loads = [
        pltpu.make_async_copy(rows_hbm.at[:, pl.ds(*span)], rows.at[:, pl.ds(*span)], in_sems.at[i])
        for i, span in enumerate(spans)
    ]
    for load in loads:
        load.start()

    def put(chip, low, pair):
        size = pair.shape[0] // 2
        keep[chip, low : low + size, :] = jnp.where(first, pair[:size], pair[size:]).astype(BF16)
        give[chip, low : low + size, :] = jnp.where(first, pair[size:], pair[:size]).astype(BF16)

    hidden = hidden_ref[...]
    for side in range(2):
        loads[side].wait()
        part = dot(hidden, rows[:, width + side * half : width + (side + 1) * half], ((0,), (0,)))
        for chip in range(chips):
            put(chip, share + side * down_share, part[chip * 2 * down_share : (chip + 1) * 2 * down_share])
    both = both_ref[...]
    stores = []
    for chip in range(chips):
        loads[2 + chip].wait()
        put(chip, 0, dot(rows[:, chip * 2 * share : (chip + 1) * 2 * share], both, ((0,), (0,))))
        stores.append(pltpu.make_async_copy(give.at[chip], give_hbm.at[chip], out_sems.at[2 * chip]))
        stores.append(pltpu.make_async_copy(keep.at[chip], keep_hbm.at[chip], out_sems.at[2 * chip + 1]))
        stores[-2].start()
        stores[-1].start()
    for store in stores:
        store.wait()


def chip_sum_kernel(chip_ref, keep_hbm, got_hbm, *refs):
    out_refs, (keep, got, sems) = refs[:-3], refs[-3:]
    chips = keep.shape[0]
    order = (2, 1, 3, 0)
    loads = []
    for s in order:
        chip = (chip_ref[0] + s) & (chips - 1)
        loads.append(pltpu.make_async_copy(keep_hbm.at[chip], keep.at[s], sems.at[2 * s]))
        loads.append(pltpu.make_async_copy(got_hbm.at[chip], got.at[s], sems.at[2 * s + 1]))
    for load in loads:
        load.start()
    for i, s in enumerate(order):
        loads[2 * i].wait()
        loads[2 * i + 1].wait()
        out_refs[s][...] = (keep[s].astype(F32) + got[s].astype(F32)).astype(BF16)


def combine_kernel(base_ref, back_ref, pick_ref, extra_ref, sum_ref):
    slots = back_ref.shape[0]
    width = back_ref.shape[1] - LANES
    tokens = sum_ref.shape[0]
    pick = pick_ref[...]
    sum_ref[:, :width] = dot(pick, back_ref[:, :width]).astype(BF16)
    expert, _, _ = slot_parts(iota((slots, LANES), 0))
    own = iota((slots, LANES), 1) == expert
    spread = jnp.where(own, back_ref[:, width:].astype(F32), 0.0).astype(BF16)
    by_expert = dot(pick, spread)
    extras = extra_ref[...].astype(F32)
    lane = iota((tokens, LANES), 1)
    expert_lane = served(lane, base_ref[0])
    result = jnp.zeros((tokens, LANES), F32)
    for k in range(TOP):
        hit = extras[:, k : k + 1] == expert_lane
        value = jnp.sum(jnp.where(hit, by_expert, 0.0), axis=1, keepdims=True)
        value = value / extras[:, TOP + k : TOP + k + 1]
        result = jnp.where(lane == k, value, result)
    sum_ref[:, width:] = result.astype(BF16)


def finish_kernel(sums_ref, in_ref, prob_ref):
    width = in_ref.shape[1]
    total = sums_ref[0].astype(F32)
    for s in range(1, FAR):
        total = total + sums_ref[s].astype(F32)
    in_ref[...] = total[:, :width].astype(BF16)
    pick = jnp.where(iota((TOP, LANES), 0) == iota((TOP, LANES), 1), 1.0, 0.0).astype(BF16)
    prob_ref[...] = dot(pick, total[:, width:].astype(BF16), ((1,), (1,))).astype(BF16)


def weight_sum_kernel(*refs):
    part_refs, (gate_ref, up_ref, down_ref) = refs[:-3], refs[-3:]
    share, hidden_width = gate_ref.shape
    down_share, width = down_ref.shape
    half = width // 2

    def part(low, size):
        result = part_refs[0][low : low + size, :].astype(F32)
        for ref in part_refs[1:]:
            result = result + ref[low : low + size, :].astype(F32)
        return result

    gate_up = part(0, share)
    gate_ref[...] = gate_up[:, :hidden_width]
    up_ref[...] = gate_up[:, hidden_width:]
    down_ref[:, :half] = part(share, down_share)
    down_ref[:, half:] = part(share + down_share, down_share)


def params(mib):
    return pltpu.CompilerParams(vmem_limit_bytes=mib * MIB)


def cost(flops, nbytes):
    return pl.CostEstimate(flops=flops, bytes_accessed=nbytes, transcendentals=0)


def per_device(layer_in, grad_out, expert_ids, gate_probs, gate_weight, up_weight, down_weight):
    block, width = layer_in.shape
    hidden_width = gate_weight.shape[2]
    chips = lax.axis_size("x")
    groups = 2 * chips
    tokens = FAR * block
    slots = NEAR * FAR * CAP
    share = width // groups
    down_share = hidden_width // groups
    part_rows = share + 2 * down_share
    core = lax.axis_index("core").astype(jnp.int32)
    chip = lax.axis_index("x").astype(jnp.int32)
    moved = core * (NEAR // 2)
    place = lax.axis_index(("far", "near", "y")) - moved + EXPERTS
    base = ((place & -NEAR) + moved).astype(jnp.int32).reshape(1)
    scalar = pl.BlockSpec(memory_space=pltpu.SMEM)
    hbm = pl.BlockSpec(memory_space=pltpu.HBM)

    def shape(*dims):
        return jax.ShapeDtypeStruct(dims, BF16)

    packed = pl.pallas_call(
        pack_kernel,
        out_shape=shape(block, 2 * width + LANES),
        in_specs=[hbm] * 3 + whole(1),
        out_specs=whole(1)[0],
        scratch_shapes=[pltpu.VMEM((TOP, block), jnp.int32), pltpu.SemaphoreType.DMA((3,))],
        compiler_params=params(60),
        name="pack_tokens",
    )(layer_in, grad_out, expert_ids.T, gate_probs.T)
    near_tokens = lax.all_gather(packed, "far", tiled=True)

    send, pick = pl.pallas_call(
        select_kernel,
        out_shape=(shape(slots, 2 * width), shape(tokens, slots)),
        in_specs=[scalar] + whole(1),
        out_specs=tuple(whole(2)),
        compiler_params=params(24),
        name="select_rows",
    )(base, near_tokens)

    exchange = functools.partial(lax.all_to_all, split_axis=0, concat_axis=0, tiled=True)
    near_exchange = functools.partial(
        exchange,
        axis_name=("x", "core", "far", "near", "y"),
        axis_index_groups=windows(groups, EXPERTS),
    )
    rows = near_exchange(send.reshape(NEAR, FAR * CAP, 2 * width)).reshape(slots, 2 * width)

    matmul = 2 * slots * width * hidden_width
    back, both, hidden = pl.pallas_call(
        expert_kernel,
        out_shape=(shape(slots, width + LANES), shape(slots, 2 * hidden_width), shape(slots, hidden_width)),
        in_specs=whole(4),
        out_specs=tuple(whole(3)),
        compiler_params=params(32),
        cost_estimate=cost(5 * matmul, 8 * MIB),
        name="expert_rows",
    )(rows, gate_weight[0], up_weight[0], down_weight[0])
    back = near_exchange(back.reshape(NEAR, FAR * CAP, width + LANES)).reshape(slots, width + LANES)

    keep, give = pl.pallas_call(
        part_kernel,
        out_shape=(shape(chips, part_rows, 2 * hidden_width),) * 2,
        in_specs=[scalar, hbm] + whole(2),
        out_specs=(hbm, hbm),
        scratch_shapes=[
            pltpu.VMEM((slots, 2 * width), BF16),
            pltpu.VMEM((chips, part_rows, 2 * hidden_width), BF16),
            pltpu.VMEM((chips, part_rows, 2 * hidden_width), BF16),
            pltpu.SemaphoreType.DMA((chips + 2,)),
            pltpu.SemaphoreType.DMA((2 * chips,)),
        ],
        compiler_params=params(52),
        cost_estimate=cost(3 * matmul, 8 * MIB),
        name="weight_parts",
    )(core.reshape(1), rows, both, hidden)
    got = lax.ppermute(give, "core", [(0, 1), (1, 0)])
    chip_sums = pl.pallas_call(
        chip_sum_kernel,
        out_shape=(shape(part_rows, 2 * hidden_width),) * chips,
        in_specs=[scalar, hbm, hbm],
        out_specs=tuple(whole(chips)),
        scratch_shapes=[
            pltpu.VMEM((chips, part_rows, 2 * hidden_width), BF16),
            pltpu.VMEM((chips, part_rows, 2 * hidden_width), BF16),
            pltpu.SemaphoreType.DMA((2 * chips,)),
        ],
        compiler_params=params(52),
        cost_estimate=cost(MIB, 6 * MIB),
        name="chip_sums",
    )(chip.reshape(1), keep, got)
    parts = [
        lax.ppermute(chip_sums[s], "x", [(i, (i + s) % chips) for i in range(chips)]) for s in (2, 1, 3)
    ] + [chip_sums[0]]

    back, _ = lax.optimization_barrier((back, chip_sums[0]))
    sums = pl.pallas_call(
        combine_kernel,
        out_shape=shape(tokens, width + LANES),
        in_specs=[scalar] + whole(3),
        out_specs=whole(1)[0],
        compiler_params=params(24),
        name="combine_rows",
    )(base, back, pick, near_tokens[:, 2 * width :])
    sums = exchange(sums.reshape(FAR, block, width + LANES), "far")

    grad_gate, grad_up, grad_down = pl.pallas_call(
        weight_sum_kernel,
        out_shape=(
            jax.ShapeDtypeStruct((share, hidden_width), F32),
            jax.ShapeDtypeStruct((share, hidden_width), F32),
            jax.ShapeDtypeStruct((down_share, width), F32),
        ),
        in_specs=whole(chips),
        out_specs=tuple(whole(3)),
        compiler_params=params(24),
        cost_estimate=cost(PLACING_FLOPS, 3 * MIB),
        name="weight_sums",
    )(*parts)
    grad_in, grad_probs = pl.pallas_call(
        finish_kernel,
        out_shape=(shape(block, width), shape(TOP, block)),
        in_specs=whole(1),
        out_specs=tuple(whole(2)),
        compiler_params=params(24),
        name="finish",
    )(sums)
    return grad_in, grad_probs.T, grad_gate[None], grad_up[None], grad_down[None]


def solution(mesh):
    groups, experts = mesh.devices.shape
    split = Mesh(
        mesh.devices.reshape(groups // 2, 2, FAR, 4, experts // NEAR), ("x", "core", "far", "near", "y")
    )
    expert = ("far", "near", "y")
    token_spec = P(("x", "core") + expert, None)
    weight_spec = P(expert, None, None)
    grad_spec = P(expert, ("x", "core"), None)
    return jax.shard_map(
        per_device,
        mesh=split,
        in_specs=(token_spec,) * 4 + (weight_spec,) * 3,
        out_specs=(token_spec,) * 2 + (grad_spec,) * 3,
        check_vma=False,
    )
```

```python
import functools

import jax
import jax.numpy as jnp
from jax import lax
from jax.experimental import pallas as pl
from jax.experimental.pallas import tpu as pltpu
from jax.sharding import Mesh, PartitionSpec as P

F32 = jnp.float32
BF16 = jnp.bfloat16
LANES = 128
CAP = 6
FAR = 4
NEAR = 16
TOP = 8
EXPERTS = 64
MIB = 1 << 20


def iota(shape, dim):
    return lax.broadcasted_iota(jnp.int32, shape, dim)


def dot(a, b, contract=((1,), (0,))):
    return lax.dot_general(a, b, (contract, ((), ())), preferred_element_type=F32)


def whole(n):
    return [pl.BlockSpec(memory_space=pltpu.VMEM)] * n


def slot_parts(i):
    sixth = lax.shift_right_logical(i * 10923, 16)
    expert = lax.shift_right_logical(i * 2731, 16)
    return expert, sixth - FAR * expert, i - CAP * sixth


def served(lane, base):
    return jnp.where(lane < NEAR, (lane + base) & (EXPERTS - 1), -1).astype(F32)


def windows(groups, experts):
    lists = []
    for g in range(groups):
        for far in range(FAR):
            start = far * NEAR + (g % 2) * (NEAR // 2)
            lists.append([g * experts + (start + j) % experts for j in range(NEAR)])
    return lists


def pack_kernel(layer_ref, grad_ref, ids_ref, probs_ref, out_ref, ids_vmem, sems):
    width = layer_ref.shape[1]
    copies = [
        pltpu.make_async_copy(ids_ref, ids_vmem, sems.at[0]),
        pltpu.make_async_copy(layer_ref, out_ref.at[:, :width], sems.at[1]),
        pltpu.make_async_copy(grad_ref, out_ref.at[:, width : 2 * width], sems.at[2]),
    ]
    for copy in copies:
        copy.start()
    choice, lane = iota((TOP, LANES), 0), iota((TOP, LANES), 1)
    ids_lane = jnp.where(lane == choice, 1.0, 0.0).astype(BF16)
    probs_lane = jnp.where(lane == choice + TOP, 1.0, 0.0).astype(BF16)
    copies[0].wait()
    ids = ids_vmem[...].astype(F32).astype(BF16)
    extras = dot(ids, ids_lane, ((0,), (0,))) + dot(probs_ref[...], probs_lane, ((0,), (0,)))
    out_ref[:, 2 * width :] = extras.astype(BF16)
    copies[1].wait()
    copies[2].wait()


def select_kernel(base_ref, tok_ref, send_ref, pick_ref):
    tokens = tok_ref.shape[0]
    slots = send_ref.shape[0]
    width = send_ref.shape[1] // 2
    block = tokens // FAR
    extras = tok_ref[:, 2 * width :].astype(F32)
    lane = iota((tokens, LANES), 1)
    expert_lane = served(lane, base_ref[0])
    member = jnp.zeros((tokens, LANES), F32)
    prob = jnp.zeros((tokens, LANES), F32)
    for k in range(TOP):
        hit = extras[:, k : k + 1] == expert_lane
        member = jnp.where(hit, 1.0, member)
        prob = jnp.where(hit, extras[:, TOP + k : TOP + k + 1], prob)
    row, col = iota((tokens, tokens), 0), iota((tokens, tokens), 1)
    shift = block.bit_length() - 1
    same = lax.shift_right_logical(row, shift) == lax.shift_right_logical(col, shift)
    earlier = jnp.where(same & (col < row), 1.0, 0.0).astype(BF16)
    rank = dot(earlier, member.astype(BF16))
    code = jnp.where(member > 0.0, rank, -1.0).astype(BF16)
    eye = jnp.where(row == col, 1.0, 0.0).astype(BF16)
    code_t = dot(code, eye, ((0,), (0,))).astype(BF16)
    prob_t = dot(prob.astype(BF16), eye, ((0,), (0,))).astype(BF16)

    expert, home, place = slot_parts(iota((slots, LANES), 0))
    spread = jnp.where(iota((slots, LANES), 1) == expert, 1.0, 0.0).astype(BF16)
    code_row = dot(spread, code_t)
    token_block = lax.shift_right_logical(iota((slots, tokens), 1), shift)
    chosen = (code_row == place.astype(F32)) & (token_block == home)
    select = jnp.where(chosen, 1.0, 0.0).astype(BF16)
    prob_row = jnp.sum(jnp.where(chosen, dot(spread, prob_t), 0.0), axis=1, keepdims=True)
    send_ref[:, :width] = dot(select, tok_ref[:, :width]).astype(BF16)
    grads = dot(select, tok_ref[:, width : 2 * width])
    send_ref[:, width:] = (prob_row * grads).astype(BF16)

    expert, home, place = slot_parts(iota((LANES, slots), 1))
    spread = jnp.where(iota((LANES, slots), 0) == expert, 1.0, 0.0).astype(BF16)
    code_col = dot(code, spread)
    token_block = lax.shift_right_logical(iota((tokens, slots), 0), shift)
    chosen = (code_col == place.astype(F32)) & (token_block == home)
    pick_ref[...] = jnp.where(chosen, 1.0, 0.0).astype(BF16)


def expert_kernel(rows_ref, gate_ref, up_ref, down_ref, ret_ref, both_ref, hidden_ref):
    width, hidden_width = gate_ref.shape
    scaled = rows_ref[:, width:]
    rows = rows_ref[:, :width]
    gate, up, down = gate_ref[...], up_ref[...], down_ref[...]
    pre_gate = dot(rows, gate)
    pre_up = dot(rows, up)
    grad_hidden = dot(scaled, down, ((1,), (1,)))
    sig = jax.nn.sigmoid(pre_gate)
    silu = pre_gate * sig
    hidden = (silu * pre_up).astype(BF16)
    prob_grad = jnp.sum(hidden.astype(F32) * grad_hidden, axis=1, keepdims=True)
    gate_grad = (grad_hidden * pre_up * sig * (1.0 + pre_gate * (1.0 - sig))).astype(BF16)
    up_grad = (grad_hidden * silu).astype(BF16)
    back = dot(gate_grad, gate, ((1,), (1,))) + dot(up_grad, up, ((1,), (1,)))
    ret_ref[:, :width] = back.astype(BF16)
    ret_ref[:, width:] = jnp.broadcast_to(prob_grad, (rows.shape[0], LANES)).astype(BF16)
    both_ref[:, :hidden_width] = gate_grad
    both_ref[:, hidden_width:] = up_grad
    hidden_ref[...] = hidden


def part_kernel(core_ref, rows_hbm, both_ref, hidden_ref, keep_hbm, give_hbm, rows, keep, give, in_sems, out_sems):
    chips, part_rows, columns = keep.shape
    hidden_width = hidden_ref.shape[1]
    width = rows.shape[1] // 2
    share = width // (2 * chips)
    down_share = hidden_width // (2 * chips)
    half = width // 2
    first = core_ref[0] == 0

    spans = [(width + side * half, half) for side in range(2)]
    spans += [(chip * 2 * share, 2 * share) for chip in range(chips)]
    loads = [
        pltpu.make_async_copy(rows_hbm.at[:, pl.ds(*span)], rows.at[:, pl.ds(*span)], in_sems.at[i])
        for i, span in enumerate(spans)
    ]
    for load in loads:
        load.start()

    def put(chip, low, pair):
        size = pair.shape[0] // 2
        keep[chip, low : low + size, :] = jnp.where(first, pair[:size], pair[size:]).astype(BF16)
        give[chip, low : low + size, :] = jnp.where(first, pair[size:], pair[:size]).astype(BF16)

    hidden = hidden_ref[...]
    for side in range(2):
        loads[side].wait()
        part = dot(hidden, rows[:, width + side * half : width + (side + 1) * half], ((0,), (0,)))
        for chip in range(chips):
            put(chip, share + side * down_share, part[chip * 2 * down_share : (chip + 1) * 2 * down_share])
    both = both_ref[...]
    stores = []
    for chip in range(chips):
        loads[2 + chip].wait()
        put(chip, 0, dot(rows[:, chip * 2 * share : (chip + 1) * 2 * share], both, ((0,), (0,))))
        stores.append(pltpu.make_async_copy(give.at[chip], give_hbm.at[chip], out_sems.at[2 * chip]))
        stores.append(pltpu.make_async_copy(keep.at[chip], keep_hbm.at[chip], out_sems.at[2 * chip + 1]))
        stores[-2].start()
        stores[-1].start()
    for store in stores:
        store.wait()


def chip_sum_kernel(chip_ref, keep_hbm, got_hbm, *refs):
    out_refs, (keep, got, sems) = refs[:-3], refs[-3:]
    chips = keep.shape[0]
    order = (2, 1, 3, 0)
    loads = []
    for s in order:
        chip = (chip_ref[0] + s) & (chips - 1)
        loads.append(pltpu.make_async_copy(keep_hbm.at[chip], keep.at[s], sems.at[2 * s]))
        loads.append(pltpu.make_async_copy(got_hbm.at[chip], got.at[s], sems.at[2 * s + 1]))
    for load in loads:
        load.start()
    for i, s in enumerate(order):
        loads[2 * i].wait()
        loads[2 * i + 1].wait()
        out_refs[s][...] = (keep[s].astype(F32) + got[s].astype(F32)).astype(BF16)


def combine_kernel(base_ref, back_ref, pick_ref, extra_ref, sum_ref):
    slots = back_ref.shape[0]
    width = back_ref.shape[1] - LANES
    tokens = sum_ref.shape[0]
    pick = pick_ref[...]
    sum_ref[:, :width] = dot(pick, back_ref[:, :width]).astype(BF16)
    expert, _, _ = slot_parts(iota((slots, LANES), 0))
    own = iota((slots, LANES), 1) == expert
    spread = jnp.where(own, back_ref[:, width:].astype(F32), 0.0).astype(BF16)
    by_expert = dot(pick, spread)
    extras = extra_ref[...].astype(F32)
    lane = iota((tokens, LANES), 1)
    expert_lane = served(lane, base_ref[0])
    result = jnp.zeros((tokens, LANES), F32)
    for k in range(TOP):
        hit = extras[:, k : k + 1] == expert_lane
        value = jnp.sum(jnp.where(hit, by_expert, 0.0), axis=1, keepdims=True)
        value = value / extras[:, TOP + k : TOP + k + 1]
        result = jnp.where(lane == k, value, result)
    sum_ref[:, width:] = result.astype(BF16)


def finish_kernel(sums_ref, in_ref, prob_ref):
    width = in_ref.shape[1]
    total = sums_ref[0].astype(F32)
    for s in range(1, FAR):
        total = total + sums_ref[s].astype(F32)
    in_ref[...] = total[:, :width].astype(BF16)
    pick = jnp.where(iota((TOP, LANES), 0) == iota((TOP, LANES), 1), 1.0, 0.0).astype(BF16)
    prob_ref[...] = dot(pick, total[:, width:].astype(BF16), ((1,), (1,))).astype(BF16)


def weight_sum_kernel(*refs):
    part_refs, (gate_ref, up_ref, down_ref) = refs[:-3], refs[-3:]
    share, hidden_width = gate_ref.shape
    down_share, width = down_ref.shape
    half = width // 2

    def part(low, size):
        result = part_refs[0][low : low + size, :].astype(F32)
        for ref in part_refs[1:]:
            result = result + ref[low : low + size, :].astype(F32)
        return result

    gate_up = part(0, share)
    gate_ref[...] = gate_up[:, :hidden_width]
    up_ref[...] = gate_up[:, hidden_width:]
    down_ref[:, :half] = part(share, down_share)
    down_ref[:, half:] = part(share + down_share, down_share)


def params(mib):
    return pltpu.CompilerParams(vmem_limit_bytes=mib * MIB)


def cost(flops, nbytes):
    return pl.CostEstimate(flops=flops, bytes_accessed=nbytes, transcendentals=0)


def per_device(layer_in, grad_out, expert_ids, gate_probs, gate_weight, up_weight, down_weight):
    block, width = layer_in.shape
    hidden_width = gate_weight.shape[2]
    chips = lax.axis_size("x")
    groups = 2 * chips
    tokens = FAR * block
    slots = NEAR * FAR * CAP
    share = width // groups
    down_share = hidden_width // groups
    part_rows = share + 2 * down_share
    core = lax.axis_index("core").astype(jnp.int32)
    chip = lax.axis_index("x").astype(jnp.int32)
    moved = core * (NEAR // 2)
    place = lax.axis_index(("far", "near", "y")) - moved + EXPERTS
    base = ((place & -NEAR) + moved).astype(jnp.int32).reshape(1)
    scalar = pl.BlockSpec(memory_space=pltpu.SMEM)
    hbm = pl.BlockSpec(memory_space=pltpu.HBM)

    def shape(*dims):
        return jax.ShapeDtypeStruct(dims, BF16)

    packed = pl.pallas_call(
        pack_kernel,
        out_shape=pltpu.VMEM((block, 2 * width + LANES), BF16),
        in_specs=[hbm] * 3 + whole(1),
        out_specs=whole(1)[0],
        scratch_shapes=[pltpu.VMEM((TOP, block), jnp.int32), pltpu.SemaphoreType.DMA((3,))],
        compiler_params=params(60),
        name="pack_tokens",
    )(layer_in, grad_out, expert_ids.T, gate_probs.T)
    near_tokens = lax.all_gather(packed, "far", tiled=True)

    send, pick = pl.pallas_call(
        select_kernel,
        out_shape=(shape(slots, 2 * width), shape(tokens, slots)),
        in_specs=[scalar] + whole(1),
        out_specs=tuple(whole(2)),
        compiler_params=params(24),
        name="select_rows",
    )(base, near_tokens)

    exchange = functools.partial(lax.all_to_all, split_axis=0, concat_axis=0, tiled=True)
    near_exchange = functools.partial(
        exchange,
        axis_name=("x", "core", "far", "near", "y"),
        axis_index_groups=windows(groups, EXPERTS),
    )
    rows = near_exchange(send.reshape(NEAR, FAR * CAP, 2 * width)).reshape(slots, 2 * width)

    matmul = 2 * slots * width * hidden_width
    back, both, hidden = pl.pallas_call(
        expert_kernel,
        out_shape=(shape(slots, width + LANES), shape(slots, 2 * hidden_width), shape(slots, hidden_width)),
        in_specs=whole(4),
        out_specs=tuple(whole(3)),
        compiler_params=params(32),
        cost_estimate=cost(5 * matmul, 8 * MIB),
        name="expert_rows",
    )(rows, gate_weight[0], up_weight[0], down_weight[0])
    back = near_exchange(back.reshape(NEAR, FAR * CAP, width + LANES)).reshape(slots, width + LANES)

    keep, give = pl.pallas_call(
        part_kernel,
        out_shape=(shape(chips, part_rows, 2 * hidden_width),) * 2,
        in_specs=[scalar, hbm] + whole(2),
        out_specs=(hbm, hbm),
        scratch_shapes=[
            pltpu.VMEM((slots, 2 * width), BF16),
            pltpu.VMEM((chips, part_rows, 2 * hidden_width), BF16),
            pltpu.VMEM((chips, part_rows, 2 * hidden_width), BF16),
            pltpu.SemaphoreType.DMA((chips + 2,)),
            pltpu.SemaphoreType.DMA((2 * chips,)),
        ],
        compiler_params=params(52),
        cost_estimate=cost(3 * matmul, 8 * MIB),
        name="weight_parts",
    )(core.reshape(1), rows, both, hidden)
    got = lax.ppermute(give, "core", [(0, 1), (1, 0)])
    chip_sums = pl.pallas_call(
        chip_sum_kernel,
        out_shape=(shape(part_rows, 2 * hidden_width),) * chips,
        in_specs=[scalar, hbm, hbm],
        out_specs=tuple(whole(chips)),
        scratch_shapes=[
            pltpu.VMEM((chips, part_rows, 2 * hidden_width), BF16),
            pltpu.VMEM((chips, part_rows, 2 * hidden_width), BF16),
            pltpu.SemaphoreType.DMA((2 * chips,)),
        ],
        compiler_params=params(52),
        cost_estimate=cost(MIB, 6 * MIB),
        name="chip_sums",
    )(chip.reshape(1), keep, got)
    parts = [
        lax.ppermute(chip_sums[s], "x", [(i, (i + s) % chips) for i in range(chips)]) for s in (2, 1, 3)
    ] + [chip_sums[0]]

    back, _ = lax.optimization_barrier((back, chip_sums[0]))
    sums = pl.pallas_call(
        combine_kernel,
        out_shape=shape(tokens, width + LANES),
        in_specs=[scalar] + whole(3),
        out_specs=whole(1)[0],
        compiler_params=params(24),
        name="combine_rows",
    )(base, back, pick, near_tokens[:, 2 * width :])
    sums = exchange(sums.reshape(FAR, block, width + LANES), "far")

    grad_gate, grad_up, grad_down = pl.pallas_call(
        weight_sum_kernel,
        out_shape=(
            jax.ShapeDtypeStruct((share, hidden_width), F32),
            jax.ShapeDtypeStruct((share, hidden_width), F32),
            jax.ShapeDtypeStruct((down_share, width), F32),
        ),
        in_specs=whole(chips),
        out_specs=tuple(whole(3)),
        compiler_params=params(24),
        cost_estimate=cost(MIB, 3 * MIB),
        name="weight_sums",
    )(*parts)
    grad_in, grad_probs = pl.pallas_call(
        finish_kernel,
        out_shape=(shape(block, width), shape(TOP, block)),
        in_specs=whole(1),
        out_specs=tuple(whole(2)),
        compiler_params=params(24),
        name="finish",
    )(sums)
    return grad_in, grad_probs.T, grad_gate[None], grad_up[None], grad_down[None]


def solution(mesh):
    groups, experts = mesh.devices.shape
    split = Mesh(
        mesh.devices.reshape(groups // 2, 2, FAR, 4, experts // NEAR), ("x", "core", "far", "near", "y")
    )
    expert = ("far", "near", "y")
    token_spec = P(("x", "core") + expert, None)
    weight_spec = P(expert, None, None)
    grad_spec = P(expert, ("x", "core"), None)
    return jax.shard_map(
        per_device,
        mesh=split,
        in_specs=(token_spec,) * 4 + (weight_spec,) * 3,
        out_specs=(token_spec,) * 2 + (grad_spec,) * 3,
        check_vma=False,
    )
```

```python
import functools

import jax
import jax.numpy as jnp
from jax import lax
from jax.experimental import pallas as pl
from jax.experimental.pallas import tpu as pltpu
from jax.sharding import Mesh, PartitionSpec as P

F32 = jnp.float32
BF16 = jnp.bfloat16
LANES = 128
CAP = 6
FAR = 4
NEAR = 16
TOP = 8
EXPERTS = 64
MIB = 1 << 20


def iota(shape, dim):
    return lax.broadcasted_iota(jnp.int32, shape, dim)


def dot(a, b, contract=((1,), (0,))):
    return lax.dot_general(a, b, (contract, ((), ())), preferred_element_type=F32)


def whole(n):
    return [pl.BlockSpec(memory_space=pltpu.VMEM)] * n


def slot_parts(i):
    sixth = lax.shift_right_logical(i * 10923, 16)
    expert = lax.shift_right_logical(i * 2731, 16)
    return expert, sixth - FAR * expert, i - CAP * sixth


def served(lane, base):
    return jnp.where(lane < NEAR, (lane + base) & (EXPERTS - 1), -1).astype(F32)


def windows(groups, experts):
    lists = []
    for g in range(groups):
        for far in range(FAR):
            start = far * NEAR + (g % 2) * (NEAR // 2)
            lists.append([g * experts + (start + j) % experts for j in range(NEAR)])
    return lists


def pack_kernel(layer_ref, grad_ref, ids_ref, probs_ref, out_ref, ids_vmem, sems):
    width = layer_ref.shape[1]
    copies = [
        pltpu.make_async_copy(ids_ref, ids_vmem, sems.at[0]),
        pltpu.make_async_copy(layer_ref, out_ref.at[:, :width], sems.at[1]),
        pltpu.make_async_copy(grad_ref, out_ref.at[:, width : 2 * width], sems.at[2]),
    ]
    for copy in copies:
        copy.start()
    choice, lane = iota((TOP, LANES), 0), iota((TOP, LANES), 1)
    ids_lane = jnp.where(lane == choice, 1.0, 0.0).astype(BF16)
    probs_lane = jnp.where(lane == choice + TOP, 1.0, 0.0).astype(BF16)
    copies[0].wait()
    ids = ids_vmem[...].astype(F32).astype(BF16)
    extras = dot(ids, ids_lane, ((0,), (0,))) + dot(probs_ref[...], probs_lane, ((0,), (0,)))
    out_ref[:, 2 * width :] = extras.astype(BF16)
    copies[1].wait()
    copies[2].wait()


def select_kernel(base_ref, tok_ref, send_ref, pick_ref):
    tokens = tok_ref.shape[0]
    slots = send_ref.shape[0]
    width = send_ref.shape[1] // 2
    block = tokens // FAR
    extras = tok_ref[:, 2 * width :].astype(F32)
    lane = iota((tokens, LANES), 1)
    expert_lane = served(lane, base_ref[0])
    member = jnp.zeros((tokens, LANES), F32)
    prob = jnp.zeros((tokens, LANES), F32)
    for k in range(TOP):
        hit = extras[:, k : k + 1] == expert_lane
        member = jnp.where(hit, 1.0, member)
        prob = jnp.where(hit, extras[:, TOP + k : TOP + k + 1], prob)
    row, col = iota((tokens, tokens), 0), iota((tokens, tokens), 1)
    shift = block.bit_length() - 1
    same = lax.shift_right_logical(row, shift) == lax.shift_right_logical(col, shift)
    earlier = jnp.where(same & (col < row), 1.0, 0.0).astype(BF16)
    rank = dot(earlier, member.astype(BF16))
    code = jnp.where(member > 0.0, rank, -1.0).astype(BF16)
    eye = jnp.where(row == col, 1.0, 0.0).astype(BF16)
    code_t = dot(code, eye, ((0,), (0,))).astype(BF16)
    prob_t = dot(prob.astype(BF16), eye, ((0,), (0,))).astype(BF16)

    expert, home, place = slot_parts(iota((slots, LANES), 0))
    spread = jnp.where(iota((slots, LANES), 1) == expert, 1.0, 0.0).astype(BF16)
    code_row = dot(spread, code_t)
    token_block = lax.shift_right_logical(iota((slots, tokens), 1), shift)
    chosen = (code_row == place.astype(F32)) & (token_block == home)
    select = jnp.where(chosen, 1.0, 0.0).astype(BF16)
    prob_row = jnp.sum(jnp.where(chosen, dot(spread, prob_t), 0.0), axis=1, keepdims=True)
    send_ref[:, :width] = dot(select, tok_ref[:, :width]).astype(BF16)
    grads = dot(select, tok_ref[:, width : 2 * width])
    send_ref[:, width:] = (prob_row * grads).astype(BF16)

    expert, home, place = slot_parts(iota((LANES, slots), 1))
    spread = jnp.where(iota((LANES, slots), 0) == expert, 1.0, 0.0).astype(BF16)
    code_col = dot(code, spread)
    token_block = lax.shift_right_logical(iota((tokens, slots), 0), shift)
    chosen = (code_col == place.astype(F32)) & (token_block == home)
    pick_ref[...] = jnp.where(chosen, 1.0, 0.0).astype(BF16)


def expert_kernel(rows_ref, gate_ref, up_ref, down_ref, ret_hbm, both_ref, hidden_ref, ret, sems):
    width, hidden_width = gate_ref.shape
    scaled = rows_ref[:, width:]
    rows = rows_ref[:, :width]
    gate, up, down = gate_ref[...], up_ref[...], down_ref[...]
    pre_gate = dot(rows, gate)
    pre_up = dot(rows, up)
    grad_hidden = dot(scaled, down, ((1,), (1,)))
    sig = jax.nn.sigmoid(pre_gate)
    silu = pre_gate * sig
    hidden = (silu * pre_up).astype(BF16)
    prob_grad = jnp.sum(hidden.astype(F32) * grad_hidden, axis=1, keepdims=True)
    gate_grad = (grad_hidden * pre_up * sig * (1.0 + pre_gate * (1.0 - sig))).astype(BF16)
    up_grad = (grad_hidden * silu).astype(BF16)
    ret[:, width:] = jnp.broadcast_to(prob_grad, (rows.shape[0], LANES)).astype(BF16)
    both_ref[:, :hidden_width] = gate_grad
    both_ref[:, hidden_width:] = up_grad
    hidden_ref[...] = hidden
    stores = []
    third = width // 3
    for i, low in enumerate((2 * third, third, 0)):
        span = slice(low, low + third)
        back = dot(gate_grad, gate_ref[span, :], ((1,), (1,))) + dot(up_grad, up_ref[span, :], ((1,), (1,)))
        ret[:, span] = back.astype(BF16)
        columns = pl.ds(low, third + LANES if i == 0 else third)
        stores.append(pltpu.make_async_copy(ret.at[:, columns], ret_hbm.at[:, columns], sems.at[i]))
        stores[-1].start()
    for store in stores:
        store.wait()


def part_kernel(core_ref, rows_hbm, both_ref, hidden_ref, keep_hbm, give_hbm, rows, keep, give, in_sems, out_sems):
    chips, part_rows, columns = keep.shape
    hidden_width = hidden_ref.shape[1]
    width = rows.shape[1] // 2
    share = width // (2 * chips)
    down_share = hidden_width // (2 * chips)
    half = width // 2
    first = core_ref[0] == 0

    spans = [(width + side * half, half) for side in range(2)]
    spans += [(chip * 2 * share, 2 * share) for chip in range(chips)]
    loads = [
        pltpu.make_async_copy(rows_hbm.at[:, pl.ds(*span)], rows.at[:, pl.ds(*span)], in_sems.at[i])
        for i, span in enumerate(spans)
    ]
    for load in loads:
        load.start()

    def put(chip, low, pair):
        size = pair.shape[0] // 2
        keep[chip, low : low + size, :] = jnp.where(first, pair[:size], pair[size:]).astype(BF16)
        give[chip, low : low + size, :] = jnp.where(first, pair[size:], pair[:size]).astype(BF16)

    hidden = hidden_ref[...]
    for side in range(2):
        loads[side].wait()
        part = dot(hidden, rows[:, width + side * half : width + (side + 1) * half], ((0,), (0,)))
        for chip in range(chips):
            put(chip, share + side * down_share, part[chip * 2 * down_share : (chip + 1) * 2 * down_share])
    both = both_ref[...]
    stores = []
    for chip in range(chips):
        loads[2 + chip].wait()
        put(chip, 0, dot(rows[:, chip * 2 * share : (chip + 1) * 2 * share], both, ((0,), (0,))))
        stores.append(pltpu.make_async_copy(give.at[chip], give_hbm.at[chip], out_sems.at[2 * chip]))
        stores.append(pltpu.make_async_copy(keep.at[chip], keep_hbm.at[chip], out_sems.at[2 * chip + 1]))
        stores[-2].start()
        stores[-1].start()
    for store in stores:
        store.wait()


def chip_sum_kernel(chip_ref, keep_hbm, got_hbm, *refs):
    out_refs, (keep, got, sems) = refs[:-3], refs[-3:]
    chips = keep.shape[0]
    order = (2, 1, 3, 0)
    loads = []
    for s in order:
        chip = (chip_ref[0] + s) & (chips - 1)
        loads.append(pltpu.make_async_copy(keep_hbm.at[chip], keep.at[s], sems.at[2 * s]))
        loads.append(pltpu.make_async_copy(got_hbm.at[chip], got.at[s], sems.at[2 * s + 1]))
    for load in loads:
        load.start()
    for i, s in enumerate(order):
        loads[2 * i].wait()
        loads[2 * i + 1].wait()
        out_refs[s][...] = (keep[s].astype(F32) + got[s].astype(F32)).astype(BF16)


def combine_kernel(base_ref, back_ref, pick_ref, extra_ref, sum_ref):
    slots = back_ref.shape[0]
    width = back_ref.shape[1] - LANES
    tokens = sum_ref.shape[0]
    pick = pick_ref[...]
    sum_ref[:, :width] = dot(pick, back_ref[:, :width]).astype(BF16)
    expert, _, _ = slot_parts(iota((slots, LANES), 0))
    own = iota((slots, LANES), 1) == expert
    spread = jnp.where(own, back_ref[:, width:].astype(F32), 0.0).astype(BF16)
    by_expert = dot(pick, spread)
    extras = extra_ref[...].astype(F32)
    lane = iota((tokens, LANES), 1)
    expert_lane = served(lane, base_ref[0])
    result = jnp.zeros((tokens, LANES), F32)
    for k in range(TOP):
        hit = extras[:, k : k + 1] == expert_lane
        value = jnp.sum(jnp.where(hit, by_expert, 0.0), axis=1, keepdims=True)
        value = value / extras[:, TOP + k : TOP + k + 1]
        result = jnp.where(lane == k, value, result)
    sum_ref[:, width:] = result.astype(BF16)


def finish_kernel(sums_ref, in_ref, prob_ref):
    width = in_ref.shape[1]
    total = sums_ref[0].astype(F32)
    for s in range(1, FAR):
        total = total + sums_ref[s].astype(F32)
    in_ref[...] = total[:, :width].astype(BF16)
    pick = jnp.where(iota((TOP, LANES), 0) == iota((TOP, LANES), 1), 1.0, 0.0).astype(BF16)
    prob_ref[...] = dot(pick, total[:, width:].astype(BF16), ((1,), (1,))).astype(BF16)


def weight_sum_kernel(*refs):
    part_refs, (gate_ref, up_ref, down_ref) = refs[:-3], refs[-3:]
    share, hidden_width = gate_ref.shape
    down_share, width = down_ref.shape
    half = width // 2

    def part(low, size):
        result = part_refs[0][low : low + size, :].astype(F32)
        for ref in part_refs[1:]:
            result = result + ref[low : low + size, :].astype(F32)
        return result

    gate_up = part(0, share)
    gate_ref[...] = gate_up[:, :hidden_width]
    up_ref[...] = gate_up[:, hidden_width:]
    down_ref[:, :half] = part(share, down_share)
    down_ref[:, half:] = part(share + down_share, down_share)


def params(mib):
    return pltpu.CompilerParams(vmem_limit_bytes=mib * MIB)


def cost(flops, nbytes):
    return pl.CostEstimate(flops=flops, bytes_accessed=nbytes, transcendentals=0)


def per_device(layer_in, grad_out, expert_ids, gate_probs, gate_weight, up_weight, down_weight):
    block, width = layer_in.shape
    hidden_width = gate_weight.shape[2]
    chips = lax.axis_size("x")
    groups = 2 * chips
    tokens = FAR * block
    slots = NEAR * FAR * CAP
    share = width // groups
    down_share = hidden_width // groups
    part_rows = share + 2 * down_share
    core = lax.axis_index("core").astype(jnp.int32)
    chip = lax.axis_index("x").astype(jnp.int32)
    moved = core * (NEAR // 2)
    place = lax.axis_index(("far", "near", "y")) - moved + EXPERTS
    base = ((place & -NEAR) + moved).astype(jnp.int32).reshape(1)
    scalar = pl.BlockSpec(memory_space=pltpu.SMEM)
    hbm = pl.BlockSpec(memory_space=pltpu.HBM)

    def shape(*dims):
        return jax.ShapeDtypeStruct(dims, BF16)

    packed = pl.pallas_call(
        pack_kernel,
        out_shape=pltpu.VMEM((block, 2 * width + LANES), BF16),
        in_specs=[hbm] * 3 + whole(1),
        out_specs=whole(1)[0],
        scratch_shapes=[pltpu.VMEM((TOP, block), jnp.int32), pltpu.SemaphoreType.DMA((3,))],
        compiler_params=params(60),
        name="pack_tokens",
    )(layer_in, grad_out, expert_ids.T, gate_probs.T)
    near_tokens = lax.all_gather(packed, "far", tiled=True)

    send, pick = pl.pallas_call(
        select_kernel,
        out_shape=(shape(slots, 2 * width), shape(tokens, slots)),
        in_specs=[scalar] + whole(1),
        out_specs=tuple(whole(2)),
        compiler_params=params(24),
        name="select_rows",
    )(base, near_tokens)

    exchange = functools.partial(lax.all_to_all, split_axis=0, concat_axis=0, tiled=True)
    near_exchange = functools.partial(
        exchange,
        axis_name=("x", "core", "far", "near", "y"),
        axis_index_groups=windows(groups, EXPERTS),
    )
    rows = near_exchange(send.reshape(NEAR, FAR * CAP, 2 * width)).reshape(slots, 2 * width)

    matmul = 2 * slots * width * hidden_width
    back, both, hidden = pl.pallas_call(
        expert_kernel,
        out_shape=(shape(slots, width + LANES), shape(slots, 2 * hidden_width), shape(slots, hidden_width)),
        in_specs=whole(4),
        out_specs=(hbm,) + tuple(whole(2)),
        scratch_shapes=[pltpu.VMEM((slots, width + LANES), BF16), pltpu.SemaphoreType.DMA((3,))],
        compiler_params=params(32),
        cost_estimate=cost(5 * matmul, 8 * MIB),
        name="expert_rows",
    )(rows, gate_weight[0], up_weight[0], down_weight[0])
    back = near_exchange(back.reshape(NEAR, FAR * CAP, width + LANES)).reshape(slots, width + LANES)

    keep, give = pl.pallas_call(
        part_kernel,
        out_shape=(shape(chips, part_rows, 2 * hidden_width),) * 2,
        in_specs=[scalar, hbm] + whole(2),
        out_specs=(hbm, hbm),
        scratch_shapes=[
            pltpu.VMEM((slots, 2 * width), BF16),
            pltpu.VMEM((chips, part_rows, 2 * hidden_width), BF16),
            pltpu.VMEM((chips, part_rows, 2 * hidden_width), BF16),
            pltpu.SemaphoreType.DMA((chips + 2,)),
            pltpu.SemaphoreType.DMA((2 * chips,)),
        ],
        compiler_params=params(52),
        cost_estimate=cost(3 * matmul, 8 * MIB),
        name="weight_parts",
    )(core.reshape(1), rows, both, hidden)
    got = lax.ppermute(give, "core", [(0, 1), (1, 0)])
    chip_sums = pl.pallas_call(
        chip_sum_kernel,
        out_shape=(shape(part_rows, 2 * hidden_width),) * chips,
        in_specs=[scalar, hbm, hbm],
        out_specs=tuple(whole(chips)),
        scratch_shapes=[
            pltpu.VMEM((chips, part_rows, 2 * hidden_width), BF16),
            pltpu.VMEM((chips, part_rows, 2 * hidden_width), BF16),
            pltpu.SemaphoreType.DMA((2 * chips,)),
        ],
        compiler_params=params(52),
        cost_estimate=cost(MIB, 6 * MIB),
        name="chip_sums",
    )(chip.reshape(1), keep, got)
    parts = [
        lax.ppermute(chip_sums[s], "x", [(i, (i + s) % chips) for i in range(chips)]) for s in (2, 1, 3)
    ] + [chip_sums[0]]

    back, _ = lax.optimization_barrier((back, chip_sums[0]))
    sums = pl.pallas_call(
        combine_kernel,
        out_shape=shape(tokens, width + LANES),
        in_specs=[scalar] + whole(3),
        out_specs=whole(1)[0],
        compiler_params=params(24),
        name="combine_rows",
    )(base, back, pick, near_tokens[:, 2 * width :])
    sums = exchange(sums.reshape(FAR, block, width + LANES), "far")

    grad_gate, grad_up, grad_down = pl.pallas_call(
        weight_sum_kernel,
        out_shape=(
            jax.ShapeDtypeStruct((share, hidden_width), F32),
            jax.ShapeDtypeStruct((share, hidden_width), F32),
            jax.ShapeDtypeStruct((down_share, width), F32),
        ),
        in_specs=whole(chips),
        out_specs=tuple(whole(3)),
        compiler_params=params(24),
        cost_estimate=cost(MIB, 3 * MIB),
        name="weight_sums",
    )(*parts)
    grad_in, grad_probs = pl.pallas_call(
        finish_kernel,
        out_shape=(shape(block, width), shape(TOP, block)),
        in_specs=whole(1),
        out_specs=tuple(whole(2)),
        compiler_params=params(24),
        name="finish",
    )(sums)
    return grad_in, grad_probs.T, grad_gate[None], grad_up[None], grad_down[None]


def solution(mesh):
    groups, experts = mesh.devices.shape
    split = Mesh(
        mesh.devices.reshape(groups // 2, 2, FAR, 4, experts // NEAR), ("x", "core", "far", "near", "y")
    )
    expert = ("far", "near", "y")
    token_spec = P(("x", "core") + expert, None)
    weight_spec = P(expert, None, None)
    grad_spec = P(expert, ("x", "core"), None)
    return jax.shard_map(
        per_device,
        mesh=split,
        in_specs=(token_spec,) * 4 + (weight_spec,) * 3,
        out_specs=(token_spec,) * 2 + (grad_spec,) * 3,
        check_vma=False,
    )
```
